32 devices in a mesh: doc: 4 (over y, x), seq: 8 (over z, core).
Axes of the slice: x: 2, y: 2, z: 4, core: 2. Of those that a mesh axis runs over, the one named last changes fastest.
Arguments:
- tokens: bfloat16 [4, 6144, 768], P('doc', 'seq'), may hold values from -6 to 6
- cotangent: bfloat16 [4, 6144, 768], P('doc', 'seq'), may hold values from -6 to 6
- counts: int32 [4], P('doc'), may hold values from 32 to 64, as said below
- positions: int32 [4, 64], P('doc'), may hold values from 0 to 6143, as said below
- lower_again: float32 [768], replicated, may hold values from 0.5 to 1.5
- lower_abias: float32 [768], replicated, may hold values from -1.5 to 1.5
- lower_query: bfloat16 [768, 768], replicated, may hold values from -0.21875 to 0.21875
- lower_key: bfloat16 [768, 768], replicated, may hold values from -0.21875 to 0.21875
- lower_value: bfloat16 [768, 768], replicated, may hold values from -0.21875 to 0.21875
- lower_out: bfloat16 [768, 768], replicated, may hold values from -1.75 to 1.75
- lower_fgain: float32 [768], replicated, may hold values from 0.5 to 1.5
- lower_fbias: float32 [768], replicated, may hold values from -1.5 to 1.5
- lower_up: bfloat16 [768, 3072], replicated, may hold values from -0.21875 to 0.21875
- lower_down: bfloat16 [3072, 768], replicated, may hold values from -0.109375 to 0.109375
- upper_again: float32 [768], replicated, may hold values from 0.5 to 1.5
- upper_abias: float32 [768], replicated, may hold values from -1.5 to 1.5
- upper_query: bfloat16 [768, 768], replicated, may hold values from -0.21875 to 0.21875
- upper_key: bfloat16 [768, 768], replicated, may hold values from -0.21875 to 0.21875
- upper_value: bfloat16 [768, 768], replicated, may hold values from -0.21875 to 0.21875
- upper_out: bfloat16 [768, 768], replicated, may hold values from -1.75 to 1.75
- upper_fgain: float32 [768], replicated, may hold values from 0.5 to 1.5
- upper_fbias: float32 [768], replicated, may hold values from -1.5 to 1.5
- upper_up: bfloat16 [768, 3072], replicated, may hold values from -0.21875 to 0.21875
- upper_down: bfloat16 [3072, 768], replicated, may hold values from -0.109375 to 0.109375
- upper_kpool: float32 [5, 768], replicated, may hold values from 0.3 to 0.9
- upper_vpool: float32 [5, 768], replicated, may hold values from 0.3 to 0.9
Outputs:
- block_out: bfloat16 [4, 6144, 768], P('doc', 'seq')
- input_grad: float32 [4, 6144, 768], P('doc', 'seq')
- grad_lower_again: float32 [768], P(('doc', 'seq'))
- grad_lower_abias: float32 [768], P(('doc', 'seq'))
- grad_lower_query: float32 [768, 768], P(('doc', 'seq'))
- grad_lower_key: float32 [768, 768], P(('doc', 'seq'))
- grad_lower_value: float32 [768, 768], P(('doc', 'seq'))
- grad_lower_out: float32 [768, 768], P(('doc', 'seq'))
- grad_lower_fgain: float32 [768], P(('doc', 'seq'))
- grad_lower_fbias: float32 [768], P(('doc', 'seq'))
- grad_lower_up: float32 [768, 3072], P(('doc', 'seq'))
- grad_lower_down: float32 [3072, 768], P(('doc', 'seq'))
- grad_upper_again: float32 [768], P(('doc', 'seq'))
- grad_upper_abias: float32 [768], P(('doc', 'seq'))
- grad_upper_query: float32 [768, 768], P(('doc', 'seq'))
- grad_upper_key: float32 [768, 768], P(('doc', 'seq'))
- grad_upper_value: float32 [768, 768], P(('doc', 'seq'))
- grad_upper_out: float32 [768, 768], P(('doc', 'seq'))
- grad_upper_fgain: float32 [768], P(('doc', 'seq'))
- grad_upper_fbias: float32 [768], P(('doc', 'seq'))
- grad_upper_up: float32 [768, 3072], P(('doc', 'seq'))
- grad_upper_down: float32 [3072, 768], P(('doc', 'seq'))
- grad_upper_kpool: float32 [5, 768], P(None, ('doc', 'seq'))
- grad_upper_vpool: float32 [5, 768], P(None, ('doc', 'seq'))
The draws below stay inside these ranges and needn't reach their ends.
Inputs may be any that keep to these rules, and one draw needn't show every extreme that they name: `counts`: some document has exactly 64 questions. The slots of a document hold distinct positions; slots below 32 lie in the document's first 768 tokens; slots at or past the document's count are not used.
All inputs are finite; a program needn't handle non-finite values.
Results may differ from the reference program's by a relative error of at most 0.025.
Values may be sent and summed in bfloat16 or wider, within the bound.
No kernel may reach another device: no remote copies, remote signals or barrier semaphores. Data moves between devices by JAX's collectives and lax.ppermute only.
A program may use at most 512 MiB of HBM per device.

```python
import jax
import jax.numpy as jnp
from jax import lax

D = 768
HDIM = 64
FF = 3072
REACH_ONE = 64
REACH_TWO = 256
KSIZE = 5
STRIDE = 4
GMAX = 64
TOK_DEV = 768
DOCS = 4
LENGTH = 6144
N_SEQ = 8


def draw_counts(key, part):
    key = jax.random.fold_in(key, 11)
    first_key, second_key = jax.random.split(key)
    drawn = jax.random.randint(first_key, (DOCS,), GMAX // 2, GMAX + 1)
    chosen = jax.random.randint(second_key, (), 0, DOCS)
    return jnp.where(jnp.arange(DOCS) == chosen, GMAX, drawn).astype(jnp.int32)


def front_slots(doc_key):
    return jax.random.permutation(doc_key, TOK_DEV)[:GMAX // 2]


def draw_positions(key, part):
    key = jax.random.fold_in(key, 23)
    length = TOK_DEV * N_SEQ
    front = GMAX // 2
    remaining = GMAX - front
    spacing = (length - TOK_DEV) // remaining
    doc_keys = jax.random.split(key, DOCS + 1)
    heads_part = jax.vmap(front_slots)(doc_keys[:DOCS])
    offsets = jax.random.randint(doc_keys[DOCS], (DOCS, remaining), 0, spacing)
    tails = TOK_DEV + jnp.arange(remaining)[None, :] * spacing + offsets
    return jnp.concatenate([heads_part, tails], axis=1).astype(jnp.int32)


def block_levels(stream_key, shape, cuts, smallest, top_value):
    factor_of = 1.0
    for position, shards_of in cuts:
        draws = jax.random.uniform(jax.random.fold_in(jax.random.fold_in(stream_key, 6), position), (shards_of,), jnp.float32, smallest / len(cuts), top_value / len(cuts))
        factor_of = factor_of * jnp.repeat(jnp.exp(draws), shape[position] // shards_of).reshape((-1,) + (1,) * (len(shape) - 1 - position))
    return factor_of


def normal_values(own_key, extent, deviation, reach, cuts=(), kind=jnp.bfloat16):
    gain = block_levels(own_key, extent, cuts, -0.22, 0.18) if cuts else 1.0
    values = jax.random.normal(own_key, extent, jnp.float32) * deviation * gain
    return jnp.minimum(jnp.maximum(values, -reach), reach).astype(kind)


def setup_inputs(seed: int = 0) -> dict:
    splits = jax.random.split(jax.random.key(seed), 27)
    return {
        "tokens": normal_values(splits[0], (DOCS, LENGTH, D), 1.0, 6.0, ((0, 4), (1, 8))),
        "cotangent": normal_values(splits[1], (DOCS, LENGTH, D), 1.0, 6.0, ((0, 4), (1, 8))),
        "counts": draw_counts(jax.random.fold_in(splits[26], 71), 0),
        "positions": draw_positions(jax.random.fold_in(splits[26], 71), 0),
        "lower_again": jnp.clip(1.0 + 0.1 * jax.random.normal(splits[4], (D,), jnp.float32), 0.5, 1.5),
        "lower_abias": normal_values(splits[5], (D,), 0.3, 1.5, (), jnp.float32),
        "lower_query": normal_values(splits[6], (D, D), D ** -0.5, 0.21875),
        "lower_key": normal_values(splits[7], (D, D), D ** -0.5, 0.21875),
        "lower_value": normal_values(splits[8], (D, D), D ** -0.5, 0.21875),
        "lower_out": normal_values(splits[9], (D, D), (D // 64) ** -0.5, 1.75),
        "lower_fgain": jnp.clip(1.0 + 0.1 * jax.random.normal(splits[10], (D,), jnp.float32), 0.5, 1.5),
        "lower_fbias": normal_values(splits[11], (D,), 0.3, 1.5, (), jnp.float32),
        "lower_up": normal_values(splits[12], (D, FF), D ** -0.5, 0.21875),
        "lower_down": normal_values(splits[13], (FF, D), FF ** -0.5, 0.109375),
        "upper_again": jnp.clip(1.0 + 0.1 * jax.random.normal(splits[14], (D,), jnp.float32), 0.5, 1.5),
        "upper_abias": normal_values(splits[15], (D,), 0.3, 1.5, (), jnp.float32),
        "upper_query": normal_values(splits[16], (D, D), D ** -0.5, 0.21875),
        "upper_key": normal_values(splits[17], (D, D), D ** -0.5, 0.21875),
        "upper_value": normal_values(splits[18], (D, D), D ** -0.5, 0.21875),
        "upper_out": normal_values(splits[19], (D, D), (D // 64) ** -0.5, 1.75),
        "upper_fgain": jnp.clip(1.0 + 0.1 * jax.random.normal(splits[20], (D,), jnp.float32), 0.5, 1.5),
        "upper_fbias": normal_values(splits[21], (D,), 0.3, 1.5, (), jnp.float32),
        "upper_up": normal_values(splits[22], (D, FF), D ** -0.5, 0.21875),
        "upper_down": normal_values(splits[23], (FF, D), FF ** -0.5, 0.109375),
        "upper_kpool": jnp.clip(jax.random.uniform(splits[24], (KSIZE, D), jnp.float32, 0.3, 0.9), 0.3, 0.9),
        "upper_vpool": jnp.clip(jax.random.uniform(splits[25], (KSIZE, D), jnp.float32, 0.3, 0.9), 0.3, 0.9),
    }


@jax.custom_vjp
def low(v):
    return lax.optimization_barrier(v.astype(jnp.bfloat16)).astype(jnp.float32)

@jax.custom_vjp
def low_back(v):
    return v

def low_keep(v):
    return (low(v), None)

def low_pass(kept, grad):
    return (grad,)

def back_keep(v):
    return (v, None)

def back_low(kept, grad):
    return (low(grad),)
low.defvjp(low_keep, low_pass)
low_back.defvjp(back_keep, back_low)
eps = 1e-05
far_below = -1e+30
highest = lax.Precision.HIGHEST

def norm_apply(hidden, norm_gain, norm_bias):
    average = lax.optimization_barrier(jnp.mean(hidden, axis=-1, keepdims=True))
    centred = hidden - average
    variance = lax.optimization_barrier(jnp.mean(centred * centred, axis=-1, keepdims=True))
    return centred * lax.rsqrt(variance + eps) * norm_gain + norm_bias

def gelu_apply(lifted):
    return jax.nn.gelu(lifted, approximate=False)

def pool_apply(blocks, rim_rows, weights):
    before = jnp.concatenate([rim_rows[None], blocks[:-1, 2:4]], axis=0)
    return weights[0] * before[:, 0] + weights[1] * before[:, 1] + weights[2] * blocks[:, 0] + weights[3] * blocks[:, 1] + weights[4] * blocks[:, 2]

def split_heads(matrix):
    return matrix.reshape(matrix.shape[0], -1, HDIM)

def project(left_op, right_op):
    return jnp.dot(left_op, right_op, precision=highest, preferred_element_type=jnp.float32)

def attend(queries, key_rows, values, allowed):
    scores = jnp.einsum('qhd,khd->hqk', split_heads(queries), split_heads(key_rows), precision=highest) * HDIM ** (-0.5)
    scores = low_back(jnp.where(allowed[None], scores, far_below))
    soft_rows = jax.nn.softmax(scores, axis=-1)
    output = jnp.einsum('hqk,khd->qhd', low(soft_rows), split_heads(values), precision=highest)
    return output.reshape(queries.shape[0], -1)

def local_attention(queries, pairs):
    length = queries.shape[0]
    model_width = queries.shape[1]
    block_rows = 512
    padded = jnp.pad(pairs, ((REACH_ONE, REACH_ONE), (0, 0)))

    def one_block(block_start):
        query_rows = lax.dynamic_slice_in_dim(queries, block_start, block_rows, 0)
        pair_rows = lax.dynamic_slice_in_dim(padded, block_start, block_rows + 2 * REACH_ONE, 0)
        token_ids = block_start + jnp.arange(block_rows, dtype=jnp.int32)
        key_ids = block_start - REACH_ONE + jnp.arange(block_rows + 2 * REACH_ONE, dtype=jnp.int32)
        allowed = (jnp.abs(token_ids[:, None] - key_ids[None, :]) <= REACH_ONE) & (key_ids >= 0)[None, :] & (key_ids < length)[None, :]
        return attend(query_rows, pair_rows[:, :model_width], pair_rows[:, model_width:], allowed)
    starts = (jnp.arange(length // block_rows) * block_rows).astype(jnp.int32)
    return lax.map(jax.checkpoint(one_block), starts).reshape(length, model_width)

def pooled_attention(queries, pooled, asked_flags):
    length = queries.shape[0]
    model_width = queries.shape[1]
    block_rows = 512
    pooled_ids = jnp.arange(pooled.shape[0], dtype=jnp.int32)

    def one_block(block_start):
        query_rows = lax.dynamic_slice_in_dim(queries, block_start, block_rows, 0)
        flag_rows = lax.dynamic_slice_in_dim(asked_flags, block_start, block_rows, 0)
        token_ids = block_start + jnp.arange(block_rows, dtype=jnp.int32)
        allowed = (jnp.abs(token_ids[:, None] - STRIDE * pooled_ids[None, :]) <= REACH_TWO) | flag_rows[:, None]
        return attend(query_rows, pooled[:, :model_width], pooled[:, model_width:], allowed)
    starts = (jnp.arange(length // block_rows) * block_rows).astype(jnp.int32)
    return lax.map(jax.checkpoint(one_block), starts).reshape(length, model_width)

def attention_layer(hidden, norm_gain, norm_bias, w_query, w_key, w_value, w_out, mixer):
    normed = low(norm_apply(hidden, norm_gain, norm_bias))
    queries = low(low_back(project(normed, w_query)))
    pairs = low(low_back(project(normed, jnp.concatenate([w_key, w_value], axis=1))))
    mixed_rows = low(low_back(mixer(queries, pairs)))
    return hidden + low_back(project(mixed_rows, w_out))

def feed_forward(hidden, norm_gain, norm_bias, w_up, w_down):
    normed = low(norm_apply(hidden, norm_gain, norm_bias))
    lifted = low_back(project(normed, w_up))
    active = low(gelu_apply(lifted))
    return hidden + low_back(project(active, w_down))

def two_layers(hidden, weights, asked_flags):
    hidden = attention_layer(hidden, weights[0], weights[1], weights[2], weights[3], weights[4], weights[5], local_attention)
    hidden = feed_forward(hidden, weights[6], weights[7], weights[8], weights[9])
    pool_weights = jnp.concatenate([weights[20], weights[21]], axis=1)

    def pooled_mixer(queries, pairs):
        pooled_count = pairs.shape[0] // STRIDE
        blocks = pairs.reshape(pooled_count, STRIDE, pairs.shape[1])
        pooled = low(pool_apply(blocks, jnp.zeros((2, pairs.shape[1]), jnp.float32), pool_weights))
        return pooled_attention(queries, pooled, asked_flags)
    hidden = attention_layer(hidden, weights[10], weights[11], weights[12], weights[13], weights[14], weights[15], pooled_mixer)
    return feed_forward(hidden, weights[16], weights[17], weights[18], weights[19])

def reference(tokens, cotangent, counts, positions, lower_again, lower_abias, lower_query, lower_key, lower_value, lower_out, lower_fgain, lower_fbias, lower_up, lower_down, upper_again, upper_abias, upper_query, upper_key, upper_value, upper_out, upper_fgain, upper_fbias, upper_up, upper_down, upper_kpool, upper_vpool):
    weights = tuple((weight.astype(jnp.float32) for weight in (lower_again, lower_abias, lower_query, lower_key, lower_value, lower_out, lower_fgain, lower_fbias, lower_up, lower_down, upper_again, upper_abias, upper_query, upper_key, upper_value, upper_out, upper_fgain, upper_fbias, upper_up, upper_down, upper_kpool, upper_vpool)))
    token_ids = jnp.arange(tokens.shape[1], dtype=jnp.int32)
    slot_ids = jnp.arange(positions.shape[1], dtype=jnp.int32)

    def per_document(totals, doc_item):
        source, grad_out, doc_count, spot_ids = doc_item
        asked_flags = jnp.any((token_ids[:, None] == spot_ids[None, :]) & (slot_ids < doc_count)[None, :], axis=1)

        def run(hidden, *layer_params):
            return two_layers(hidden, layer_params, asked_flags)
        result, pull_back = jax.vjp(run, source.astype(jnp.float32), *weights)
        grads = pull_back(grad_out.astype(jnp.float32))
        totals = tuple((carried + added for carried, added in zip(totals, grads[1:])))
        return (totals, (result.astype(jnp.bfloat16), grads[0]))
    initial = tuple((jnp.zeros_like(weight) for weight in weights))
    totals, (block_out, input_grad) = lax.scan(per_document, initial, (tokens, cotangent, counts, positions))
    return (block_out, input_grad, totals[0], totals[1], totals[2], totals[3], totals[4], totals[5], totals[6], totals[7], totals[8], totals[9], totals[10], totals[11], totals[12], totals[13], totals[14], totals[15], totals[16], totals[17], totals[18], totals[19], totals[20], totals[21])
```

```python
import functools

import jax
import jax.numpy as jnp
from jax import lax
from jax.experimental import pallas as pl
from jax.experimental.pallas import tpu as pltpu
from jax.sharding import PartitionSpec as P

HDIM = 64
REACH_ONE = 64
REACH_TWO = 256
STRIDE = 4
TAPS = 5
QB = 128
PAIR = 2 * HDIM
WIN_ONE = QB + 2 * REACH_ONE
SIDE = REACH_TWO // STRIDE
WIN_TWO = QB // STRIDE + 2 * SIDE
RAW = 16
eps = 1e-05
far_below = -1e30
scale = HDIM**-0.5
f32 = jnp.float32
bf16 = jnp.bfloat16

MILLS = 0.34
MILLS_POLY = (
    0.13590356504727755,
    0.13101844409724564,
    0.1513778923259517,
    -0.01998659482308463,
    0.25210690821609844,
    -0.1936388145328779,
    0.04321858184569336,
)
INV_SQRT_2PI = 0.3989422804014327


def nn(a, b):
    return lax.dot_general(a, b, (((1,), (0,)), ((), ())), preferred_element_type=f32)


def nt(a, b):
    return lax.dot_general(a, b, (((1,), (1,)), ((), ())), preferred_element_type=f32)


def tn(a, b):
    return lax.dot_general(a, b, (((0,), (0,)), ((), ())), preferred_element_type=f32)


def norm_rows(x, gain, bias):
    average = jnp.mean(x, axis=-1, keepdims=True)
    centred = x - average
    variance = jnp.mean(centred * centred, axis=-1, keepdims=True)
    return centred * lax.rsqrt(variance + eps) * gain + bias


def norm_back(x, gain, grad):
    average = jnp.mean(x, axis=-1, keepdims=True)
    centred = x - average
    variance = jnp.mean(centred * centred, axis=-1, keepdims=True)
    spread = lax.rsqrt(variance + eps)
    unit = centred * spread
    lifted = grad * gain
    first = jnp.mean(lifted, axis=-1, keepdims=True)
    second = jnp.mean(lifted * unit, axis=-1, keepdims=True)
    back = spread * (lifted - first - unit * second)
    return back, jnp.sum(grad * unit, axis=0, keepdims=True), jnp.sum(grad, axis=0, keepdims=True)


def gelu_both(u):
    t = 1.0 / (1.0 + MILLS * jnp.abs(u))
    e = jnp.exp(-0.5 * (u * u))
    poly = jnp.full_like(u, MILLS_POLY[-1])
    for c in MILLS_POLY[-2::-1]:
        poly = poly * t + c
    tail = poly * (t * e)
    cdf = jnp.where(u >= 0, 1.0 - tail, tail)
    return u * cdf, cdf + u * e * INV_SQRT_2PI


def whole(*shape):
    return pl.BlockSpec(shape, lambda *_: (0,) * len(shape), pipeline_mode=pl.Buffered(1))


def smem():
    return pl.BlockSpec(memory_space=pltpu.SMEM)


def params(mib, flops=0, size=0):
    return dict(
        compiler_params=pltpu.CompilerParams(vmem_limit_bytes=mib << 20),
        cost_estimate=pl.CostEstimate(flops=flops, bytes_accessed=size, transcendentals=0),
    )


def sds(shape, dtype):
    return jax.ShapeDtypeStruct(shape, dtype)


def tiles(rows, step):
    return [slice(i, i + step) for i in range(0, rows, step)]


def project_kernel(x, gain, bias, wq, wk, wv, normed, q, k, v):
    for rows in tiles(x.shape[0], 256):
        normed[rows] = norm_rows(x[rows].astype(f32), gain[...], bias[...]).astype(bf16)
        for w, out in ((wq, q), (wk, k), (wv, v)):
            out[rows] = nn(normed[rows], w[...]).astype(bf16)


def project(x, gain, bias, wq, wk, wv):
    n, d = x.shape
    return pl.pallas_call(
        project_kernel,
        out_shape=[sds((n, d), bf16)] * 4,
        in_specs=[whole(n, d), whole(1, d), whole(1, d)] + [whole(d, d)] * 3,
        out_specs=[whole(n, d)] * 4,
        grid=(1,),
        **params(40, 6 * n * d * d, 10 * n * d + 6 * d * d),
    )(x, gain, bias, wq, wk, wv)


def head_masks(rows):
    lane = lax.broadcasted_iota(jnp.int32, (rows, PAIR), 1)
    return lane < HDIM


def both_heads(x):
    first = head_masks(x.shape[0])
    zero = jnp.zeros_like(x)
    return jnp.concatenate([jnp.where(first, x, zero), jnp.where(first, zero, x)], axis=0)


def own_blocks(x):
    n = x.shape[1] // 2
    return jnp.concatenate([x[:HDIM, :n], x[HDIM:, n:]], axis=0).T


def softmax_columns(scores):
    top = jnp.max(scores, axis=0, keepdims=True)
    raised = jnp.exp(scores - top)
    total = jnp.sum(raised, axis=0, keepdims=True)
    return (raised * (1.0 / total)).astype(bf16)


def window_bias(kind):
    win = WIN_ONE if kind == 1 else WIN_TWO
    key = lax.broadcasted_iota(jnp.int32, (win, QB), 0)
    query = lax.broadcasted_iota(jnp.int32, (win, QB), 1)
    if kind == 1:
        offset, reach = key - query, 2 * REACH_ONE
    else:
        offset, reach = STRIDE * key - query, 2 * REACH_TWO
    return jnp.where((offset >= 0) & (offset <= reach), 0.0, far_below)


def edge_bias(bias, start, edge, length, flags):
    win = bias.shape[0]
    key = lax.broadcasted_iota(jnp.int32, bias.shape, 0) + start
    if start < edge:
        limit = jnp.where(flags[0] > 0, edge, 0)
        bias = jnp.where(key < limit, far_below, bias)
    if start + win > length - edge:
        limit = jnp.where(flags[1] > 0, length - edge, length)
        bias = jnp.where(key >= limit, far_below, bias)
    return bias


def attend_block(qb, kb, vb, bias):
    scores = nt(kb, both_heads(qb * scale)) + jnp.concatenate([bias, bias], axis=1)
    weights = softmax_columns(scores)
    return own_blocks(tn(vb, weights)), weights


def back_block(qb, kb, vb, weights, grad):
    grad_two = both_heads(grad)
    change = nt(vb, grad_two)
    share = weights.astype(f32)
    inner = jnp.sum(share * change, axis=0, keepdims=True) / jnp.sum(share, axis=0, keepdims=True)
    grad_scores = (share * (change - inner)).astype(bf16)
    grad_values = nn(weights, grad_two)
    grad_keys = nn(grad_scores, both_heads(qb * scale))
    grad_queries = own_blocks(tn(kb, grad_scores)) * scale
    return grad_queries, grad_keys, grad_values


def local_kernel(flags, q, k, v, kl, vl, kr, vr, out, weights, kw, vw, base):
    n = q.shape[0]

    @pl.when(pl.program_id(0) == 0)
    def _():
        base[...] = window_bias(1)

    for wide, left, own, right in ((kw, kl, k, kr), (vw, vl, v, vr)):
        wide[:REACH_ONE] = left[...]
        wide[REACH_ONE : REACH_ONE + n] = own[...]
        wide[REACH_ONE + n :] = right[...]
    for b, rows in enumerate(tiles(n, QB)):
        window = slice(b * QB, b * QB + WIN_ONE)
        bias = edge_bias(base[...], b * QB, REACH_ONE, n + 2 * REACH_ONE, flags)
        mixed, w = attend_block(q[rows], kw[window], vw[window], bias)
        out[rows] = mixed.astype(bf16)
        weights[0, b] = w


def pair_block(rows, offset=0):
    return pl.BlockSpec((rows, PAIR), lambda g, offset=offset: (0, g + offset))


def local_attention(flags, q, k, v, left, right):
    n, d = q.shape
    pairs, blocks = d // PAIR, n // QB
    wide = n + 2 * REACH_ONE
    return pl.pallas_call(
        local_kernel,
        out_shape=[sds((n, d), bf16), sds((pairs, blocks, WIN_ONE, 2 * QB), bf16)],
        grid=(pairs,),
        in_specs=[smem()]
        + [pair_block(n)] * 3
        + [pair_block(REACH_ONE), pair_block(REACH_ONE, pairs)] * 2,
        out_specs=[
            pair_block(n),
            pl.BlockSpec((1, blocks, WIN_ONE, 2 * QB), lambda g: (g, 0, 0, 0)),
        ],
        scratch_shapes=[
            pltpu.VMEM((wide, PAIR), bf16),
            pltpu.VMEM((wide, PAIR), bf16),
            pltpu.VMEM((WIN_ONE, QB), f32),
        ],
        **params(24, 4 * n * WIN_ONE * d * 2, 12 * n * d),
    )(flags, q, k, v, left, left, right, right)


def local_back_kernel(
    q, k, v, kl, vl, kr, vr, weights, grad, gq, gk, gv, gkl, gvl, gkr, gvr, kw, vw, ka, va
):
    n = q.shape[0]
    for wide, left, own, right in ((kw, kl, k, kr), (vw, vl, v, vr)):
        wide[:REACH_ONE] = left[...]
        wide[REACH_ONE : REACH_ONE + n] = own[...]
        wide[REACH_ONE + n :] = right[...]
    ka[...] = jnp.zeros_like(ka)
    va[...] = jnp.zeros_like(va)
    for b, rows in enumerate(tiles(n, QB)):
        window = slice(b * QB, b * QB + WIN_ONE)
        gqb, gkb, gvb = back_block(q[rows], kw[window], vw[window], weights[0, b], grad[rows])
        gq[rows] = gqb.astype(bf16)
        ka[window] += gkb
        va[window] += gvb
    for wide, left, own, right in ((ka, gkl, gk, gkr), (va, gvl, gv, gvr)):
        left[...] = wide[:REACH_ONE]
        own[...] = wide[REACH_ONE : REACH_ONE + n]
        right[...] = wide[REACH_ONE + n :]


def local_back(q, k, v, left, right, weights, grad):
    n, d = q.shape
    pairs, blocks = d // PAIR, n // QB
    wide = n + 2 * REACH_ONE
    return pl.pallas_call(
        local_back_kernel,
        out_shape=[sds((n, d), bf16), sds((n, d), f32), sds((n, d), f32)] + [sds((REACH_ONE, d), f32)] * 4,
        grid=(pairs,),
        in_specs=[pair_block(n)] * 3
        + [pair_block(REACH_ONE), pair_block(REACH_ONE, pairs)] * 2
        + [pl.BlockSpec((1, blocks, WIN_ONE, 2 * QB), lambda g: (g, 0, 0, 0))]
        + [pair_block(n)],
        out_specs=[pair_block(n)] * 3 + [pair_block(REACH_ONE)] * 4,
        scratch_shapes=[pltpu.VMEM((wide, PAIR), bf16)] * 2 + [pltpu.VMEM((wide, PAIR), f32)] * 2,
        **params(24, 10 * n * WIN_ONE * d * 2, 24 * n * d),
    )(q, k, v, left, left, right, right, weights, grad)


def first_pooled(tile, rim, raw, taps):
    row = (
        taps[0:1] * rim[0:1].astype(f32)
        + taps[1:2] * rim[1:2].astype(f32)
        + taps[2:3] * raw[0:1].astype(f32)
        + taps[3:4] * raw[1:2].astype(f32)
        + taps[4:5] * raw[2:3].astype(f32)
    )
    first = lax.broadcasted_iota(jnp.int32, tile.shape, 0) == 0
    return jnp.where(first, row, tile.astype(f32)).astype(bf16)


def pooled_window(wide, left, own, right, mine, taps):
    n = own.shape[0]
    wide[:SIDE] = left[:SIDE]
    wide[SIDE : SIDE + n] = own[...]
    wide[SIDE + n :] = right[:SIDE]
    rim = left[SIDE:].astype(f32)[RAW - 2 :]
    raw = mine[:RAW].astype(f32)
    wide[SIDE : SIDE + RAW] = first_pooled(own[:RAW], rim, raw, taps)
    rim = mine[RAW:].astype(f32)[RAW - 2 :]
    raw = right[SIDE:].astype(f32)
    wide[SIDE + n : SIDE + n + RAW] = first_pooled(right[:RAW], rim, raw, taps)


def near_kernel(flags, q, pk, pv, lk, lv, rk, rv, mk, mv, tk, tv, out, weights, kw, vw, base):
    n = q.shape[0]

    @pl.when(pl.program_id(0) == 0)
    def _():
        base[...] = window_bias(2)

    pooled_window(kw, lk, pk, rk, mk, tk[...])
    pooled_window(vw, lv, pv, rv, mv, tv[...])
    step = QB // STRIDE
    for b, rows in enumerate(tiles(n, QB)):
        window = slice(b * step, b * step + WIN_TWO)
        bias = edge_bias(base[...], b * step, SIDE, kw.shape[0], flags)
        mixed, w = attend_block(q[rows], kw[window], vw[window], bias)
        out[rows] = mixed.astype(bf16)
        weights[0, b] = w


def near_attention(flags, q, pooled, left, right, mine, taps):
    n, d = q.shape
    pairs, blocks, m = d // PAIR, n // QB, n // STRIDE
    wide = m + 2 * SIDE
    two = lambda rows: [pair_block(rows), pair_block(rows, pairs)]
    return pl.pallas_call(
        near_kernel,
        out_shape=[
            sds((n, d), bf16),
            sds((pairs, blocks, WIN_TWO, 2 * QB), bf16),
            sds((wide, d), bf16),
            sds((wide, d), bf16),
        ],
        grid=(pairs,),
        in_specs=[smem(), pair_block(n)] + two(m) + two(SIDE + RAW) * 2 + two(2 * RAW) + two(8),
        out_specs=[
            pair_block(n),
            pl.BlockSpec((1, blocks, WIN_TWO, 2 * QB), lambda g: (g, 0, 0, 0)),
            pair_block(wide),
            pair_block(wide),
        ],
        scratch_shapes=[pltpu.VMEM((WIN_TWO, QB), f32)],
        **params(24, 4 * n * WIN_TWO * d * 2, 10 * n * d),
    )(flags, q, pooled, pooled, left, left, right, right, mine, mine, taps, taps)


def asked_kernel(q, kw, vw, out):
    n = kw.shape[0] - 2 * SIDE
    own = slice(SIDE, SIDE + n)
    slots = q.shape[0]
    scores = nt(kw[own], both_heads(q[...] * scale))
    top = jnp.max(scores, axis=0, keepdims=True)
    raised = jnp.exp(scores - top).astype(bf16)
    total = jnp.sum(raised.astype(f32), axis=0, keepdims=True)
    sums = tn(vw[own], raised)
    column = lax.broadcasted_iota(jnp.int32, (HDIM, 2 * slots), 1)
    out[0, :HDIM] = jnp.where(column < slots, sums[:HDIM], sums[HDIM:])
    row = lax.broadcasted_iota(jnp.int32, (8, 2 * slots), 0)
    out[0, HDIM:] = jnp.where(row == 0, top, jnp.where(row == 1, total, 0.0))


def asked_part(q, kw, vw):
    slots, d = q.shape
    pairs, wide = d // PAIR, kw.shape[0]
    return pl.pallas_call(
        asked_kernel,
        out_shape=sds((pairs, HDIM + 8, 2 * slots), f32),
        grid=(pairs,),
        in_specs=[pair_block(slots), pair_block(wide), pair_block(wide)],
        out_specs=pl.BlockSpec((1, HDIM + 8, 2 * slots), lambda g: (g, 0, 0)),
        **params(16, 4 * slots * wide * d, 4 * wide * d),
    )(q, kw, vw)


def near_back_kernel(q, kw, vw, weights, grad, gq, gk, gv):
    n = q.shape[0]
    gk[...] = jnp.zeros_like(gk)
    gv[...] = jnp.zeros_like(gv)
    step = QB // STRIDE
    for b, rows in enumerate(tiles(n, QB)):
        window = slice(b * step, b * step + WIN_TWO)
        gqb, gkb, gvb = back_block(q[rows], kw[window], vw[window], weights[0, b], grad[rows])
        gq[rows] = gqb.astype(bf16)
        gk[window] += gkb
        gv[window] += gvb


def near_back(q, kw, vw, weights, grad):
    n, d = q.shape
    pairs, blocks, wide = d // PAIR, n // QB, kw.shape[0]
    return pl.pallas_call(
        near_back_kernel,
        out_shape=[sds((n, d), bf16), sds((wide, d), f32), sds((wide, d), f32)],
        grid=(pairs,),
        in_specs=[pair_block(n), pair_block(wide), pair_block(wide)]
        + [pl.BlockSpec((1, blocks, WIN_TWO, 2 * QB), lambda g: (g, 0, 0, 0))]
        + [pair_block(n)],
        out_specs=[pair_block(n), pair_block(wide), pair_block(wide)],
        **params(24, 10 * n * WIN_TWO * d * 2, 20 * n * d),
    )(q, kw, vw, weights, grad)


def asked_back_kernel(q, kw, vw, logsum, mixed, grad, gk_near, gv_near, gq, gk, gv):
    n = kw.shape[0] - 2 * SIDE
    own = slice(SIDE, SIDE + n)
    slots = q.shape[0]
    kb, vb = kw[own], vw[own]
    q_two = both_heads(q[...] * scale)
    weights = jnp.exp(nt(kb, q_two) - logsum[0, 0:1])
    grad_two = both_heads(grad[...])
    change = nt(vb, grad_two)
    by_feature = (grad[...].astype(f32) * mixed[...]).T
    inner = [jnp.sum(by_feature[rows], axis=0, keepdims=True) for rows in tiles(PAIR, HDIM)]
    grad_scores = (weights * (change - jnp.concatenate(inner, axis=1))).astype(bf16)
    gk[...] = gk_near[...]
    gv[...] = gv_near[...]
    gk[own] += nn(grad_scores, q_two)
    gv[own] += nn(weights.astype(bf16), grad_two)
    queries = tn(grad_scores, kb) * scale
    gq[...] = jnp.where(head_masks(slots), queries[:slots], queries[slots:])


def asked_back(q, kw, vw, logsum, mixed, grad, gk, gv):
    slots, d = q.shape
    pairs, wide = d // PAIR, kw.shape[0]
    return pl.pallas_call(
        asked_back_kernel,
        out_shape=[sds((slots, d), f32), sds((wide, d), f32), sds((wide, d), f32)],
        grid=(pairs,),
        in_specs=[pair_block(slots), pair_block(wide), pair_block(wide)]
        + [pl.BlockSpec((1, 8, 2 * slots), lambda g: (g, 0, 0))]
        + [pair_block(slots)] * 2
        + [pair_block(wide)] * 2,
        out_specs=[pair_block(slots), pair_block(wide), pair_block(wide)],
        **params(16, 10 * slots * wide * d, 20 * wide * d),
    )(q, kw, vw, logsum, mixed, grad, gk, gv)


def pool_rows(held, taps):
    m = (held.shape[0] - 8) // STRIDE
    total = taps[0:1] * held[pl.ds(6, m, stride=STRIDE)]
    for t in range(1, TAPS):
        total = total + taps[t : t + 1] * held[pl.ds(6 + t, m, stride=STRIDE)]
    return total.astype(bf16)


def lower_kernel(
    x, mixed, wo, fgain, fbias, up, down, again, abias, wq, wk, wv, kpool, vpool, sel,
    hidden_b, normed_b, active, slope, hidden_c, normed_c, q, k, v, pooled, mine, to_left, to_right, asked,
    held,
):
    step = pl.program_id(0)
    n, d = x.shape

    @pl.when(step == 0)
    def _():
        for rows in tiles(n, 256):
            h = x[rows].astype(f32) + nn(mixed[rows], wo[...])
            hidden_b[rows] = h
            hidden_c[rows] = h
            normed_b[rows] = norm_rows(h, fgain[...], fbias[...]).astype(bf16)

    for rows in tiles(n, 256):
        a, s = gelu_both(nn(normed_b[rows], up[...]))
        a = a.astype(bf16)
        active[rows] = a
        slope[rows] = s.astype(bf16)
        hidden_c[rows] += nn(a, down[...])

    @pl.when(step == pl.num_programs(0) - 1)
    def _():
        for rows in tiles(n, 256):
            normed_c[rows] = norm_rows(hidden_c[rows], again[...], abias[...]).astype(bf16)
            q[rows] = nn(normed_c[rows], wq[...]).astype(bf16)
        m = n // STRIDE
        held[:, :8] = jnp.zeros((d // PAIR, 8, PAIR), f32)
        for w, out, taps, lanes in ((wk, k, kpool, slice(0, d)), (wv, v, vpool, slice(d, 2 * d))):
            for rows in tiles(n, 256):
                made = nn(normed_c[rows], w[...]).astype(bf16)
                out[rows] = made
                for i, c in enumerate(tiles(d, PAIR)):
                    held[i, 8 + rows.start : 8 + rows.stop] = made[:, c].astype(f32)
            for i, c in enumerate(tiles(d, PAIR)):
                part = slice(lanes.start + c.start, lanes.start + c.stop)
                pooled[:, part] = pool_rows(held.at[i], taps[:, c])
            mine[:RAW, lanes] = out[:RAW]
            mine[RAW:, lanes] = out[n - RAW :]
        to_right[:SIDE] = pooled[m - SIDE :]
        to_right[SIDE:] = mine[RAW:]
        to_left[:SIDE] = pooled[:SIDE]
        to_left[SIDE:] = mine[:RAW]
        asked[...] = nn(sel[...], q[...]).astype(bf16)


def lower_forward(x, mixed, wo, fgain, fbias, up, down, again, abias, wq, wk, wv, kpool, vpool, sel):
    n, d = x.shape
    ff, slots, m = up.shape[1], sel.shape[0], n // STRIDE
    fc = 512
    return pl.pallas_call(
        lower_kernel,
        out_shape=[
            sds((n, d), f32), sds((n, d), bf16), sds((n, ff), bf16), sds((n, ff), bf16), sds((n, d), f32),
            sds((n, d), bf16), sds((n, d), bf16), sds((n, d), bf16), sds((n, d), bf16),
            sds((m, 2 * d), bf16), sds((2 * RAW, 2 * d), bf16), sds((SIDE + RAW, 2 * d), bf16),
            sds((SIDE + RAW, 2 * d), bf16), sds((slots, d), bf16),
        ],
        grid=(ff // fc,),
        in_specs=[
            whole(n, d), whole(n, d), whole(d, d), whole(1, d), whole(1, d),
            pl.BlockSpec((d, fc), lambda c: (0, c)), pl.BlockSpec((fc, d), lambda c: (c, 0)),
            whole(1, d), whole(1, d), whole(d, d), whole(d, d), whole(d, d), whole(8, d), whole(8, d),
            whole(slots, n),
        ],
        out_specs=[
            whole(n, d), whole(n, d), pl.BlockSpec((n, fc), lambda c: (0, c)),
            pl.BlockSpec((n, fc), lambda c: (0, c)), whole(n, d), whole(n, d), whole(n, d), whole(n, d),
            whole(n, d), whole(m, 2 * d), whole(2 * RAW, 2 * d), whole(SIDE + RAW, 2 * d),
            whole(SIDE + RAW, 2 * d), whole(slots, d),
        ],
        scratch_shapes=[pltpu.VMEM((d // PAIR, n + 8, PAIR), f32)],
        **params(56, 4 * n * d * ff + 8 * n * d * d, 8 * n * ff + 40 * n * d),
    )(x, mixed, wo, fgain, fbias, up, down, again, abias, wq, wk, wv, kpool, vpool, sel)


def by_owner(perm, x):
    return nt(perm, x).astype(bf16)


def place_hidden(order, group, chunk, rows, wide):
    count = order.shape[0]
    held = chunk.T
    size = held.shape[0] // count
    for s in range(count):
        start = pl.multiple_of(order[s] * size, size)
        wide[pl.ds(start, size), rows] = held[s * size : (s + 1) * size].astype(wide.dtype)


def hidden_scratch(n, fc, seqs):
    return pltpu.VMEM((fc, n), f32 if fc // seqs % 16 else bf16)


def two_halves(left, right, first, second):
    half = left.shape[0] // 2
    first[...] = nn(left[:half].astype(bf16), right[...]).astype(bf16).reshape(first.shape)
    second[...] = nn(left[half:].astype(bf16), right[...]).astype(bf16).reshape(second.shape)


def finish_back(n, hidden, grad, gain, grad_norm, grad_hidden, sums):
    sums[...] = jnp.zeros_like(sums)
    for rows in tiles(n, 128):
        back, by_gain, by_bias = norm_back(hidden[rows], gain[...], grad_norm[rows])
        grad_hidden[rows] = grad[rows].astype(f32) + back
        sums[0:1] += by_gain
        sums[1:2] += by_bias


def hidden_specs(d, ff, docs):
    fc = ff // docs
    last = docs - 1
    into = [
        pl.BlockSpec((d, fc), lambda c, *_: (0, jnp.minimum(c, last))),
        pl.BlockSpec((fc, d), lambda c, *_: (jnp.minimum(c, last), 0)),
    ]
    lanes = pl.BlockSpec((d // 2, fc), lambda c, *_: (0, c))
    rows = pl.BlockSpec(
        (1, fc // 2, d), lambda c, docs, *_: (docs[jnp.minimum(c, last)], 0, 0)
    )
    out = [lanes, lanes, rows, rows]
    shapes = [sds((d // 2, ff + d), bf16)] * 2 + [sds((docs, fc // 2, d), bf16)] * 2
    return into, out, shapes


def upper_kernel(
    doc_order, seq_order, hidden_c, near, asked, sel, cot, wo, fgain, fbias, perm, up, down,
    out, mixed, grad_d, grad_mixed, grad_asked, up_keep, up_send, down_keep, down_send, sums,
    hidden_d, normed, hidden_e, grad_norm, flag, normed_t, active_t, lifted,
):
    step = pl.program_id(0)
    n, d = near.shape
    last = pl.num_programs(0) - 1

    @pl.when(step == 0)
    def _():
        slots = sel.shape[0]
        flag[...] = tn(sel[...], jnp.ones((slots, PAIR), bf16))
        for rows in tiles(n, 256):
            here = jnp.concatenate([flag[rows]] * (d // PAIR), axis=1) > 0.5
            placed = tn(sel[:, rows], asked[...])
            mixed[rows] = jnp.where(here, placed, near[rows].astype(f32)).astype(bf16)
            h = hidden_c[rows] + nn(mixed[rows], wo[...])
            hidden_d[rows] = h
            hidden_e[rows] = h
            normed[rows] = norm_rows(h, fgain[...], fbias[...]).astype(bf16)
        normed_t[...] = by_owner(perm[...], normed[...])
        grad_norm[...] = jnp.zeros_like(grad_norm)

    @pl.when(step < last)
    def _():
        for rows in tiles(n, 256):
            a, s = gelu_both(nn(normed[rows], up[...]))
            a = a.astype(bf16)
            hidden_e[rows] += nn(a, down[...])
            place_hidden(seq_order, step, a, rows, active_t)
            g = (nt(cot[rows], down[...]) * s).astype(bf16)
            grad_norm[rows] += nt(g, up[...])
            lifted[rows] = g
        two_halves(normed_t, lifted, up_keep, up_send)
        two_halves(active_t, cot, down_keep, down_send)

    @pl.when(step == last)
    def _():
        for rows in tiles(n, 256):
            out[rows] = hidden_e[rows].astype(bf16)
        finish_back(n, hidden_d, cot, fgain, grad_norm, grad_d, sums)
        for rows in tiles(n, 256):
            branch = grad_d[rows].astype(bf16)
            lifted[rows] = branch
            grad_mixed[rows] = nt(branch, wo[...]).astype(bf16)
        normed_t[...] = by_owner(perm[...], mixed[...])
        two_halves(normed_t, lifted, up_keep, up_send)
        grad_asked[...] = nn(sel[...], grad_mixed[...]).astype(bf16)
        for rows in tiles(n, 256):
            here = jnp.concatenate([flag[rows]] * (d // PAIR), axis=1) > 0.5
            g = grad_mixed[rows]
            grad_mixed[rows] = jnp.where(here, 0.0, g.astype(f32)).astype(bf16)


def upper_both(doc_order, seq_order, hidden_c, near, asked, sel, cot, wo, fgain, fbias, perm, up, down):
    n, d = near.shape
    ff, slots = up.shape[1], sel.shape[0]
    docs, seqs = doc_order.shape[0], seq_order.shape[0]
    into, outof, shapes = hidden_specs(d, ff, docs)
    fc = ff // docs
    return pl.pallas_call(
        upper_kernel,
        out_shape=[
            sds((n, d), bf16), sds((n, d), bf16), sds((n, d), f32), sds((n, d), bf16), sds((slots, d), bf16),
            *shapes, sds((8, d), f32),
        ],
        grid_spec=pltpu.PrefetchScalarGridSpec(
            num_scalar_prefetch=2,
            grid=(docs + 1,),
            in_specs=[
                whole(n, d), whole(n, d), whole(slots, d), whole(slots, n), whole(n, d), whole(d, d), whole(1, d),
                whole(1, d), whole(d, d), *into,
            ],
            out_specs=[
                whole(n, d), whole(n, d), whole(n, d), whole(n, d), whole(slots, d), *outof, whole(8, d),
            ],
            scratch_shapes=[
                pltpu.VMEM((n, d), f32), pltpu.VMEM((n, d), bf16), pltpu.VMEM((n, d), f32), pltpu.VMEM((n, d), f32),
                pltpu.VMEM((n, PAIR), f32), pltpu.VMEM((d, n), bf16), hidden_scratch(n, fc, seqs),
                pltpu.VMEM((n, fc), bf16),
            ],
        ),
        **params(58, 12 * n * d * ff + 6 * n * d * d, 8 * d * ff + 40 * n * d),
    )(doc_order, seq_order, hidden_c, near, asked, sel, cot, wo, fgain, fbias, perm, up, down)


def unpool(held, gp, following, taps, made):
    m = gp.shape[0]
    last = lax.broadcasted_iota(jnp.int32, gp.shape, 0) == m - 1
    later = jnp.where(last, following, pltpu.roll(gp, m - 1, 0))
    made[pl.ds(0, m, stride=STRIDE)] = taps[2:3] * gp
    made[pl.ds(1, m, stride=STRIDE)] = taps[3:4] * gp
    made[pl.ds(2, m, stride=STRIDE)] = taps[4:5] * gp + taps[0:1] * later
    made[pl.ds(3, m, stride=STRIDE)] = taps[1:2] * later
    return [
        jnp.sum(gp * held[pl.ds(6 + t, m, stride=STRIDE)], axis=0, keepdims=True) for t in range(TAPS)
    ]


def upper_project_kernel(
    gq_near, gq_asked, sel, gpk, gpv, near_left, near_right, next_row, k, v, rim, kpool, vpool, normed, hidden, grad,
    gain, wq, wk, wv, perm,
    gw_keep, gw_send, grad_c, sums,
    gq, gkv, held, made, grad_norm, normed_t,
):
    n, d = gq_near.shape
    m = n // STRIDE
    normed_t[...] = by_owner(perm[...], normed[...])
    for rows in tiles(n, 256):
        gq[rows] = (gq_near[rows].astype(f32) + tn(sel[:, rows], gq_asked[...])).astype(bf16)
    two_halves(normed_t, gq, gw_keep.at[:, :d], gw_send.at[:, :d])
    grad_norm[...] = nt(gq[...], wq[...])
    sums[...] = jnp.zeros_like(sums)
    for i, (gp, x, taps, w) in enumerate(((gpk, k, kpool, wk), (gpv, v, vpool, wv))):
        for c in tiles(d, PAIR):
            lanes = slice(i * d + c.start, i * d + c.stop)
            held[:8] = rim[RAW - 8 :, lanes]
            held[8:] = x[:, c].astype(f32)
            total = gp[:, c]
            edge = jnp.zeros((m - 2 * SIDE, PAIR), f32)
            total = total + jnp.concatenate([near_left[:, lanes], edge, near_right[:, lanes]], axis=0)
            parts = unpool(held, total, next_row[0:1, lanes], taps[:, c], made)
            gkv[:, c] = made[...].astype(bf16)
            for t, part in enumerate(parts):
                sums[8 * i + t : 8 * i + t + 1, c] = part
        part = slice((1 + i) * d, (2 + i) * d)
        two_halves(normed_t, gkv, gw_keep.at[:, part], gw_send.at[:, part])
        grad_norm[...] += nt(gkv[...], w[...])
    sums[16:18] = jnp.zeros((2, d), f32)
    for rows in tiles(n, 128):
        back, by_gain, by_bias = norm_back(hidden[rows], gain[...], grad_norm[rows])
        grad_c[rows] = grad[rows] + back
        sums[16:17] += by_gain
        sums[17:18] += by_bias


def upper_project_back(
    gq_near, gq_asked, sel, gpk, gpv, near_left, near_right, next_row, k, v, rim, kpool, vpool, normed, hidden, grad,
    gain, wq, wk, wv, perm,
):
    n, d = gq_near.shape
    slots, m = sel.shape[0], n // STRIDE
    return pl.pallas_call(
        upper_project_kernel,
        out_shape=[sds((d // 2, 3 * d), bf16)] * 2 + [sds((n, d), f32), sds((24, d), f32)],
        grid=(1,),
        in_specs=[
            whole(n, d), whole(slots, d), whole(slots, n), whole(m, d), whole(m, d), whole(SIDE, 2 * d),
            whole(SIDE, 2 * d), whole(8, 2 * d), whole(n, d), whole(n, d), whole(RAW, 2 * d), whole(8, d),
            whole(8, d), whole(n, d), whole(n, d), whole(n, d), whole(1, d), whole(d, d), whole(d, d), whole(d, d), whole(d, d),
        ],
        out_specs=[whole(d // 2, 3 * d)] * 2 + [whole(n, d), whole(24, d)],
        scratch_shapes=[
            pltpu.VMEM((n, d), bf16), pltpu.VMEM((n, d), bf16), pltpu.VMEM((n + 8, PAIR), f32),
            pltpu.VMEM((n, PAIR), f32), pltpu.VMEM((n, d), f32), pltpu.VMEM((d, n), bf16),
        ],
        **params(58, 12 * n * d * d, 30 * n * d),
    )(
        gq_near, gq_asked, sel, gpk, gpv, near_left, near_right, next_row, k, v, rim, kpool, vpool, normed, hidden,
        grad, gain, wq, wk, wv, perm,
    )


def lower_project_kernel(
    gq, gk, gv, kl, vl, kr, vr, normed, x, grad, gain, wq, wk, wv, perm, sums_b, sums_c, sums_d,
    gw_keep, gw_send, grad_in,
    gkv, grad_norm, normed_t, sums,
):
    n, d = gq.shape
    normed_t[...] = by_owner(perm[...], normed[...])
    two_halves(normed_t, gq, gw_keep.at[:, :d], gw_send.at[:, :d])
    grad_norm[...] = nt(gq[...], wq[...])
    for i, (g, left, right, w) in enumerate(((gk, kl, kr, wk), (gv, vl, vr, wv))):
        gkv[...] = g[...].astype(bf16)
        gkv[:REACH_ONE] = (g[:REACH_ONE] + left[...]).astype(bf16)
        gkv[n - REACH_ONE :] = (g[n - REACH_ONE :] + right[...]).astype(bf16)
        part = slice((1 + i) * d, (2 + i) * d)
        two_halves(normed_t, gkv, gw_keep.at[:, part], gw_send.at[:, part])
        grad_norm[...] += nt(gkv[...], w[...])
    sums[...] = jnp.zeros_like(sums)
    for rows in tiles(n, 128):
        back, by_gain, by_bias = norm_back(x[rows].astype(f32), gain[...], grad_norm[rows])
        grad_in[rows] = grad[rows] + back
        sums[0:1] += by_gain
        sums[1:2] += by_bias
    sums[8:16] = sums_b[...]
    sums[16:40] = sums_c[...]
    sums[40:48] = sums_d[...]
    for half, out in zip(tiles(d, d // 2), (gw_keep, gw_send)):
        out[:, 3 * d :] = nt(perm[half], sums[...].astype(bf16)).astype(bf16)


def lower_project_back(gq, gk, gv, left, right, normed, x, grad, gain, wq, wk, wv, perm, sums_b, sums_c, sums_d):
    n, d = gq.shape
    half = lambda i: pl.BlockSpec((REACH_ONE, d), lambda *_: (0, i))
    return pl.pallas_call(
        lower_project_kernel,
        out_shape=[sds((d // 2, 3 * d + PAIR), bf16)] * 2 + [sds((n, d), f32)],
        grid=(1,),
        in_specs=[whole(n, d)] * 3
        + [half(0), half(1)] * 2
        + [whole(n, d)] * 3
        + [whole(1, d)]
        + [whole(d, d)] * 4
        + [whole(8, d), whole(24, d), whole(8, d)],
        out_specs=[whole(d // 2, 3 * d + PAIR)] * 2 + [whole(n, d)],
        scratch_shapes=[
            pltpu.VMEM((n, d), bf16),
            pltpu.VMEM((n, d), f32),
            pltpu.VMEM((d, n), bf16),
            pltpu.VMEM((PAIR, d), f32),
        ],
        **params(58, 12 * n * d * d, 24 * n * d),
    )(gq, gk, gv, left, left, right, right, normed, x, grad, gain, wq, wk, wv, perm, sums_b, sums_c, sums_d)


def lower_back_kernel(
    doc_order, seq_order, grad_c, hidden_b, normed, active, slope, mixed, wo, fgain, perm, up, down,
    up_keep, up_send, down_keep, down_send, grad_b, grad_mixed, sums,
    branch, grad_norm, normed_t, active_t, lifted,
):
    step = pl.program_id(0)
    n, d = grad_c.shape
    last = pl.num_programs(0) - 1

    @pl.when(step == 0)
    def _():
        branch[...] = grad_c[...].astype(bf16)
        normed_t[...] = by_owner(perm[...], normed[...])
        grad_norm[...] = jnp.zeros_like(grad_norm)

    @pl.when(step < last)
    def _():
        for rows in tiles(n, 256):
            g = (nt(branch[rows], down[...]) * slope[rows].astype(f32)).astype(bf16)
            grad_norm[rows] += nt(g, up[...])
            lifted[rows] = g
            place_hidden(seq_order, step, active[rows], rows, active_t)
        two_halves(active_t, branch, down_keep, down_send)
        two_halves(normed_t, lifted, up_keep, up_send)

    @pl.when(step == last)
    def _():
        finish_back(n, hidden_b, grad_c, fgain, grad_norm, grad_b, sums)
        for rows in tiles(n, 256):
            branch[rows] = grad_b[rows].astype(bf16)
            grad_mixed[rows] = nt(branch[rows], wo[...]).astype(bf16)
        normed_t[...] = by_owner(perm[...], mixed[...])
        two_halves(normed_t, branch, up_keep, up_send)


def lower_back(doc_order, seq_order, grad_c, hidden_b, normed, active, slope, mixed, wo, fgain, perm, up, down):
    n, d = grad_c.shape
    ff = up.shape[1]
    docs, seqs = doc_order.shape[0], seq_order.shape[0]
    fc = ff // docs
    into, outof, shapes = hidden_specs(d, ff, docs)
    lanes = pl.BlockSpec((n, fc), lambda c, *_: (0, jnp.minimum(c, docs - 1)))
    return pl.pallas_call(
        lower_back_kernel,
        out_shape=[*shapes, sds((n, d), f32), sds((n, d), bf16), sds((8, d), f32)],
        grid_spec=pltpu.PrefetchScalarGridSpec(
            num_scalar_prefetch=2,
            grid=(docs + 1,),
            in_specs=[
                whole(n, d), whole(n, d), whole(n, d), lanes, lanes, whole(n, d), whole(d, d), whole(1, d),
                whole(d, d), *into,
            ],
            out_specs=[*outof, whole(n, d), whole(n, d), whole(8, d)],
            scratch_shapes=[
                pltpu.VMEM((n, d), bf16), pltpu.VMEM((n, d), f32), pltpu.VMEM((d, n), bf16),
                hidden_scratch(n, fc, seqs), pltpu.VMEM((n, fc), bf16),
            ],
        ),
        **params(58, 8 * n * d * ff + 4 * n * d * d, 12 * n * ff + 30 * n * d),
    )(doc_order, seq_order, grad_c, hidden_b, normed, active, slope, mixed, wo, fgain, perm, up, down)


def shifted(value, steps):
    count = lax.axis_size("seq")
    pairs = [(i, i + steps) for i in range(count) if 0 <= i + steps < count]
    return lax.ppermute(value, "seq", pairs)


def exchanged(value, axis, bit):
    count = lax.axis_size(axis)
    return lax.ppermute(value, axis, [(i, i ^ bit) for i in range(count)])


def bits(axis, first=1):
    count = lax.axis_size(axis)
    return [(axis, 1 << b) for b in range(count.bit_length()) if first <= 1 << b < count]


def orders():
    cores = [("seq", 1)]
    return cores + bits("doc") + bits("seq", 2), cores + bits("doc")[::-1] + bits("seq", 2)


def owners(order):
    count = lax.axis_size("doc") * lax.axis_size("seq")
    flips = {"doc": [], "seq": []}
    for axis in flips:
        for p in range(count):
            flips[axis].append(sum(b for i, (a, b) in enumerate(order) if a == axis and p >> (len(order) - 1 - i) & 1))
    return tuple(lax.axis_index(a) ^ jnp.array(flips[a], jnp.int32) for a in ("doc", "seq"))


def permutation(order, d):
    doc, seq = owners(order)
    owner = doc * lax.axis_size("seq") + seq
    size = d // owner.shape[0]
    source = (owner[:, None] * size + jnp.arange(size, dtype=jnp.int32)[None, :]).reshape(-1)
    return (source[:, None] == jnp.arange(d, dtype=jnp.int32)[None, :]).astype(bf16)


def hidden_orders(order):
    def places(axis):
        steps = [b for a, b in order if a == axis]
        value = jnp.arange(lax.axis_size(axis), dtype=jnp.int32) ^ lax.axis_index(axis)
        place = jnp.zeros_like(value)
        for b in steps:
            place = 2 * place + (value // b) % 2
        return place

    return places("doc"), places("seq")


class Halving:
    def __init__(self, keep, send, order):
        self.order, self.at = order, 1
        self.terms = [keep, exchanged(send, *order[0])]

    def step(self):
        half = self.terms[0].shape[0] // 2
        send = self.total(half).astype(bf16)
        got = exchanged(send, *self.order[self.at])
        self.at += 1
        self.terms = [t[:half] for t in self.terms] + [got]

    def total(self, start=0):
        out = self.terms[0][start:].astype(f32)
        for t in self.terms[1:]:
            out = out + t[start:].astype(f32)
        return out


def stage(values, *halvings):
    values, terms = lax.optimization_barrier((values, [h.terms for h in halvings]))
    for h, t in zip(halvings, terms):
        h.terms = t
    return values


def summed(value, steps):
    for step in steps:
        value = value + exchanged(value, *step)
    return value


def merged(part, steps):
    for step in steps:
        other = exchanged(part, *step)
        tops = part[:, HDIM : HDIM + 1], other[:, HDIM : HDIM + 1]
        top = jnp.maximum(*tops)
        both = part * jnp.exp(tops[0] - top) + other * jnp.exp(tops[1] - top)
        row = lax.broadcasted_iota(jnp.int32, part.shape, 1)
        part = jnp.where(row == HDIM, top, both)
    return part


def body(
    tokens, cotangent, counts, positions, lower_again, lower_abias, lower_query, lower_key, lower_value, lower_out,
    lower_fgain, lower_fbias, lower_up, lower_down, upper_again, upper_abias, upper_query, upper_key, upper_value,
    upper_out, upper_fgain, upper_fbias, upper_up, upper_down, upper_kpool, upper_vpool,
):
    seq_count = lax.axis_size("seq")
    seq_index = lax.axis_index("seq")
    x, cot = tokens[0], cotangent[0]
    n, d = x.shape
    m = n // STRIDE
    row = lambda g: g.reshape(1, d)
    flags = jnp.stack([seq_index == 0, seq_index == seq_count - 1]).astype(jnp.int32)
    slot_count = positions.shape[1]
    slots = jnp.arange(slot_count, dtype=jnp.int32)
    place = jnp.where(slots < counts[0], positions[0] - seq_index * n, -1)
    sel = (place[:, None] == jnp.arange(n, dtype=jnp.int32)[None, :]).astype(bf16)
    kpool = jnp.pad(upper_kpool, ((0, 8 - TAPS), (0, 0)))
    vpool = jnp.pad(upper_vpool, ((0, 8 - TAPS), (0, 0)))
    taps = jnp.concatenate([kpool, vpool], axis=1)
    low_first, high_first = orders()
    perm_low, perm_high = permutation(low_first, d), permutation(high_first, d)
    doc_order, seq_order = hidden_orders(high_first)
    along = bits("seq")

    norm_a, qa, ka, va = project(x, row(lower_again), row(lower_abias), lower_query, lower_key, lower_value)
    ends = lambda rows: jnp.concatenate([ka[rows], va[rows]], axis=1)
    left = shifted(ends(slice(n - REACH_ONE, n)), 1)
    right = shifted(ends(slice(0, REACH_ONE)), -1)
    mixed_a, weights_a = local_attention(flags, qa, ka, va, left, right)
    (
        hidden_b, norm_b, active_b, slope_b, hidden_c, norm_c, qc, kc, vc, pooled, mine, to_left, to_right, asked_q,
    ) = lower_forward(
        x, mixed_a, lower_out, row(lower_fgain), row(lower_fbias), lower_up, lower_down, row(upper_again),
        row(upper_abias), upper_query, upper_key, upper_value, kpool, vpool, sel,
    )
    from_left = shifted(to_right, 1)
    from_right = shifted(to_left, -1)
    asked_q = summed(asked_q, along)
    near, weights_c, kw, vw = near_attention(flags, qc, pooled, from_left, from_right, mine, taps)
    part = asked_part(asked_q, kw, vw)
    part = merged(part, along)
    total = part[:, HDIM + 1 : HDIM + 2]
    logsum = jnp.broadcast_to(part[:, HDIM : HDIM + 1] + jnp.log(total), (d // PAIR, 8, 2 * slot_count))
    asked = part[:, :HDIM] / total
    asked = asked.reshape(d // PAIR, HDIM, 2, slot_count).transpose(3, 0, 2, 1).reshape(slot_count, d)

    (
        out, mixed_c, grad_d, grad_mixed_c, grad_asked, up_keep, up_send, down_keep, down_send, sums_d,
    ) = upper_both(
        doc_order, seq_order, hidden_c, near, asked.astype(bf16), sel, cot, upper_out, row(upper_fgain),
        row(upper_fbias), perm_low, upper_up, upper_down,
    )
    flat = lambda x: x.reshape(-1, d)
    gu_up = Halving(up_keep, up_send, low_first)
    gu_down = Halving(flat(down_keep), flat(down_send), high_first)
    grad_asked = summed(grad_asked, along)
    gq_near, gkw, gvw = near_back(qc, kw, vw, weights_c, grad_mixed_c)
    gkw, gvw, grad_asked = stage((gkw, gvw, grad_asked), gu_up, gu_down)
    gu_up.step()
    gu_down.step()
    gq_asked, gkw, gvw = asked_back(asked_q, kw, vw, logsum, asked, grad_asked, gkw, gvw)
    gq_asked = summed(gq_asked, along).astype(bf16)
    own = slice(SIDE, SIDE + m)
    both = lambda rows: jnp.concatenate([gkw[rows], gvw[rows]], axis=1)
    first_row = both(slice(SIDE, SIDE + 8))
    back_left = both(slice(0, SIDE))
    back_right = both(slice(SIDE + m, m + 2 * SIDE))
    got = shifted(jnp.concatenate([back_left, first_row], axis=0), -1)
    add_last, next_row = got[:SIDE], got[SIDE:]
    add_first = shifted(back_right, 1)
    next_row = next_row + back_right[:8]
    gw_keep, gw_send, grad_c, sums_c = upper_project_back(
        gq_near, gq_asked, sel, gkw[own], gvw[own], add_first, add_last, next_row, kc, vc,
        from_left[SIDE:].astype(f32), kpool, vpool, norm_c, hidden_c, grad_d, row(upper_again), upper_query, upper_key,
        upper_value, perm_high,
    )
    grad_c, gw_send = stage((grad_c, gw_send), gu_up, gu_down)
    gu_up.step()
    gu_down.step()
    gu_qkv = Halving(gw_keep, gw_send, high_first)
    up_keep, up_send, down_keep, down_send, grad_b, grad_mixed_a, sums_b = lower_back(
        doc_order, seq_order, grad_c, hidden_b, norm_b, active_b, slope_b, mixed_a, lower_out, row(lower_fgain),
        perm_low, lower_up, lower_down,
    )
    grad_mixed_a, up_send, down_send = stage((grad_mixed_a, up_send, down_send), gu_up, gu_down, gu_qkv)
    gl_up = Halving(up_keep, up_send, low_first)
    gl_down = Halving(flat(down_keep), flat(down_send), high_first)
    gu_up.step()
    gu_down.step()
    gu_qkv.step()
    gq, gk, gv, gkl, gvl, gkr, gvr = local_back(qa, ka, va, left, right, weights_a, grad_mixed_a)
    gq, gk, gv, gkl, gvl, gkr, gvr = stage((gq, gk, gv, gkl, gvl, gkr, gvr), gu_up, gu_down, gu_qkv, gl_up, gl_down)
    back_last = shifted(jnp.concatenate([gkl, gvl], axis=1), -1)
    back_first = shifted(jnp.concatenate([gkr, gvr], axis=1), 1)
    gl_up.step()
    gl_down.step()
    gu_up.step()
    gu_down.step()
    gu_qkv.step()
    gw_keep, gw_send, grad_in = lower_project_back(
        gq, gk, gv, back_first, back_last, norm_a, x, grad_b, row(lower_again), lower_query, lower_key, lower_value,
        perm_low, sums_b, sums_c, sums_d,
    )
    gw_send = stage(gw_send, gu_up, gu_down, gu_qkv)
    gl_qkv = Halving(gw_keep, gw_send, low_first)
    every = (gl_up, gl_down, gl_qkv, gu_up, gu_down, gu_qkv)
    while any(h.at < len(h.order) for h in every):
        for h in every:
            if h.at < len(h.order):
                h.step()
    gu_up, gu_down, gu_qkv, gl_up, gl_down, gl_qkv = (
        h.total() for h in (gu_up, gu_down, gu_qkv, gl_up, gl_down, gl_qkv)
    )
    small = gl_qkv[:, 3 * d :].T
    sums_a, sums_b, sums_c, sums_d = small[:8], small[8:16], small[16:40], small[40:48]
    ff = lower_up.shape[1]
    part = lambda got, i: got[:, i * d : (i + 1) * d]
    return (
        out[None],
        grad_in[None],
        sums_a[0],
        sums_a[1],
        part(gl_qkv, 0),
        part(gl_qkv, 1),
        part(gl_qkv, 2),
        gl_up[:, ff:],
        sums_b[0],
        sums_b[1],
        gl_up[:, :ff],
        gl_down,
        sums_c[16],
        sums_c[17],
        part(gu_qkv, 0),
        part(gu_qkv, 1),
        part(gu_qkv, 2),
        gu_up[:, ff:],
        sums_d[0],
        sums_d[1],
        gu_up[:, :ff],
        gu_down,
        sums_c[0:TAPS],
        sums_c[8 : 8 + TAPS],
    )


def solution(mesh):
    tokens = P("doc", "seq", None)
    every = ("doc", "seq")
    vector, matrix, taps = P(every), P(every, None), P(None, every)
    layer = (vector, vector, matrix, matrix, matrix, matrix, vector, vector, matrix, matrix)
    return jax.shard_map(
        body,
        mesh=mesh,
        in_specs=(tokens, tokens, P("doc"), P("doc", None)) + (P(),) * 22,
        out_specs=(tokens, tokens) + layer + layer + (taps, taps),
        check_vma=False,
    )
```

```python
import functools

import jax
import jax.numpy as jnp
from jax import lax
from jax.experimental import pallas as pl
from jax.experimental.pallas import tpu as pltpu
from jax.sharding import PartitionSpec as P

HDIM = 64
REACH_ONE = 64
REACH_TWO = 256
STRIDE = 4
TAPS = 5
QB = 128
PAIR = 2 * HDIM
WIN_ONE = QB + 2 * REACH_ONE
SIDE = REACH_TWO // STRIDE
WIN_TWO = QB // STRIDE + 2 * SIDE
RAW = 16
eps = 1e-05
GROUP = 6
far_below = -1e30
scale = HDIM**-0.5
f32 = jnp.float32
bf16 = jnp.bfloat16

MILLS = 0.34
MILLS_POLY = (
    0.13590356504727755,
    0.13101844409724564,
    0.1513778923259517,
    -0.01998659482308463,
    0.25210690821609844,
    -0.1936388145328779,
    0.04321858184569336,
)
INV_SQRT_2PI = 0.3989422804014327


def nn(a, b):
    return lax.dot_general(a, b, (((1,), (0,)), ((), ())), preferred_element_type=f32)


def nt(a, b):
    return lax.dot_general(a, b, (((1,), (1,)), ((), ())), preferred_element_type=f32)


def tn(a, b):
    return lax.dot_general(a, b, (((0,), (0,)), ((), ())), preferred_element_type=f32)


def norm_rows(x, gain, bias):
    average = jnp.mean(x, axis=-1, keepdims=True)
    centred = x - average
    variance = jnp.mean(centred * centred, axis=-1, keepdims=True)
    return centred * lax.rsqrt(variance + eps) * gain + bias


def norm_back(x, gain, grad):
    average = jnp.mean(x, axis=-1, keepdims=True)
    centred = x - average
    variance = jnp.mean(centred * centred, axis=-1, keepdims=True)
    spread = lax.rsqrt(variance + eps)
    unit = centred * spread
    lifted = grad * gain
    first = jnp.mean(lifted, axis=-1, keepdims=True)
    second = jnp.mean(lifted * unit, axis=-1, keepdims=True)
    back = spread * (lifted - first - unit * second)
    return back, jnp.sum(grad * unit, axis=0, keepdims=True), jnp.sum(grad, axis=0, keepdims=True)


def gelu_both(u):
    t = 1.0 / (1.0 + MILLS * jnp.abs(u))
    e = jnp.exp(-0.5 * (u * u))
    poly = jnp.full_like(u, MILLS_POLY[-1])
    for c in MILLS_POLY[-2::-1]:
        poly = poly * t + c
    tail = poly * (t * e)
    cdf = jnp.where(u >= 0, 1.0 - tail, tail)
    return u * cdf, cdf + u * e * INV_SQRT_2PI


def whole(*shape):
    return pl.BlockSpec(shape, lambda *_: (0,) * len(shape), pipeline_mode=pl.Buffered(1))


def smem():
    return pl.BlockSpec(memory_space=pltpu.SMEM)


def params(flops, size, mib=58):
    return dict(
        compiler_params=pltpu.CompilerParams(vmem_limit_bytes=mib << 20),
        cost_estimate=pl.CostEstimate(flops=flops, bytes_accessed=size, transcendentals=0),
    )


def sds(shape, dtype):
    return jax.ShapeDtypeStruct(shape, dtype)


def anywhere():
    return pl.BlockSpec(memory_space=pl.ANY)


class Mover:
    def __init__(self, sources, buffers, sems):
        self.buffers = buffers
        self.copies = [pltpu.make_async_copy(s, b, sems.at[i]) for i, (s, b) in enumerate(zip(sources, buffers))]

    def start(self, *which):
        for i in which or range(len(self.copies)):
            self.copies[i].start()

    def wait(self, *which):
        for i in which or range(len(self.copies)):
            self.copies[i].wait()

    def got(self, i):
        self.copies[i].wait()
        return self.buffers[i]


def moved_call(kernel, ins, outs, scratch, cost):
    def body(*refs):
        n_in, n_out = len(ins), len(outs)
        sources, targets, rest = refs[:n_in], refs[n_in : n_in + n_out], refs[n_in + n_out :]
        in_bufs, out_bufs, rest = rest[:n_in], rest[n_in : n_in + n_out], rest[n_in + n_out :]
        in_sems, out_sems, *rest = rest
        came = Mover(sources, in_bufs, in_sems)
        came.start()
        gone = Mover(out_bufs, targets, out_sems)
        kernel(came, out_bufs, gone, *rest)
        gone.wait()

    return pl.pallas_call(
        body,
        out_shape=list(outs),
        in_specs=[anywhere()] * len(ins),
        out_specs=[anywhere()] * len(outs),
        scratch_shapes=[pltpu.VMEM(x.shape, x.dtype) for x in (*ins, *outs)]
        + [pltpu.SemaphoreType.DMA((len(ins),)), pltpu.SemaphoreType.DMA((len(outs),))]
        + scratch,
        **params(*cost),
    )(*ins)


def tiles(rows, step):
    return [slice(i, i + step) for i in range(0, rows, step)]


def project_kernel(came, outs, gone):
    x, gain, bias = (came.got(i) for i in range(3))
    normed = outs[0]
    parts = tiles(x.shape[0], 256)
    for rows in parts:
        normed[rows] = norm_rows(x[rows].astype(f32), gain[...], bias[...]).astype(bf16)
    gone.start(0)
    for i in range(1, 4):
        w = came.got(2 + i)
        for rows in parts:
            outs[i][rows] = nn(normed[rows], w[...]).astype(bf16)
        gone.start(i)


def project(x, gain, bias, wk, wv, wq):
    n, d = x.shape
    return moved_call(
        project_kernel, (x, gain, bias, wk, wv, wq), [sds((n, d), bf16)] * 4, [], (6 * n * d * d, 10 * n * d + 6 * d * d)
    )


def head_masks(rows):
    lane = lax.broadcasted_iota(jnp.int32, (rows, PAIR), 1)
    return lane < HDIM


def both_heads(x):
    first = head_masks(x.shape[0])
    zero = jnp.zeros_like(x)
    return jnp.concatenate([jnp.where(first, x, zero), jnp.where(first, zero, x)], axis=0)


def own_blocks(x):
    n = x.shape[1] // 2
    return jnp.concatenate([x[:HDIM, :n], x[HDIM:, n:]], axis=0).T


def softmax_columns(scores):
    top = jnp.max(scores, axis=0, keepdims=True)
    raised = jnp.exp(scores - top)
    total = jnp.sum(raised, axis=0, keepdims=True)
    return (raised * (1.0 / total)).astype(bf16)


def window_bias(kind):
    win = WIN_ONE if kind == 1 else WIN_TWO
    key = lax.broadcasted_iota(jnp.int32, (win, QB), 0)
    query = lax.broadcasted_iota(jnp.int32, (win, QB), 1)
    if kind == 1:
        offset, reach = key - query, 2 * REACH_ONE
    else:
        offset, reach = STRIDE * key - query, 2 * REACH_TWO
    return jnp.where((offset >= 0) & (offset <= reach), 0.0, far_below)


def edge_bias(bias, start, edge, length, flags):
    win = bias.shape[0]
    key = lax.broadcasted_iota(jnp.int32, bias.shape, 0) + start
    if start < edge:
        limit = jnp.where(flags[0] > 0, edge, 0)
        bias = jnp.where(key < limit, far_below, bias)
    if start + win > length - edge:
        limit = jnp.where(flags[1] > 0, length - edge, length)
        bias = jnp.where(key >= limit, far_below, bias)
    return bias


def attend_blocks(blocks):
    scores = [nt(kb, both_heads(qb * scale)) for qb, kb, _, _ in blocks]
    weights = [softmax_columns(s + jnp.concatenate([b[3], b[3]], axis=1)) for s, b in zip(scores, blocks)]
    outs = [tn(b[2], w) for b, w in zip(blocks, weights)]
    return [own_blocks(o) for o in outs], weights


def back_blocks(blocks):
    grads = [both_heads(grad) for *_, grad in blocks]
    changes = [nt(b[2], g) for b, g in zip(blocks, grads)]
    values = [nn(b[3], g) for b, g in zip(blocks, grads)]
    scores = []
    for b, change in zip(blocks, changes):
        share = b[3].astype(f32)
        inner = jnp.sum(share * change, axis=0, keepdims=True) / jnp.sum(share, axis=0, keepdims=True)
        scores.append((share * (change - inner)).astype(bf16))
    keys = [nn(g, both_heads(b[0] * scale)) for g, b in zip(scores, blocks)]
    queries = [own_blocks(tn(b[1], g)) * scale for g, b in zip(scores, blocks)]
    return queries, keys, values


def local_kernel(flags, q, k, v, kl, vl, kr, vr, out, weights, kw, vw, base):
    n = q.shape[0]

    @pl.when(pl.program_id(0) == 0)
    def _():
        base[...] = window_bias(1)

    for wide, left, own, right in ((kw, kl, k, kr), (vw, vl, v, vr)):
        wide[:REACH_ONE] = left[...]
        wide[REACH_ONE : REACH_ONE + n] = own[...]
        wide[REACH_ONE + n :] = right[...]
    todo = []
    for b, rows in enumerate(tiles(n, QB)):
        window = slice(b * QB, b * QB + WIN_ONE)
        bias = edge_bias(base[...], b * QB, REACH_ONE, n + 2 * REACH_ONE, flags)
        todo.append((q[rows], kw[window], vw[window], bias))
    for b in range(0, len(todo), GROUP):
        for i, (mixed, w) in enumerate(zip(*attend_blocks(todo[b : b + GROUP]))):
            out[(b + i) * QB : (b + i + 1) * QB] = mixed.astype(bf16)
            weights[0, b + i] = w


def pair_block(rows, offset=0):
    return pl.BlockSpec((rows, PAIR), lambda g, offset=offset: (0, g + offset))


def two_rows(rows):
    return pl.BlockSpec((2, rows, PAIR), lambda g: (0, 0, g))


def local_attention(flags, q, k, v, left, right):
    n, d = q.shape
    pairs, blocks = d // PAIR, n // QB
    wide = n + 2 * REACH_ONE
    return pl.pallas_call(
        local_kernel,
        out_shape=[sds((n, d), bf16), sds((pairs, blocks, WIN_ONE, 2 * QB), bf16)],
        grid=(pairs,),
        in_specs=[smem()]
        + [pair_block(n)] * 3
        + [pair_block(REACH_ONE), pair_block(REACH_ONE, pairs)] * 2,
        out_specs=[
            pair_block(n),
            pl.BlockSpec((1, blocks, WIN_ONE, 2 * QB), lambda g: (g, 0, 0, 0)),
        ],
        scratch_shapes=[
            pltpu.VMEM((wide, PAIR), bf16),
            pltpu.VMEM((wide, PAIR), bf16),
            pltpu.VMEM((WIN_ONE, QB), f32),
        ],
        **params(4 * n * WIN_ONE * d * 2, 12 * n * d),
    )(flags, q, k, v, left, left, right, right)


def local_back_kernel(
    q, k, v, kl, vl, kr, vr, weights, grad, gq, gk, gv, to_left, to_right, kw, vw, ka, va
):
    n = q.shape[0]
    for wide, left, own, right in ((kw, kl, k, kr), (vw, vl, v, vr)):
        wide[:REACH_ONE] = left[...]
        wide[REACH_ONE : REACH_ONE + n] = own[...]
        wide[REACH_ONE + n :] = right[...]
    ka[...] = jnp.zeros_like(ka)
    va[...] = jnp.zeros_like(va)
    todo = []
    for b, rows in enumerate(tiles(n, QB)):
        window = slice(b * QB, b * QB + WIN_ONE)
        todo.append((q[rows], kw[window], vw[window], weights[0, b], grad[rows]))
    for first in range(0, len(todo), GROUP):
        for i, (gqb, gkb, gvb) in enumerate(zip(*back_blocks(todo[first : first + GROUP]))):
            b = first + i
            window = slice(b * QB, b * QB + WIN_ONE)
            gq[b * QB : (b + 1) * QB] = gqb.astype(bf16)
            ka[window] += gkb
            va[window] += gvb
    for i, (wide, own) in enumerate(((ka, gk), (va, gv))):
        to_left[i] = wide[:REACH_ONE]
        own[...] = wide[REACH_ONE : REACH_ONE + n]
        to_right[i] = wide[REACH_ONE + n :]


def local_back(q, k, v, left, right, weights, grad):
    n, d = q.shape
    pairs, blocks = d // PAIR, n // QB
    wide = n + 2 * REACH_ONE
    return pl.pallas_call(
        local_back_kernel,
        out_shape=[sds((n, d), bf16), sds((n, d), f32), sds((n, d), f32)] + [sds((2, REACH_ONE, d), f32)] * 2,
        grid=(pairs,),
        in_specs=[pair_block(n)] * 3
        + [pair_block(REACH_ONE), pair_block(REACH_ONE, pairs)] * 2
        + [pl.BlockSpec((1, blocks, WIN_ONE, 2 * QB), lambda g: (g, 0, 0, 0))]
        + [pair_block(n)],
        out_specs=[pair_block(n)] * 3 + [two_rows(REACH_ONE)] * 2,
        scratch_shapes=[pltpu.VMEM((wide, PAIR), bf16)] * 2 + [pltpu.VMEM((wide, PAIR), f32)] * 2,
        **params(10 * n * WIN_ONE * d * 2, 24 * n * d),
    )(q, k, v, left, left, right, right, weights, grad)


def first_pooled(tile, rim, raw, taps):
    row = (
        taps[0:1] * rim[0:1].astype(f32)
        + taps[1:2] * rim[1:2].astype(f32)
        + taps[2:3] * raw[0:1].astype(f32)
        + taps[3:4] * raw[1:2].astype(f32)
        + taps[4:5] * raw[2:3].astype(f32)
    )
    first = lax.broadcasted_iota(jnp.int32, tile.shape, 0) == 0
    return jnp.where(first, row, tile.astype(f32)).astype(bf16)


def pooled_window(wide, left, own, right, mine, taps):
    n = own.shape[0]
    wide[:SIDE] = left[:SIDE]
    wide[SIDE : SIDE + n] = own[...]
    wide[SIDE + n :] = right[:SIDE]
    rim = left[SIDE:].astype(f32)[RAW - 2 :]
    raw = mine[:RAW].astype(f32)
    wide[SIDE : SIDE + RAW] = first_pooled(own[:RAW], rim, raw, taps)
    rim = mine[RAW:].astype(f32)[RAW - 2 :]
    raw = right[SIDE:].astype(f32)
    wide[SIDE + n : SIDE + n + RAW] = first_pooled(right[:RAW], rim, raw, taps)


def near_kernel(flags, q, pk, pv, lk, lv, rk, rv, mk, mv, tk, tv, out, weights, kw, vw, base):
    n = q.shape[0]

    @pl.when(pl.program_id(0) == 0)
    def _():
        base[...] = window_bias(2)

    pooled_window(kw, lk, pk, rk, mk, tk[...])
    pooled_window(vw, lv, pv, rv, mv, tv[...])
    step = QB // STRIDE
    todo = []
    for b, rows in enumerate(tiles(n, QB)):
        window = slice(b * step, b * step + WIN_TWO)
        bias = edge_bias(base[...], b * step, SIDE, kw.shape[0], flags)
        todo.append((q[rows], kw[window], vw[window], bias))
    for b in range(0, len(todo), GROUP):
        for i, (mixed, w) in enumerate(zip(*attend_blocks(todo[b : b + GROUP]))):
            out[(b + i) * QB : (b + i + 1) * QB] = mixed.astype(bf16)
            weights[0, b + i] = w


def near_attention(flags, q, pooled, left, right, mine, taps):
    n, d = q.shape
    pairs, blocks, m = d // PAIR, n // QB, n // STRIDE
    wide = m + 2 * SIDE
    two = lambda rows: [pair_block(rows), pair_block(rows, pairs)]
    return pl.pallas_call(
        near_kernel,
        out_shape=[
            sds((n, d), bf16),
            sds((pairs, blocks, WIN_TWO, 2 * QB), bf16),
            sds((wide, d), bf16),
            sds((wide, d), bf16),
        ],
        grid=(pairs,),
        in_specs=[smem(), pair_block(n)] + two(m) + two(SIDE + RAW) * 2 + two(2 * RAW) + two(8),
        out_specs=[
            pair_block(n),
            pl.BlockSpec((1, blocks, WIN_TWO, 2 * QB), lambda g: (g, 0, 0, 0)),
            pair_block(wide),
            pair_block(wide),
        ],
        scratch_shapes=[pltpu.VMEM((WIN_TWO, QB), f32)],
        **params(4 * n * WIN_TWO * d * 2, 10 * n * d),
    )(flags, q, pooled, pooled, left, left, right, right, mine, mine, taps, taps)


def asked_kernel(q, kw, vw, out):
    own = slice(SIDE, kw.shape[0] - SIDE)
    slots = q.shape[0]
    column = lax.broadcasted_iota(jnp.int32, (HDIM, 2 * slots), 1)
    row = lax.broadcasted_iota(jnp.int32, (8, 2 * slots), 0)
    parts = tiles(q.shape[1], PAIR)
    scores = [nt(kw[own, c], both_heads(q[:, c] * scale)) for c in parts]
    tops = [jnp.max(s, axis=0, keepdims=True) for s in scores]
    raised = [jnp.exp(s - top).astype(bf16) for s, top in zip(scores, tops)]
    sums = [tn(vw[own, c], r) for c, r in zip(parts, raised)]
    for g, (top, r, x) in enumerate(zip(tops, raised, sums)):
        total = jnp.sum(r.astype(f32), axis=0, keepdims=True)
        out[g, :HDIM] = jnp.where(column < slots, x[:HDIM], x[HDIM:])
        out[g, HDIM:] = jnp.where(row == 0, top, jnp.where(row == 1, total, 0.0))


def asked_part(q, kw, vw):
    slots, d = q.shape
    pairs, wide = d // PAIR, kw.shape[0]
    return pl.pallas_call(
        asked_kernel,
        out_shape=sds((pairs, HDIM + 8, 2 * slots), f32),
        grid=(1,),
        in_specs=[whole(slots, d), whole(wide, d), whole(wide, d)],
        out_specs=whole(pairs, HDIM + 8, 2 * slots),
        **params(4 * slots * wide * d, 4 * wide * d),
    )(q, kw, vw)


def near_back_kernel(q, kw, vw, weights, grad, gq, own, to_left, to_right, gk, gv):
    n = q.shape[0]
    gk[...] = jnp.zeros_like(gk)
    gv[...] = jnp.zeros_like(gv)
    step = QB // STRIDE
    todo = []
    for b, rows in enumerate(tiles(n, QB)):
        window = slice(b * step, b * step + WIN_TWO)
        todo.append((q[rows], kw[window], vw[window], weights[0, b], grad[rows]))
    for first in range(0, len(todo), GROUP):
        for i, (gqb, gkb, gvb) in enumerate(zip(*back_blocks(todo[first : first + GROUP]))):
            b = first + i
            window = slice(b * step, b * step + WIN_TWO)
            gq[b * QB : (b + 1) * QB] = gqb.astype(bf16)
            gk[window] += gkb
            gv[window] += gvb
    m = gk.shape[0] - 2 * SIDE
    for i, wide in enumerate((gk, gv)):
        own[i] = wide[SIDE : SIDE + m]
        to_left[i] = wide[: SIDE + 8]
        to_right[i] = wide[SIDE + m :]


def near_back(q, kw, vw, weights, grad):
    n, d = q.shape
    pairs, blocks, wide = d // PAIR, n // QB, kw.shape[0]
    sizes = (wide - 2 * SIDE, SIDE + 8, SIDE)
    return pl.pallas_call(
        near_back_kernel,
        out_shape=[sds((n, d), bf16)] + [sds((2, r, d), f32) for r in sizes],
        grid=(pairs,),
        in_specs=[pair_block(n), pair_block(wide), pair_block(wide)]
        + [pl.BlockSpec((1, blocks, WIN_TWO, 2 * QB), lambda g: (g, 0, 0, 0))]
        + [pair_block(n)],
        out_specs=[pair_block(n)] + [two_rows(r) for r in sizes],
        scratch_shapes=[pltpu.VMEM((wide, PAIR), f32)] * 2,
        **params(10 * n * WIN_TWO * d * 2, 20 * n * d),
    )(q, kw, vw, weights, grad)


def asked_back_kernel(flags, q, kw, vw, logsum, mixed, grad, near, near_next, gq, own, following):
    m = near.shape[1]
    reach = slice(SIDE, SIDE + m + RAW)
    slots = q.shape[0]
    open_end = jnp.where(flags[1] > 0, 0.0, 1.0)
    parts = tiles(q.shape[1], PAIR)
    queries = [both_heads(q[:, c] * scale) for c in parts]
    grads = [both_heads(grad[:, c]) for c in parts]
    scores = [nt(kw[reach, c], x) for c, x in zip(parts, queries)]
    changes = [nt(vw[reach, c], x) for c, x in zip(parts, grads)]
    weights = [jnp.exp(s - logsum[g, 0:1]) for g, s in enumerate(scores)]
    values = [nn(w.astype(bf16), x) for w, x in zip(weights, grads)]
    grad_scores = []
    for c, w, change in zip(parts, weights, changes):
        by_feature = (grad[:, c].astype(f32) * mixed[:, c]).T
        inner = [jnp.sum(by_feature[rows], axis=0, keepdims=True) for rows in tiles(PAIR, HDIM)]
        grad_scores.append((w * (change - jnp.concatenate(inner, axis=1))).astype(bf16))
    keys = [nn(x, y) for x, y in zip(grad_scores, queries)]
    backs = [tn(x[:m], kw[reach, c][:m]) * scale for c, x in zip(parts, grad_scores)]
    for c, key, value, back in zip(parts, keys, values, backs):
        for i, wide in enumerate((key, value)):
            own[i, :, c] = near[i, :, c] + wide[:m]
            following[i, :, c] = (near_next[i, :, c] + wide[m : m + 8]) * open_end
        gq[:, c] = jnp.where(head_masks(slots), back[:slots], back[slots:]).astype(bf16)


def asked_back(flags, q, kw, vw, logsum, mixed, grad, near, near_next):
    slots, d = q.shape
    pairs, wide, m = d // PAIR, kw.shape[0], near.shape[1]
    return pl.pallas_call(
        asked_back_kernel,
        out_shape=[sds((slots, d), bf16), sds((2, m, d), f32), sds((2, 8, d), f32)],
        grid=(1,),
        in_specs=[
            smem(), whole(slots, d), whole(wide, d), whole(wide, d), whole(pairs, 8, 2 * slots), whole(slots, d),
            whole(slots, d), whole(2, m, d), whole(2, 8, d),
        ],
        out_specs=[whole(slots, d), whole(2, m, d), whole(2, 8, d)],
        **params(10 * slots * wide * d, 20 * wide * d),
    )(flags, q, kw, vw, logsum, mixed, grad, near, near_next)


def pool_rows(held, taps):
    m = (held.shape[0] - 8) // STRIDE
    total = taps[0:1] * held[pl.ds(6, m, stride=STRIDE)]
    for t in range(1, TAPS):
        total = total + taps[t : t + 1] * held[pl.ds(6 + t, m, stride=STRIDE)]
    return total.astype(bf16)


def lower_kernel(
    x, mixed, wo, fgain, fbias, up, down, again, abias, wq, wk, wv, kpool, vpool, sel,
    hidden_b, normed_b, active, slope, hidden_c, normed_c, q, k, v, pooled, mine, to_left, to_right, asked,
    held,
):
    step = pl.program_id(0)
    n, d = x.shape

    @pl.when(step == 0)
    def _():
        for rows in tiles(n, 256):
            h = x[rows].astype(f32) + nn(mixed[rows], wo[...])
            hidden_b[rows] = h
            hidden_c[rows] = h
            normed_b[rows] = norm_rows(h, fgain[...], fbias[...]).astype(bf16)

    for rows in tiles(n, 256):
        a, s = gelu_both(nn(normed_b[rows], up[...]))
        a = a.astype(bf16)
        active[rows] = a
        slope[rows] = s.astype(bf16)
        hidden_c[rows] += nn(a, down[...])

    @pl.when(step == pl.num_programs(0) - 1)
    def _():
        for rows in tiles(n, 256):
            normed_c[rows] = norm_rows(hidden_c[rows], again[...], abias[...]).astype(bf16)
            q[rows] = nn(normed_c[rows], wq[...]).astype(bf16)
        m = n // STRIDE
        held[:, :8] = jnp.zeros((d // PAIR, 8, PAIR), f32)
        for w, out, taps, lanes in ((wk, k, kpool, slice(0, d)), (wv, v, vpool, slice(d, 2 * d))):
            for rows in tiles(n, 256):
                made = nn(normed_c[rows], w[...]).astype(bf16)
                out[rows] = made
                for i, c in enumerate(tiles(d, PAIR)):
                    held[i, 8 + rows.start : 8 + rows.stop] = made[:, c].astype(f32)
            for i, c in enumerate(tiles(d, PAIR)):
                part = slice(lanes.start + c.start, lanes.start + c.stop)
                pooled[:, part] = pool_rows(held.at[i], taps[:, c])
            mine[:RAW, lanes] = out[:RAW]
            mine[RAW:, lanes] = out[n - RAW :]
        to_right[:SIDE] = pooled[m - SIDE :]
        to_right[SIDE:] = mine[RAW:]
        to_left[:SIDE] = pooled[:SIDE]
        to_left[SIDE:] = mine[:RAW]
        asked[...] = nn(sel[...], q[...]).astype(bf16)


def lower_forward(x, mixed, wo, fgain, fbias, up, down, again, abias, wq, wk, wv, kpool, vpool, sel):
    n, d = x.shape
    ff, slots, m = up.shape[1], sel.shape[0], n // STRIDE
    fc = 512
    return pl.pallas_call(
        lower_kernel,
        out_shape=[
            sds((n, d), f32), sds((n, d), bf16), sds((n, ff), bf16), sds((n, ff), bf16), sds((n, d), f32),
            sds((n, d), bf16), sds((n, d), bf16), sds((n, d), bf16), sds((n, d), bf16),
            sds((m, 2 * d), bf16), sds((2 * RAW, 2 * d), bf16), sds((SIDE + RAW, 2 * d), bf16),
            sds((SIDE + RAW, 2 * d), bf16), sds((slots, d), bf16),
        ],
        grid=(ff // fc,),
        in_specs=[
            whole(n, d), whole(n, d), whole(d, d), whole(1, d), whole(1, d),
            pl.BlockSpec((d, fc), lambda c: (0, c)), pl.BlockSpec((fc, d), lambda c: (c, 0)),
            whole(1, d), whole(1, d), whole(d, d), whole(d, d), whole(d, d), whole(8, d), whole(8, d),
            whole(slots, n),
        ],
        out_specs=[
            whole(n, d), whole(n, d), pl.BlockSpec((n, fc), lambda c: (0, c)),
            pl.BlockSpec((n, fc), lambda c: (0, c)), whole(n, d), whole(n, d), whole(n, d), whole(n, d),
            whole(n, d), whole(m, 2 * d), whole(2 * RAW, 2 * d), whole(SIDE + RAW, 2 * d),
            whole(SIDE + RAW, 2 * d), whole(slots, d),
        ],
        scratch_shapes=[pltpu.VMEM((d // PAIR, n + 8, PAIR), f32)],
        **params(4 * n * d * ff + 8 * n * d * d, 8 * n * ff + 40 * n * d),
    )(x, mixed, wo, fgain, fbias, up, down, again, abias, wq, wk, wv, kpool, vpool, sel)


def by_owner(perm, x):
    return nt(perm, x).astype(bf16)


def place_hidden(order, group, chunk, rows, wide):
    count = order.shape[0]
    held = chunk.T
    size = held.shape[0] // count
    for s in range(count):
        start = pl.multiple_of(order[s] * size, size)
        wide[pl.ds(start, size), rows] = held[s * size : (s + 1) * size].astype(wide.dtype)


def hidden_scratch(n, fc, seqs):
    return pltpu.VMEM((fc, n), f32 if fc // seqs % 16 else bf16)


def two_halves(left, right, first, second):
    half = left.shape[0] // 2
    first[...] = nn(left[:half].astype(bf16), right[...]).astype(bf16).reshape(first.shape)
    second[...] = nn(left[half:].astype(bf16), right[...]).astype(bf16).reshape(second.shape)


def finish_back(n, hidden, grad, gain, grad_norm, grad_hidden, sums):
    sums[...] = jnp.zeros_like(sums)
    for rows in tiles(n, 128):
        back, by_gain, by_bias = norm_back(hidden[rows], gain[...], grad_norm[rows])
        grad_hidden[rows] = grad[rows].astype(f32) + back
        sums[0:1] += by_gain
        sums[1:2] += by_bias


def hidden_specs(d, ff, docs, more=1):
    fc = ff // docs
    last = docs - 1
    into = [
        pl.BlockSpec((d, fc), lambda c, *_: (0, jnp.minimum(c, last))),
        pl.BlockSpec((fc, d), lambda c, *_: (jnp.minimum(c, last), 0)),
    ]
    lanes = pl.BlockSpec((d // 2, fc), lambda c, *_: (0, c))
    rows = pl.BlockSpec(
        (1, fc // 2, d), lambda c, docs, *_: (docs[jnp.minimum(c, last)], 0, 0)
    )
    out = [lanes, lanes, rows, rows]
    shapes = [sds((d // 2, ff + more * d), bf16)] * 2 + [sds((docs, fc // 2, d), bf16)] * 2
    return into, out, shapes


def upper_kernel(
    doc_order, seq_order, hidden_c, near, asked, sel, cot, wo, fgain, fbias, perm, up, down,
    out, mixed, grad_d, grad_mixed, grad_asked, up_keep, up_send, down_keep, down_send, sums,
    hidden_d, normed, hidden_e, grad_norm, flag, normed_t, active_t, lifted,
):
    step = pl.program_id(0)
    n, d = near.shape
    last = pl.num_programs(0) - 1

    @pl.when(step == 0)
    def _():
        slots = sel.shape[0]
        flag[...] = tn(sel[...], jnp.ones((slots, PAIR), bf16))
        for rows in tiles(n, 256):
            here = jnp.concatenate([flag[rows]] * (d // PAIR), axis=1) > 0.5
            placed = tn(sel[:, rows], asked[...])
            mixed[rows] = jnp.where(here, placed, near[rows].astype(f32)).astype(bf16)
            h = hidden_c[rows] + nn(mixed[rows], wo[...])
            hidden_d[rows] = h
            hidden_e[rows] = h
            normed[rows] = norm_rows(h, fgain[...], fbias[...]).astype(bf16)
        normed_t[...] = by_owner(perm[...], normed[...])
        grad_norm[...] = jnp.zeros_like(grad_norm)

    @pl.when(step < last)
    def _():
        for rows in tiles(n, 256):
            a, s = gelu_both(nn(normed[rows], up[...]))
            a = a.astype(bf16)
            hidden_e[rows] += nn(a, down[...])
            place_hidden(seq_order, step, a, rows, active_t)
            g = (nt(cot[rows], down[...]) * s).astype(bf16)
            grad_norm[rows] += nt(g, up[...])
            lifted[rows] = g
        two_halves(normed_t, lifted, up_keep, up_send)
        two_halves(active_t, cot, down_keep, down_send)

    @pl.when(step == last)
    def _():
        for rows in tiles(n, 256):
            out[rows] = hidden_e[rows].astype(bf16)
        finish_back(n, hidden_d, cot, fgain, grad_norm, grad_d, sums)
        for rows in tiles(n, 256):
            branch = grad_d[rows].astype(bf16)
            lifted[rows] = branch
            grad_mixed[rows] = nt(branch, wo[...]).astype(bf16)
        normed_t[...] = by_owner(perm[...], mixed[...])
        two_halves(normed_t, lifted, up_keep, up_send)
        grad_asked[...] = nn(sel[...], grad_mixed[...]).astype(bf16)
        for rows in tiles(n, 256):
            here = jnp.concatenate([flag[rows]] * (d // PAIR), axis=1) > 0.5
            g = grad_mixed[rows]
            grad_mixed[rows] = jnp.where(here, 0.0, g.astype(f32)).astype(bf16)


def upper_both(doc_order, seq_order, hidden_c, near, asked, sel, cot, wo, fgain, fbias, perm, up, down):
    n, d = near.shape
    ff, slots = up.shape[1], sel.shape[0]
    docs, seqs = doc_order.shape[0], seq_order.shape[0]
    into, outof, shapes = hidden_specs(d, ff, docs)
    fc = ff // docs
    return pl.pallas_call(
        upper_kernel,
        out_shape=[
            sds((n, d), bf16), sds((n, d), bf16), sds((n, d), f32), sds((n, d), bf16), sds((slots, d), bf16),
            *shapes, sds((8, d), f32),
        ],
        grid_spec=pltpu.PrefetchScalarGridSpec(
            num_scalar_prefetch=2,
            grid=(docs + 1,),
            in_specs=[
                whole(n, d), whole(n, d), whole(slots, d), whole(slots, n), whole(n, d), whole(d, d), whole(1, d),
                whole(1, d), whole(d, d), *into,
            ],
            out_specs=[
                whole(n, d), whole(n, d), whole(n, d), whole(n, d), whole(slots, d), *outof, whole(8, d),
            ],
            scratch_shapes=[
                pltpu.VMEM((n, d), f32), pltpu.VMEM((n, d), bf16), pltpu.VMEM((n, d), f32), pltpu.VMEM((n, d), f32),
                pltpu.VMEM((n, PAIR), f32), pltpu.VMEM((d, n), bf16), hidden_scratch(n, fc, seqs),
                pltpu.VMEM((n, fc), bf16),
            ],
        ),
        **params(12 * n * d * ff + 6 * n * d * d, 8 * d * ff + 40 * n * d),
    )(doc_order, seq_order, hidden_c, near, asked, sel, cot, wo, fgain, fbias, perm, up, down)


def unpool(held, gp, following, taps, made):
    m = gp.shape[0]
    last = lax.broadcasted_iota(jnp.int32, gp.shape, 0) == m - 1
    later = jnp.where(last, following, pltpu.roll(gp, m - 1, 0))
    made[pl.ds(0, m, stride=STRIDE)] = taps[2:3] * gp
    made[pl.ds(1, m, stride=STRIDE)] = taps[3:4] * gp
    made[pl.ds(2, m, stride=STRIDE)] = taps[4:5] * gp + taps[0:1] * later
    made[pl.ds(3, m, stride=STRIDE)] = taps[1:2] * later
    return [
        jnp.sum(gp * held[pl.ds(6 + t, m, stride=STRIDE)], axis=0, keepdims=True) for t in range(TAPS)
    ]


def upper_pairs_kernel(came, outs, gone, gkv, held, made, normed_t):
    gw_keep, gw_send, grad_norm, sums = outs
    normed, perm = came.got(0), came.got(1)
    normed_t[...] = by_owner(perm[...], normed[...])
    gp, from_left, from_right, following, rim = (came.got(i) for i in range(2, 7))
    sums[...] = jnp.zeros_like(sums)
    n, d = normed.shape
    m = n // STRIDE
    for i in range(2):
        x, taps, w = (came.got(7 + 3 * i + j) for j in range(3))
        for c in tiles(d, PAIR):
            held[:8] = rim[RAW - 8 :, i * d + c.start : i * d + c.stop].astype(f32)
            held[8:] = x[:, c].astype(f32)
            total = gp[i, :, c]
            edge = jnp.zeros((m - 2 * SIDE, PAIR), f32)
            total = total + jnp.concatenate([from_left[i, :, c], edge, from_right[i, :SIDE, c]], axis=0)
            later = from_right[i, SIDE : SIDE + 1, c] + following[i, 0:1, c]
            parts = unpool(held, total, later, taps[:, c], made)
            gkv[:, c] = made[...].astype(bf16)
            for t, part in enumerate(parts):
                sums[8 * i + t : 8 * i + t + 1, c] = part
        if i == 0:
            grad_norm[...] = nt(gkv[...], w[...])
        else:
            grad_norm[...] += nt(gkv[...], w[...])
            gone.start(2, 3)
        part = slice(i * d, (i + 1) * d)
        two_halves(normed_t, gkv, gw_keep.at[:, part], gw_send.at[:, part])
    gone.start(0, 1)


def upper_pairs_back(gp, from_left, from_right, following, k, v, rim, kpool, vpool, normed, wk, wv, perm):
    n, d = k.shape
    return moved_call(
        upper_pairs_kernel,
        (normed, perm, gp, from_left, from_right, following, rim, k, kpool, wk, v, vpool, wv),
        [sds((d // 2, 2 * d), bf16)] * 2 + [sds((n, d), f32), sds((16, d), f32)],
        [
            pltpu.VMEM((n, d), bf16),
            pltpu.VMEM((n + 8, PAIR), f32),
            pltpu.VMEM((n, PAIR), f32),
            pltpu.VMEM((d, n), bf16),
        ],
        (10 * n * d * d, 20 * n * d),
    )


def upper_queries_kernel(came, outs, gone, grad_norm):
    gq, grad_c, branch, sums = outs
    gq_near, gq_asked, sel = (came.got(i) for i in range(3))
    n, d = gq_near.shape
    for rows in tiles(n, 256):
        gq[rows] = (gq_near[rows].astype(f32) + tn(sel[:, rows], gq_asked[...])).astype(bf16)
    gone.start(0)
    wq, pairs_norm = came.got(3), came.got(4)
    for rows in tiles(n, 256):
        grad_norm[rows] = pairs_norm[rows] + nt(gq[rows], wq[...])
    hidden, grad, gain = (came.got(i) for i in range(5, 8))
    finish_back(n, hidden, grad, gain, grad_norm, grad_c, sums)
    branch[...] = grad_c[...].astype(bf16)
    gone.start(1, 2, 3)


def upper_queries_back(gq_near, gq_asked, sel, hidden, grad, pairs_norm, gain, wq):
    n, d = gq_near.shape
    return moved_call(
        upper_queries_kernel,
        (gq_near, gq_asked, sel, wq, pairs_norm, hidden, grad, gain),
        [sds((n, d), bf16), sds((n, d), f32), sds((n, d), bf16), sds((8, d), f32)],
        [pltpu.VMEM((n, d), f32)],
        (2 * n * d * d, 24 * n * d),
    )


def lower_project_kernel(came, outs, gone, gkv, grad_norm, low_t, sums):
    gw_keep, gw_send, grad_in = outs
    normed, low = came.got(0), came.got(1)
    n, d = normed.shape
    low_t[...] = by_owner(low[...], normed[...])
    gq, wq = came.got(2), came.got(3)
    grad_norm[...] = nt(gq[...], wq[...])
    two_halves(low_t, gq, gw_keep.at[:, :d], gw_send.at[:, :d])
    left, right = came.got(4), came.got(5)
    for i in range(2):
        g, w = came.got(6 + 2 * i), came.got(7 + 2 * i)
        gkv[...] = g[...].astype(bf16)
        gkv[:REACH_ONE] = (g[:REACH_ONE] + left[i]).astype(bf16)
        gkv[n - REACH_ONE :] = (g[n - REACH_ONE :] + right[i]).astype(bf16)
        grad_norm[...] += nt(gkv[...], w[...])
        part = slice((1 + i) * d, (2 + i) * d)
        two_halves(low_t, gkv, gw_keep.at[:, part], gw_send.at[:, part])
    x, grad, gain = (came.got(i) for i in range(10, 13))
    sums[...] = jnp.zeros_like(sums)
    for rows in tiles(n, 128):
        back, by_gain, by_bias = norm_back(x[rows].astype(f32), gain[...], grad_norm[rows])
        grad_in[rows] = grad[rows] + back
        sums[0:1] += by_gain
        sums[1:2] += by_bias
    gone.start(2)
    at = 8
    for i in range(13, 17):
        part = came.got(i)
        sums[at : at + part.shape[0]] = part[...]
        at += part.shape[0]
    for rows, out in zip(tiles(d, d // 2), (gw_keep, gw_send)):
        out[:, 3 * d :] = nt(low[rows], sums[...].astype(bf16)).astype(bf16)
    gone.start(0, 1)


def lower_project_back(gq, gk, gv, left, right, normed, x, grad, gain, wq, wk, wv, low, *sums):
    n, d = gq.shape
    return moved_call(
        lower_project_kernel,
        (normed, low, gq, wq, left, right, gk, wk, gv, wv, x, grad, gain, *sums),
        [sds((d // 2, 3 * d + PAIR), bf16)] * 2 + [sds((n, d), f32)],
        [pltpu.VMEM((n, d), bf16), pltpu.VMEM((n, d), f32), pltpu.VMEM((d, n), bf16), pltpu.VMEM((PAIR, d), f32)],
        (14 * n * d * d, 24 * n * d),
    )


def lower_back_kernel(
    doc_order, seq_order, branch_c, normed, fgain, perm, active, slope, up, down, grad_c, hidden_b, mixed, wo, gq_upper, normed_upper,
    up_keep, up_send, down_keep, down_send, grad_b, grad_mixed, sums,
    branch, grad_norm, normed_t, active_t, lifted, grad_held, hidden_held, mixed_held, wo_held, gq_held, upper_held, sems,
):
    step = pl.program_id(0)
    n, d = branch_c.shape
    last = pl.num_programs(0) - 2
    late = Mover(
        (grad_c, hidden_b, mixed, wo, gq_upper, normed_upper),
        (grad_held, hidden_held, mixed_held, wo_held, gq_held, upper_held),
        sems,
    )

    @pl.when(step == 0)
    def _():
        late.start()
        normed_t[...] = by_owner(perm[...], normed[...])
        grad_norm[...] = jnp.zeros_like(grad_norm)

    @pl.when(step < last)
    def _():
        for rows in tiles(n, 256):
            g = (nt(branch_c[rows], down[...]) * slope[rows].astype(f32)).astype(bf16)
            grad_norm[rows] += nt(g, up[...])
            lifted[rows] = g
            place_hidden(seq_order, step, active[rows], rows, active_t)
        two_halves(active_t, branch_c, down_keep, down_send)
        two_halves(normed_t, lifted, up_keep, up_send)

    @pl.when(step == last)
    def _():
        late.wait()
        finish_back(n, hidden_held, grad_held, fgain, grad_norm, grad_b, sums)
        for rows in tiles(n, 256):
            branch[rows] = grad_b[rows].astype(bf16)
            grad_mixed[rows] = nt(branch[rows], wo_held[...]).astype(bf16)
        normed_t[...] = by_owner(perm[...], mixed_held[...])
        two_halves(normed_t, branch, up_keep, up_send)

    @pl.when(step == last + 1)
    def _():
        normed_t[...] = by_owner(perm[...], upper_held[...])
        two_halves(normed_t, gq_held, up_keep, up_send)


def lower_back(
    doc_order, seq_order, branch_c, grad_c, hidden_b, normed, active, slope, mixed, wo, fgain, perm, up, down, gq_upper,
    normed_upper,
):
    n, d = grad_c.shape
    ff = up.shape[1]
    docs, seqs = doc_order.shape[0], seq_order.shape[0]
    fc = ff // docs
    into, outof, shapes = hidden_specs(d, ff, docs, 2)
    lanes = pl.BlockSpec((n, fc), lambda c, *_: (0, jnp.minimum(c, docs - 1)))
    return pl.pallas_call(
        lower_back_kernel,
        out_shape=[*shapes, sds((n, d), f32), sds((n, d), bf16), sds((8, d), f32)],
        grid_spec=pltpu.PrefetchScalarGridSpec(
            num_scalar_prefetch=2,
            grid=(docs + 2,),
            in_specs=[
                whole(n, d), whole(n, d), whole(1, d), whole(d, d), lanes, lanes, *into, *[anywhere()] * 6,
            ],
            out_specs=[*outof, whole(n, d), whole(n, d), whole(8, d)],
            scratch_shapes=[
                pltpu.VMEM((n, d), bf16), pltpu.VMEM((n, d), f32), pltpu.VMEM((d, n), bf16),
                hidden_scratch(n, fc, seqs), pltpu.VMEM((n, fc), bf16),
                pltpu.VMEM((n, d), f32), pltpu.VMEM((n, d), f32), pltpu.VMEM((n, d), bf16), pltpu.VMEM((d, d), bf16),
                pltpu.VMEM((n, d), bf16), pltpu.VMEM((n, d), bf16), pltpu.SemaphoreType.DMA((6,)),
            ],
        ),
        **params(8 * n * d * ff + 4 * n * d * d, 12 * n * ff + 30 * n * d),
    )(
        doc_order, seq_order, branch_c, normed, fgain, perm, active, slope, up, down, grad_c, hidden_b, mixed, wo,
        gq_upper, normed_upper,
    )


def shifted(value, steps):
    count = lax.axis_size("seq")
    pairs = [(i, i + steps) for i in range(count) if 0 <= i + steps < count]
    return lax.ppermute(value, "seq", pairs)


def exchanged(value, axis, bit):
    count = lax.axis_size(axis)
    return lax.ppermute(value, axis, [(i, i ^ bit) for i in range(count)])


def bits(axis, first=1):
    count = lax.axis_size(axis)
    return [(axis, 1 << b) for b in range(count.bit_length()) if first <= 1 << b < count]


def orders():
    cores = [("seq", 1)]
    return cores + bits("doc") + bits("seq", 2), cores + bits("doc")[::-1] + bits("seq", 2)


def owners(order):
    count = lax.axis_size("doc") * lax.axis_size("seq")
    flips = {"doc": [], "seq": []}
    for axis in flips:
        for p in range(count):
            flips[axis].append(sum(b for i, (a, b) in enumerate(order) if a == axis and p >> (len(order) - 1 - i) & 1))
    return tuple(lax.axis_index(a) ^ jnp.array(flips[a], jnp.int32) for a in ("doc", "seq"))


def permutation(order, d):
    doc, seq = owners(order)
    owner = doc * lax.axis_size("seq") + seq
    size = d // owner.shape[0]
    source = (owner[:, None] * size + jnp.arange(size, dtype=jnp.int32)[None, :]).reshape(-1)
    return (source[:, None] == jnp.arange(d, dtype=jnp.int32)[None, :]).astype(bf16)


def hidden_orders(order):
    def places(axis):
        steps = [b for a, b in order if a == axis]
        value = jnp.arange(lax.axis_size(axis), dtype=jnp.int32) ^ lax.axis_index(axis)
        place = jnp.zeros_like(value)
        for b in steps:
            place = 2 * place + (value // b) % 2
        return place

    return places("doc"), places("seq")


class Halving:
    def __init__(self, keep, send, order):
        self.order, self.at, self.rows = order, 1, keep.shape[0]
        self.terms = [keep, exchanged(send, *order[0])]

    def prepare(self):
        self.rows //= 2
        self.send = self.total(self.rows).astype(bf16)

    def go(self):
        self.terms = self.terms + [exchanged(self.send, *self.order[self.at])]
        self.at += 1

    def left(self):
        return self.at < len(self.order)

    def total(self, start=0):
        out = None
        for t in self.terms:
            t = t[start : start + self.rows].astype(f32)
            out = t if out is None else out + t
        return out


def stepped(order):
    steps = []
    for axis, bit in order:
        if axis == "seq" and bit > 1 and steps[-1][0][0] == "seq" and steps[-1][0][1] > 1 and len(steps[-1]) == 1:
            steps[-1] = steps[-1] + [(axis, bit)]
        else:
            steps.append([(axis, bit)])
    return steps


def flips(step):
    axis = step[0][0]
    places = range(len(step))
    return [(axis, sum(step[i][1] for i in places if p >> (len(step) - 1 - i) & 1)) for p in range(1, 1 << len(step))]


def tied(*values):
    return lax.optimization_barrier(values)


def arrived(values, *halvings):
    values, terms = tied(values, [h.terms for h in halvings])
    for h, t in zip(halvings, terms):
        h.terms = t
    return values


def sent(values, *halvings):
    for h in halvings:
        h.prepare()
    values, _ = tied(values, [h.send for h in halvings])
    for h in halvings:
        h.go()
    return values


def in_turn(halvings):
    before = None
    for h in halvings:
        if h.left():
            if before is not None:
                h.terms, _ = tied(h.terms, before)
            h.prepare()
            before = h.send
            h.go()


def others(value, step):
    return [exchanged(value, *f) for f in flips(step)]


def summed(value, steps):
    for step in steps:
        value = sum(others(value, step), value)
    return value


def merged_apart(part, steps):
    half = part.shape[0] // 2
    axis, bit = steps[0][0]
    second = (lax.axis_index(axis) & bit) > 0
    mine = jnp.where(second, part[half:], part[:half])
    other = exchanged(jnp.where(second, part[:half], part[half:]), axis, bit)
    mine = merged(merge(mine, other), steps[1:])
    other = exchanged(mine, axis, bit)
    return jnp.concatenate([jnp.where(second, other, mine), jnp.where(second, mine, other)], axis=0)


def merge(*parts):
    tops = [p[:, HDIM : HDIM + 1] for p in parts]
    top = functools.reduce(jnp.maximum, tops)
    total = sum(p * jnp.exp(t - top) for p, t in zip(parts, tops))
    row = lax.broadcasted_iota(jnp.int32, total.shape, 1)
    return jnp.where(row == HDIM, top, total)


def merged(part, steps):
    for step in steps:
        part = merge(part, *others(part, step))
    return part


def body(
    tokens, cotangent, counts, positions, lower_again, lower_abias, lower_query, lower_key, lower_value, lower_out,
    lower_fgain, lower_fbias, lower_up, lower_down, upper_again, upper_abias, upper_query, upper_key, upper_value,
    upper_out, upper_fgain, upper_fbias, upper_up, upper_down, upper_kpool, upper_vpool,
):
    seq_count = lax.axis_size("seq")
    seq_index = lax.axis_index("seq")
    x, cot = tokens[0], cotangent[0]
    n, d = x.shape
    m = n // STRIDE
    row = lambda g: g.reshape(1, d)
    flags = jnp.stack([seq_index == 0, seq_index == seq_count - 1]).astype(jnp.int32)
    slot_count = positions.shape[1]
    slots = jnp.arange(slot_count, dtype=jnp.int32)
    place = jnp.where(slots < counts[0], positions[0] - seq_index * n, -1)
    sel = (place[:, None] == jnp.arange(n, dtype=jnp.int32)[None, :]).astype(bf16)
    kpool = jnp.pad(upper_kpool, ((0, 8 - TAPS), (0, 0)))
    vpool = jnp.pad(upper_vpool, ((0, 8 - TAPS), (0, 0)))
    taps = jnp.concatenate([kpool, vpool], axis=1)
    low_first, high_first = orders()
    perm_low, perm_high = permutation(low_first, d), permutation(high_first, d)
    doc_order, seq_order = hidden_orders(high_first)
    along = stepped(bits("seq"))

    norm_a, ka, va, qa = project(x, row(lower_again), row(lower_abias), lower_key, lower_value, lower_query)
    ends = lambda rows: jnp.concatenate([ka[rows], va[rows]], axis=1)
    left = shifted(ends(slice(n - REACH_ONE, n)), 1)
    right = shifted(ends(slice(0, REACH_ONE)), -1)
    mixed_a, weights_a = local_attention(flags, qa, ka, va, left, right)
    (
        hidden_b, norm_b, active_b, slope_b, hidden_c, norm_c, qc, kc, vc, pooled, mine, to_left, to_right, asked_q,
    ) = lower_forward(
        x, mixed_a, lower_out, row(lower_fgain), row(lower_fbias), lower_up, lower_down, row(upper_again),
        row(upper_abias), upper_query, upper_key, upper_value, kpool, vpool, sel,
    )
    from_left = shifted(to_right, 1)
    from_right = shifted(to_left, -1)
    asked_q = summed(asked_q, along[:1])
    more = others(asked_q, along[1])
    near, weights_c, kw, vw = near_attention(flags, qc, pooled, from_left, from_right, mine, taps)
    asked_q, more, kw = tied(asked_q, more, kw)
    asked_q = summed(sum(more, asked_q), along[2:])
    part = merged_apart(asked_part(asked_q, kw, vw), along)
    total = part[:, HDIM + 1 : HDIM + 2]
    logsum = jnp.broadcast_to(part[:, HDIM : HDIM + 1] + jnp.log(total), (d // PAIR, 8, 2 * slot_count))
    asked = part[:, :HDIM] / total
    asked = asked.reshape(d // PAIR, HDIM, 2, slot_count).transpose(3, 0, 2, 1).reshape(slot_count, d)

    (
        out, mixed_c, grad_d, grad_mixed_c, grad_asked, up_keep, up_send, down_keep, down_send, sums_d,
    ) = upper_both(
        doc_order, seq_order, hidden_c, near, asked.astype(bf16), sel, cot, upper_out, row(upper_fgain),
        row(upper_fbias), perm_low, upper_up, upper_down,
    )
    flat = lambda x: x.reshape(-1, d)
    gu_up = Halving(up_keep, up_send, low_first)
    gu_down = Halving(flat(down_keep), flat(down_send), high_first)
    more = others(grad_asked, along[0])
    gq_near, near_own, to_left, to_right = near_back(qc, kw, vw, weights_c, grad_mixed_c)
    grad_asked, more, near_own, to_left, to_right = arrived(
        (grad_asked, more, near_own, to_left, to_right), gu_up, gu_down
    )
    grad_asked = sum(more, grad_asked)
    more = others(grad_asked, along[1])
    from_left_back = shifted(to_right, 1)
    from_right_back = shifted(to_left, -1)
    grad_asked, more = sent((grad_asked, more), gu_up, gu_down)
    grad_asked = summed(sum(more, grad_asked), along[2:])
    gq_asked, gp, following = asked_back(
        flags, asked_q, kw, vw, logsum, asked, grad_asked, near_own, to_right[:, :8]
    )
    gq_asked = summed(gq_asked, along[:1])
    more = others(gq_asked, along[1])
    gw_keep, gw_send, pairs_norm, sums_p = upper_pairs_back(
        gp, from_left_back, from_right_back, following, kc, vc, from_left[SIDE:], kpool, vpool, norm_c, upper_key,
        upper_value, perm_high,
    )
    gu_pair = Halving(gw_keep, gw_send, high_first)
    gq_asked, more, pairs_norm = tied(gq_asked, more, pairs_norm)
    gq_asked = summed(sum(more, gq_asked), along[2:])
    gq_upper, grad_c, branch_c, sums_c = upper_queries_back(
        gq_near, gq_asked, sel, hidden_c, grad_d, pairs_norm, row(upper_again), upper_query
    )
    branch_c = arrived(branch_c, gu_up, gu_down, gu_pair)
    branch_c = sent(branch_c, gu_up, gu_down, gu_pair)
    up_keep, up_send, down_keep, down_send, grad_b, grad_mixed_a, sums_b = lower_back(
        doc_order, seq_order, branch_c, grad_c, hidden_b, norm_b, active_b, slope_b, mixed_a, lower_out,
        row(lower_fgain), perm_low, lower_up, lower_down, gq_upper, norm_c,
    )
    grad_mixed_a, up_send, down_send = arrived((grad_mixed_a, up_send, down_send), gu_up, gu_down, gu_pair)
    gl_up = Halving(up_keep, up_send, low_first)
    gl_down = Halving(flat(down_keep), flat(down_send), high_first)
    grad_mixed_a = sent(grad_mixed_a, gu_up, gu_down, gu_pair)
    grad_mixed_a = arrived(grad_mixed_a, gl_up, gl_down)
    grad_mixed_a = sent(grad_mixed_a, gl_up, gl_down)
    gq, gk, gv, to_left, to_right = local_back(qa, ka, va, left, right, weights_a, grad_mixed_a)
    back_last = shifted(to_left, -1)
    back_first = shifted(to_right, 1)
    grad_b, gq = arrived((grad_b, gq), gu_up, gu_pair)
    back_first, back_last = sent((back_first, back_last), gu_up, gu_pair)
    back_first, back_last = arrived((back_first, back_last), gu_down)
    grad_b = sent(grad_b, gu_down)
    gw_keep, gw_send, grad_in = lower_project_back(
        gq, gk, gv, back_first, back_last, norm_a, x, grad_b, row(lower_again), lower_query, lower_key, lower_value,
        perm_low, sums_b, sums_c, sums_d, sums_p,
    )
    gw_send = arrived(gw_send, gu_pair, gu_up, gu_down, gl_up, gl_down)
    gl_qkv = Halving(gw_keep, gw_send, low_first)
    in_turn([gl_up, gl_down, gl_qkv, gu_pair, gl_down, gl_up, gl_qkv, gl_down, gl_up, gl_qkv, gl_qkv])
    every = (gl_up, gl_down, gl_qkv, gu_up, gu_down, gu_pair)
    while any(h.left() for h in every):
        in_turn(every)
    gu_up, gu_down, gu_pair, gl_up, gl_down, gl_qkv = (
        h.total() for h in (gu_up, gu_down, gu_pair, gl_up, gl_down, gl_qkv)
    )
    small = gl_qkv[:, 3 * d :].T
    sums_a, sums_b, sums_c, sums_d, sums_p = (small[r] for r in (*tiles(32, 8), slice(32, 48)))
    ff = lower_up.shape[1]
    part = lambda got, i: got[:, i * d : (i + 1) * d]
    return (
        out[None],
        grad_in[None],
        sums_a[0],
        sums_a[1],
        part(gl_qkv, 0),
        part(gl_qkv, 1),
        part(gl_qkv, 2),
        gl_up[:, ff : ff + d],
        sums_b[0],
        sums_b[1],
        gl_up[:, :ff],
        gl_down,
        sums_c[0],
        sums_c[1],
        gl_up[:, ff + d :],
        part(gu_pair, 0),
        part(gu_pair, 1),
        gu_up[:, ff:],
        sums_d[0],
        sums_d[1],
        gu_up[:, :ff],
        gu_down,
        sums_p[0:TAPS],
        sums_p[8 : 8 + TAPS],
    )


def solution(mesh):
    tokens = P("doc", "seq", None)
    every = ("doc", "seq")
    vector, matrix, taps = P(every), P(every, None), P(None, every)
    layer = (vector, vector, matrix, matrix, matrix, matrix, vector, vector, matrix, matrix)
    return jax.shard_map(
        body,
        mesh=mesh,
        in_specs=(tokens, tokens, P("doc"), P("doc", None)) + (P(),) * 22,
        out_specs=(tokens, tokens) + layer + layer + (taps, taps),
        check_vma=False,
    )
```

```python
import functools

import jax
import jax.numpy as jnp
from jax import lax
from jax.experimental import pallas as pl
from jax.experimental.pallas import tpu as pltpu
from jax.sharding import PartitionSpec as P

HDIM = 64
REACH_ONE = 64
REACH_TWO = 256
STRIDE = 4
TAPS = 5
QB = 128
PAIR = 2 * HDIM
WIN_ONE = QB + 2 * REACH_ONE
SIDE = REACH_TWO // STRIDE
WIN_TWO = QB // STRIDE + 2 * SIDE
RAW = 16
eps = 1e-05
GROUP = 6
far_below = -1e30
scale = HDIM**-0.5
f32 = jnp.float32
bf16 = jnp.bfloat16

MILLS = 0.34
MILLS_POLY = (
    0.13590356504727755,
    0.13101844409724564,
    0.1513778923259517,
    -0.01998659482308463,
    0.25210690821609844,
    -0.1936388145328779,
    0.04321858184569336,
)
INV_SQRT_2PI = 0.3989422804014327


def nn(a, b):
    return lax.dot_general(a, b, (((1,), (0,)), ((), ())), preferred_element_type=f32)


def nt(a, b):
    return lax.dot_general(a, b, (((1,), (1,)), ((), ())), preferred_element_type=f32)


def tn(a, b):
    return lax.dot_general(a, b, (((0,), (0,)), ((), ())), preferred_element_type=f32)


def norm_rows(x, gain, bias):
    average = jnp.mean(x, axis=-1, keepdims=True)
    centred = x - average
    variance = jnp.mean(centred * centred, axis=-1, keepdims=True)
    return centred * lax.rsqrt(variance + eps) * gain + bias


def norm_back(x, gain, grad):
    average = jnp.mean(x, axis=-1, keepdims=True)
    centred = x - average
    variance = jnp.mean(centred * centred, axis=-1, keepdims=True)
    spread = lax.rsqrt(variance + eps)
    unit = centred * spread
    lifted = grad * gain
    first = jnp.mean(lifted, axis=-1, keepdims=True)
    second = jnp.mean(lifted * unit, axis=-1, keepdims=True)
    back = spread * (lifted - first - unit * second)
    return back, jnp.sum(grad * unit, axis=0, keepdims=True), jnp.sum(grad, axis=0, keepdims=True)


def gelu_both(u):
    t = 1.0 / (1.0 + MILLS * jnp.abs(u))
    e = jnp.exp(-0.5 * (u * u))
    poly = jnp.full_like(u, MILLS_POLY[-1])
    for c in MILLS_POLY[-2::-1]:
        poly = poly * t + c
    tail = poly * (t * e)
    cdf = jnp.where(u >= 0, 1.0 - tail, tail)
    return u * cdf, cdf + u * e * INV_SQRT_2PI


def whole(*shape):
    return pl.BlockSpec(shape, lambda *_: (0,) * len(shape), pipeline_mode=pl.Buffered(1))


def smem():
    return pl.BlockSpec(memory_space=pltpu.SMEM)


def params(flops, size, mib=58):
    return dict(
        compiler_params=pltpu.CompilerParams(vmem_limit_bytes=mib << 20),
        cost_estimate=pl.CostEstimate(flops=flops, bytes_accessed=size, transcendentals=0),
    )


def sds(shape, dtype):
    return jax.ShapeDtypeStruct(shape, dtype)


def anywhere():
    return pl.BlockSpec(memory_space=pl.ANY)


class Mover:
    def __init__(self, sources, buffers, sems):
        self.buffers = buffers
        self.copies = [pltpu.make_async_copy(s, b, sems.at[i]) for i, (s, b) in enumerate(zip(sources, buffers))]

    def start(self, *which):
        for i in which or range(len(self.copies)):
            self.copies[i].start()

    def wait(self, *which):
        for i in which or range(len(self.copies)):
            self.copies[i].wait()

    def got(self, i):
        self.copies[i].wait()
        return self.buffers[i]


def moved_call(kernel, ins, outs, scratch, cost):
    def body(*refs):
        n_in, n_out = len(ins), len(outs)
        sources, targets, rest = refs[:n_in], refs[n_in : n_in + n_out], refs[n_in + n_out :]
        in_bufs, out_bufs, rest = rest[:n_in], rest[n_in : n_in + n_out], rest[n_in + n_out :]
        in_sems, out_sems, *rest = rest
        came = Mover(sources, in_bufs, in_sems)
        came.start()
        gone = Mover(out_bufs, targets, out_sems)
        kernel(came, out_bufs, gone, *rest)
        gone.wait()

    return pl.pallas_call(
        body,
        out_shape=list(outs),
        in_specs=[anywhere()] * len(ins),
        out_specs=[anywhere()] * len(outs),
        scratch_shapes=[pltpu.VMEM(x.shape, x.dtype) for x in (*ins, *outs)]
        + [pltpu.SemaphoreType.DMA((len(ins),)), pltpu.SemaphoreType.DMA((len(outs),))]
        + scratch,
        **params(*cost),
    )(*ins)


NORMS = ("lower_again", "lower_abias", "lower_fgain", "lower_fbias")
NORMS += ("upper_again", "upper_abias", "upper_fgain", "upper_fbias")


def of_norm(vectors, name):
    i = NORMS.index(name)
    return vectors.at[i : i + 1]


def tiles(rows, step):
    return [slice(i, i + step) for i in range(0, rows, step)]


def project_kernel(came, outs, gone):
    x, vectors = came.got(0), came.got(1)
    gain, bias = vectors.at[0:1], vectors.at[1:2]
    normed = outs[0]
    parts = tiles(x.shape[0], 256)
    for rows in parts:
        normed[rows] = norm_rows(x[rows].astype(f32), gain[...], bias[...]).astype(bf16)
    gone.start(0)
    for i in range(1, 4):
        w = came.got(1 + i)
        for rows in parts:
            outs[i][rows] = nn(normed[rows], w[...]).astype(bf16)
        gone.start(i)


def project(x, vectors, wk, wv, wq):
    n, d = x.shape
    return moved_call(
        project_kernel, (x, vectors, wk, wv, wq), [sds((n, d), bf16)] * 4, [], (6 * n * d * d, 10 * n * d + 6 * d * d)
    )


def head_masks(rows):
    lane = lax.broadcasted_iota(jnp.int32, (rows, PAIR), 1)
    return lane < HDIM


def both_heads(x):
    first = head_masks(x.shape[0])
    zero = jnp.zeros_like(x)
    return jnp.concatenate([jnp.where(first, x, zero), jnp.where(first, zero, x)], axis=0)


def own_blocks(x):
    n = x.shape[1] // 2
    return jnp.concatenate([x[:HDIM, :n], x[HDIM:, n:]], axis=0).T


def softmax_columns(scores):
    top = jnp.max(scores, axis=0, keepdims=True)
    raised = jnp.exp(scores - top)
    total = jnp.sum(raised, axis=0, keepdims=True)
    return (raised * (1.0 / total)).astype(bf16)


def window_bias(kind):
    win = WIN_ONE if kind == 1 else WIN_TWO
    key = lax.broadcasted_iota(jnp.int32, (win, QB), 0)
    query = lax.broadcasted_iota(jnp.int32, (win, QB), 1)
    if kind == 1:
        offset, reach = key - query, 2 * REACH_ONE
    else:
        offset, reach = STRIDE * key - query, 2 * REACH_TWO
    return jnp.where((offset >= 0) & (offset <= reach), 0.0, far_below)


def edge_bias(bias, start, edge, length, flags):
    win = bias.shape[0]
    key = lax.broadcasted_iota(jnp.int32, bias.shape, 0) + start
    if start < edge:
        limit = jnp.where(flags[0] > 0, edge, 0)
        bias = jnp.where(key < limit, far_below, bias)
    if start + win > length - edge:
        limit = jnp.where(flags[1] > 0, length - edge, length)
        bias = jnp.where(key >= limit, far_below, bias)
    return bias


def attend_blocks(blocks):
    scores = [nt(kb, both_heads(qb * scale)) for qb, kb, _, _ in blocks]
    weights = [softmax_columns(s + jnp.concatenate([b[3], b[3]], axis=1)) for s, b in zip(scores, blocks)]
    outs = [tn(b[2], w) for b, w in zip(blocks, weights)]
    return [own_blocks(o) for o in outs], weights


def back_blocks(blocks):
    grads = [both_heads(grad) for *_, grad in blocks]
    changes = [nt(b[2], g) for b, g in zip(blocks, grads)]
    values = [nn(b[3], g) for b, g in zip(blocks, grads)]
    scores = []
    for b, change in zip(blocks, changes):
        share = b[3].astype(f32)
        inner = jnp.sum(share * change, axis=0, keepdims=True) / jnp.sum(share, axis=0, keepdims=True)
        scores.append((share * (change - inner)).astype(bf16))
    keys = [nn(g, both_heads(b[0] * scale)) for g, b in zip(scores, blocks)]
    queries = [own_blocks(tn(b[1], g)) * scale for g, b in zip(scores, blocks)]
    return queries, keys, values


def local_kernel(flags, q, k, v, kl, vl, kr, vr, out, weights, kw, vw, base):
    n = q.shape[0]

    @pl.when(pl.program_id(0) == 0)
    def _():
        base[...] = window_bias(1)

    for wide, left, own, right in ((kw, kl, k, kr), (vw, vl, v, vr)):
        wide[:REACH_ONE] = left[...]
        wide[REACH_ONE : REACH_ONE + n] = own[...]
        wide[REACH_ONE + n :] = right[...]
    todo = []
    for b, rows in enumerate(tiles(n, QB)):
        window = slice(b * QB, b * QB + WIN_ONE)
        bias = edge_bias(base[...], b * QB, REACH_ONE, n + 2 * REACH_ONE, flags)
        todo.append((q[rows], kw[window], vw[window], bias))
    for b in range(0, len(todo), GROUP):
        for i, (mixed, w) in enumerate(zip(*attend_blocks(todo[b : b + GROUP]))):
            out[(b + i) * QB : (b + i + 1) * QB] = mixed.astype(bf16)
            weights[0, b + i] = w


def pair_block(rows, offset=0):
    return pl.BlockSpec((rows, PAIR), lambda g, offset=offset: (0, g + offset))


def two_rows(rows):
    return pl.BlockSpec((2, rows, PAIR), lambda g: (0, 0, g))


def local_attention(flags, q, k, v, left, right):
    n, d = q.shape
    pairs, blocks = d // PAIR, n // QB
    wide = n + 2 * REACH_ONE
    return pl.pallas_call(
        local_kernel,
        out_shape=[sds((n, d), bf16), sds((pairs, blocks, WIN_ONE, 2 * QB), bf16)],
        grid=(pairs,),
        in_specs=[smem()]
        + [pair_block(n)] * 3
        + [pair_block(REACH_ONE), pair_block(REACH_ONE, pairs)] * 2,
        out_specs=[
            pair_block(n),
            pl.BlockSpec((1, blocks, WIN_ONE, 2 * QB), lambda g: (g, 0, 0, 0)),
        ],
        scratch_shapes=[
            pltpu.VMEM((wide, PAIR), bf16),
            pltpu.VMEM((wide, PAIR), bf16),
            pltpu.VMEM((WIN_ONE, QB), f32),
        ],
        **params(4 * n * WIN_ONE * d * 2, 12 * n * d),
    )(flags, q, k, v, left, left, right, right)


def local_back_kernel(
    q, k, v, kl, vl, kr, vr, weights, grad, gq, gk, gv, to_left, to_right, kw, vw, ka, va
):
    n = q.shape[0]
    for wide, left, own, right in ((kw, kl, k, kr), (vw, vl, v, vr)):
        wide[:REACH_ONE] = left[...]
        wide[REACH_ONE : REACH_ONE + n] = own[...]
        wide[REACH_ONE + n :] = right[...]
    ka[...] = jnp.zeros_like(ka)
    va[...] = jnp.zeros_like(va)
    todo = []
    for b, rows in enumerate(tiles(n, QB)):
        window = slice(b * QB, b * QB + WIN_ONE)
        todo.append((q[rows], kw[window], vw[window], weights[0, b], grad[rows]))
    for first in range(0, len(todo), GROUP):
        for i, (gqb, gkb, gvb) in enumerate(zip(*back_blocks(todo[first : first + GROUP]))):
            b = first + i
            window = slice(b * QB, b * QB + WIN_ONE)
            gq[b * QB : (b + 1) * QB] = gqb.astype(bf16)
            ka[window] += gkb
            va[window] += gvb
    for i, (wide, own) in enumerate(((ka, gk), (va, gv))):
        to_left[i] = wide[:REACH_ONE]
        own[...] = wide[REACH_ONE : REACH_ONE + n]
        to_right[i] = wide[REACH_ONE + n :]


def local_back(q, k, v, left, right, weights, grad):
    n, d = q.shape
    pairs, blocks = d // PAIR, n // QB
    wide = n + 2 * REACH_ONE
    return pl.pallas_call(
        local_back_kernel,
        out_shape=[sds((n, d), bf16), sds((n, d), f32), sds((n, d), f32)] + [sds((2, REACH_ONE, d), f32)] * 2,
        grid=(pairs,),
        in_specs=[pair_block(n)] * 3
        + [pair_block(REACH_ONE), pair_block(REACH_ONE, pairs)] * 2
        + [pl.BlockSpec((1, blocks, WIN_ONE, 2 * QB), lambda g: (g, 0, 0, 0))]
        + [pair_block(n)],
        out_specs=[pair_block(n)] * 3 + [two_rows(REACH_ONE)] * 2,
        scratch_shapes=[pltpu.VMEM((wide, PAIR), bf16)] * 2 + [pltpu.VMEM((wide, PAIR), f32)] * 2,
        **params(10 * n * WIN_ONE * d * 2, 24 * n * d),
    )(q, k, v, left, left, right, right, weights, grad)


def first_pooled(tile, rim, raw, taps):
    row = (
        taps[0:1] * rim[0:1].astype(f32)
        + taps[1:2] * rim[1:2].astype(f32)
        + taps[2:3] * raw[0:1].astype(f32)
        + taps[3:4] * raw[1:2].astype(f32)
        + taps[4:5] * raw[2:3].astype(f32)
    )
    first = lax.broadcasted_iota(jnp.int32, tile.shape, 0) == 0
    return jnp.where(first, row, tile.astype(f32)).astype(bf16)


def pooled_window(wide, left, own, right, mine, taps):
    n = own.shape[0]
    wide[:SIDE] = left[:SIDE]
    wide[SIDE : SIDE + n] = own[...]
    wide[SIDE + n :] = right[:SIDE]
    rim = left[SIDE:].astype(f32)[RAW - 2 :]
    raw = mine[:RAW].astype(f32)
    wide[SIDE : SIDE + RAW] = first_pooled(own[:RAW], rim, raw, taps)
    rim = mine[RAW:].astype(f32)[RAW - 2 :]
    raw = right[SIDE:].astype(f32)
    wide[SIDE + n : SIDE + n + RAW] = first_pooled(right[:RAW], rim, raw, taps)


def near_kernel(flags, q, pk, pv, lk, lv, rk, rv, mk, mv, tk, tv, out, weights, kw, vw, base):
    n = q.shape[0]

    @pl.when(pl.program_id(0) == 0)
    def _():
        base[...] = window_bias(2)

    pooled_window(kw, lk, pk, rk, mk, tk[...])
    pooled_window(vw, lv, pv, rv, mv, tv[...])
    step = QB // STRIDE
    todo = []
    for b, rows in enumerate(tiles(n, QB)):
        window = slice(b * step, b * step + WIN_TWO)
        bias = edge_bias(base[...], b * step, SIDE, kw.shape[0], flags)
        todo.append((q[rows], kw[window], vw[window], bias))
    for b in range(0, len(todo), GROUP):
        for i, (mixed, w) in enumerate(zip(*attend_blocks(todo[b : b + GROUP]))):
            out[(b + i) * QB : (b + i + 1) * QB] = mixed.astype(bf16)
            weights[0, b + i] = w


def near_attention(flags, q, pooled, left, right, mine, taps):
    n, d = q.shape
    pairs, blocks, m = d // PAIR, n // QB, n // STRIDE
    wide = m + 2 * SIDE
    two = lambda rows: [pair_block(rows), pair_block(rows, pairs)]
    return pl.pallas_call(
        near_kernel,
        out_shape=[
            sds((n, d), bf16),
            sds((pairs, blocks, WIN_TWO, 2 * QB), bf16),
            sds((wide, d), bf16),
            sds((wide, d), bf16),
        ],
        grid=(pairs,),
        in_specs=[smem(), pair_block(n)] + two(m) + two(SIDE + RAW) * 2 + two(2 * RAW) + two(8),
        out_specs=[
            pair_block(n),
            pl.BlockSpec((1, blocks, WIN_TWO, 2 * QB), lambda g: (g, 0, 0, 0)),
            pair_block(wide),
            pair_block(wide),
        ],
        scratch_shapes=[pltpu.VMEM((WIN_TWO, QB), f32)],
        **params(4 * n * WIN_TWO * d * 2, 10 * n * d),
    )(flags, q, pooled, pooled, left, left, right, right, mine, mine, taps, taps)


def asked_kernel(q, kw, vw, out):
    own = slice(SIDE, kw.shape[0] - SIDE)
    slots = q.shape[0]
    column = lax.broadcasted_iota(jnp.int32, (HDIM, 2 * slots), 1)
    row = lax.broadcasted_iota(jnp.int32, (8, 2 * slots), 0)
    parts = tiles(q.shape[1], PAIR)
    scores = [nt(kw[own, c], both_heads(q[:, c] * scale)) for c in parts]
    tops = [jnp.max(s, axis=0, keepdims=True) for s in scores]
    raised = [jnp.exp(s - top).astype(bf16) for s, top in zip(scores, tops)]
    sums = [tn(vw[own, c], r) for c, r in zip(parts, raised)]
    for g, (top, r, x) in enumerate(zip(tops, raised, sums)):
        total = jnp.sum(r.astype(f32), axis=0, keepdims=True)
        out[g, :HDIM] = jnp.where(column < slots, x[:HDIM], x[HDIM:])
        out[g, HDIM:] = jnp.where(row == 0, top, jnp.where(row == 1, total, 0.0))


def asked_part(q, kw, vw):
    slots, d = q.shape
    pairs, wide = d // PAIR, kw.shape[0]
    return pl.pallas_call(
        asked_kernel,
        out_shape=sds((pairs, HDIM + 8, 2 * slots), f32),
        grid=(1,),
        in_specs=[whole(slots, d), whole(wide, d), whole(wide, d)],
        out_specs=whole(pairs, HDIM + 8, 2 * slots),
        **params(4 * slots * wide * d, 4 * wide * d),
    )(q, kw, vw)


def near_back_kernel(q, kw, vw, weights, grad, gq, own, to_left, to_right, gk, gv):
    n = q.shape[0]
    gk[...] = jnp.zeros_like(gk)
    gv[...] = jnp.zeros_like(gv)
    step = QB // STRIDE
    todo = []
    for b, rows in enumerate(tiles(n, QB)):
        window = slice(b * step, b * step + WIN_TWO)
        todo.append((q[rows], kw[window], vw[window], weights[0, b], grad[rows]))
    for first in range(0, len(todo), GROUP):
        for i, (gqb, gkb, gvb) in enumerate(zip(*back_blocks(todo[first : first + GROUP]))):
            b = first + i
            window = slice(b * step, b * step + WIN_TWO)
            gq[b * QB : (b + 1) * QB] = gqb.astype(bf16)
            gk[window] += gkb
            gv[window] += gvb
    m = gk.shape[0] - 2 * SIDE
    for i, wide in enumerate((gk, gv)):
        own[i] = wide[SIDE : SIDE + m]
        to_left[i] = wide[: SIDE + 8]
        to_right[i] = wide[SIDE + m :]


def near_back(q, kw, vw, weights, grad):
    n, d = q.shape
    pairs, blocks, wide = d // PAIR, n // QB, kw.shape[0]
    sizes = (wide - 2 * SIDE, SIDE + 8, SIDE)
    return pl.pallas_call(
        near_back_kernel,
        out_shape=[sds((n, d), bf16)] + [sds((2, r, d), f32) for r in sizes],
        grid=(pairs,),
        in_specs=[pair_block(n), pair_block(wide), pair_block(wide)]
        + [pl.BlockSpec((1, blocks, WIN_TWO, 2 * QB), lambda g: (g, 0, 0, 0))]
        + [pair_block(n)],
        out_specs=[pair_block(n)] + [two_rows(r) for r in sizes],
        scratch_shapes=[pltpu.VMEM((wide, PAIR), f32)] * 2,
        **params(10 * n * WIN_TWO * d * 2, 20 * n * d),
    )(q, kw, vw, weights, grad)


def asked_back_kernel(flags, q, kw, vw, logsum, mixed, grad, near, near_next, gq, own, following):
    m = near.shape[1]
    reach = slice(SIDE, SIDE + m + RAW)
    slots = q.shape[0]
    open_end = jnp.where(flags[1] > 0, 0.0, 1.0)
    parts = tiles(q.shape[1], PAIR)
    queries = [both_heads(q[:, c] * scale) for c in parts]
    grads = [both_heads(grad[:, c]) for c in parts]
    scores = [nt(kw[reach, c], x) for c, x in zip(parts, queries)]
    changes = [nt(vw[reach, c], x) for c, x in zip(parts, grads)]
    weights = [jnp.exp(s - logsum[g, 0:1]) for g, s in enumerate(scores)]
    values = [nn(w.astype(bf16), x) for w, x in zip(weights, grads)]
    grad_scores = []
    for c, w, change in zip(parts, weights, changes):
        by_feature = (grad[:, c].astype(f32) * mixed[:, c]).T
        inner = [jnp.sum(by_feature[rows], axis=0, keepdims=True) for rows in tiles(PAIR, HDIM)]
        grad_scores.append((w * (change - jnp.concatenate(inner, axis=1))).astype(bf16))
    keys = [nn(x, y) for x, y in zip(grad_scores, queries)]
    backs = [tn(x[:m], kw[reach, c][:m]) * scale for c, x in zip(parts, grad_scores)]
    for c, key, value, back in zip(parts, keys, values, backs):
        for i, wide in enumerate((key, value)):
            own[i, :, c] = near[i, :, c] + wide[:m]
            following[i, :, c] = (near_next[i, :, c] + wide[m : m + 8]) * open_end
        gq[:, c] = jnp.where(head_masks(slots), back[:slots], back[slots:]).astype(bf16)


def asked_back(flags, q, kw, vw, logsum, mixed, grad, near, near_next):
    slots, d = q.shape
    pairs, wide, m = d // PAIR, kw.shape[0], near.shape[1]
    return pl.pallas_call(
        asked_back_kernel,
        out_shape=[sds((slots, d), bf16), sds((2, m, d), f32), sds((2, 8, d), f32)],
        grid=(1,),
        in_specs=[
            smem(), whole(slots, d), whole(wide, d), whole(wide, d), whole(pairs, 8, 2 * slots), whole(slots, d),
            whole(slots, d), whole(2, m, d), whole(2, 8, d),
        ],
        out_specs=[whole(slots, d), whole(2, m, d), whole(2, 8, d)],
        **params(10 * slots * wide * d, 20 * wide * d),
    )(flags, q, kw, vw, logsum, mixed, grad, near, near_next)


def pool_rows(held, taps):
    m = (held.shape[0] - 8) // STRIDE
    total = taps[0:1] * held[pl.ds(6, m, stride=STRIDE)]
    for t in range(1, TAPS):
        total = total + taps[t : t + 1] * held[pl.ds(6 + t, m, stride=STRIDE)]
    return total.astype(bf16)


def lower_kernel(
    x, mixed, wo, vectors, up, down, kpool, vpool, sel, wq_from, wk_from, wv_from,
    active, slope, pooled, mine, to_left, to_right, asked, *rest,
):
    fgain, fbias = of_norm(vectors, "lower_fgain"), of_norm(vectors, "lower_fbias")
    again, abias = of_norm(vectors, "upper_again"), of_norm(vectors, "upper_abias")
    targets, bufs, (wq, wk, wv, held, in_sems, out_sems) = rest[:7], rest[7:14], rest[14:]
    hidden_b, normed_b, hidden_c, normed_c, q, k, v = bufs
    gone = Mover(bufs, targets, out_sems)
    came = Mover((wq_from, wk_from, wv_from), (wq, wk, wv), in_sems)
    step = pl.program_id(0)
    n, d = x.shape

    @pl.when(step == 0)
    def _():
        came.start()
        for rows in tiles(n, 256):
            h = x[rows].astype(f32) + nn(mixed[rows], wo[...])
            hidden_b[rows] = h
            hidden_c[rows] = h
            normed_b[rows] = norm_rows(h, fgain[...], fbias[...]).astype(bf16)
        gone.start(0, 1)

    for rows in tiles(n, 256):
        a, s = gelu_both(nn(normed_b[rows], up[...]))
        a = a.astype(bf16)
        active[rows] = a
        slope[rows] = s.astype(bf16)
        hidden_c[rows] += nn(a, down[...])

    @pl.when(step == pl.num_programs(0) - 1)
    def _():
        gone.start(2)
        came.wait()
        for rows in tiles(n, 256):
            normed_c[rows] = norm_rows(hidden_c[rows], again[...], abias[...]).astype(bf16)
            q[rows] = nn(normed_c[rows], wq[...]).astype(bf16)
        gone.start(3, 4)
        m = n // STRIDE
        held[:, :8] = jnp.zeros((d // PAIR, 8, PAIR), f32)
        for j, (w, out, taps, lanes) in enumerate(((wk, k, kpool, slice(0, d)), (wv, v, vpool, slice(d, 2 * d)))):
            for rows in tiles(n, 256):
                made = nn(normed_c[rows], w[...]).astype(bf16)
                out[rows] = made
                for i, c in enumerate(tiles(d, PAIR)):
                    held[i, 8 + rows.start : 8 + rows.stop] = made[:, c].astype(f32)
            gone.start(5 + j)
            for i, c in enumerate(tiles(d, PAIR)):
                part = slice(lanes.start + c.start, lanes.start + c.stop)
                pooled[:, part] = pool_rows(held.at[i], taps[:, c])
            mine[:RAW, lanes] = out[:RAW]
            mine[RAW:, lanes] = out[n - RAW :]
        to_right[:SIDE] = pooled[m - SIDE :]
        to_right[SIDE:] = mine[RAW:]
        to_left[:SIDE] = pooled[:SIDE]
        to_left[SIDE:] = mine[:RAW]
        asked[...] = nn(sel[...], q[...]).astype(bf16)
        gone.wait()


def lower_forward(x, mixed, wo, vectors, up, down, wq, wk, wv, kpool, vpool, sel):
    n, d = x.shape
    ff, slots, m = up.shape[1], sel.shape[0], n // STRIDE
    fc = 512
    lanes = pl.BlockSpec((n, fc), lambda c: (0, c))
    moved = [sds((n, d), t) for t in (f32, bf16, f32, bf16, bf16, bf16, bf16)]
    small = [(m, 2 * d), (2 * RAW, 2 * d), (SIDE + RAW, 2 * d), (SIDE + RAW, 2 * d), (slots, d)]
    got = pl.pallas_call(
        lower_kernel,
        out_shape=[sds((n, ff), bf16)] * 2 + [sds(x, bf16) for x in small] + moved,
        grid=(ff // fc,),
        in_specs=[
            whole(n, d), whole(n, d), whole(d, d), whole(len(NORMS), d),
            pl.BlockSpec((d, fc), lambda c: (0, c)), pl.BlockSpec((fc, d), lambda c: (c, 0)),
            whole(8, d), whole(8, d), whole(slots, n), *[anywhere()] * 3,
        ],
        out_specs=[lanes, lanes] + [whole(*x) for x in small] + [anywhere()] * len(moved),
        scratch_shapes=[pltpu.VMEM(x.shape, x.dtype) for x in moved]
        + [pltpu.VMEM((d, d), bf16)] * 3
        + [pltpu.VMEM((d // PAIR, n + 8, PAIR), f32)]
        + [pltpu.SemaphoreType.DMA((3,)), pltpu.SemaphoreType.DMA((len(moved),))],
        **params(4 * n * d * ff + 8 * n * d * d, 8 * n * ff + 40 * n * d),
    )(x, mixed, wo, vectors, up, down, kpool, vpool, sel, wq, wk, wv)
    active, slope, pooled, mine, to_left, to_right, asked, hidden_b, normed_b, hidden_c, normed_c, q, k, v = got
    return (
        hidden_b, normed_b, active, slope, hidden_c, normed_c, q, k, v, pooled, mine, to_left, to_right, asked,
    )


def by_owner(perm, x):
    return nt(perm, x).astype(bf16)


def place_hidden(order, group, chunk, rows, wide):
    count = order.shape[0]
    held = chunk.T
    size = held.shape[0] // count
    for s in range(count):
        start = pl.multiple_of(order[s] * size, size)
        wide[pl.ds(start, size), rows] = held[s * size : (s + 1) * size].astype(wide.dtype)


def hidden_scratch(n, fc, seqs):
    return pltpu.VMEM((fc, n), f32 if fc // seqs % 16 else bf16)


def two_halves(left, right, first, second):
    half = left.shape[0] // 2
    first[...] = nn(left[:half].astype(bf16), right[...]).astype(bf16).reshape(first.shape)
    second[...] = nn(left[half:].astype(bf16), right[...]).astype(bf16).reshape(second.shape)


def finish_back(n, hidden, grad, gain, grad_norm, grad_hidden, sums):
    sums[...] = jnp.zeros_like(sums)
    for rows in tiles(n, 128):
        back, by_gain, by_bias = norm_back(hidden[rows], gain[...], grad_norm[rows])
        grad_hidden[rows] = grad[rows].astype(f32) + back
        sums[0:1] += by_gain
        sums[1:2] += by_bias


def hidden_specs(d, ff, docs, more=1):
    fc = ff // docs
    last = docs - 1
    into = [
        pl.BlockSpec((d, fc), lambda c, *_: (0, jnp.minimum(c, last))),
        pl.BlockSpec((fc, d), lambda c, *_: (jnp.minimum(c, last), 0)),
    ]
    lanes = pl.BlockSpec((d // 2, fc), lambda c, *_: (0, c))
    rows = pl.BlockSpec(
        (1, fc // 2, d), lambda c, docs, *_: (docs[jnp.minimum(c, last)], 0, 0)
    )
    out = [lanes, lanes, rows, rows]
    shapes = [sds((d // 2, ff + more * d), bf16)] * 2 + [sds((docs, fc // 2, d), bf16)] * 2
    return into, out, shapes


def upper_kernel(
    doc_order, seq_order, hidden_c, near, asked, sel, cot, wo, vectors, perm, up, down,
    grad_asked, up_keep, up_send, down_keep, down_send, sums, out_to, mixed_to, grad_d_to, grad_mixed_to,
    out, mixed, grad_d, grad_mixed, hidden_d, normed, hidden_e, grad_norm, flag, normed_t, active_t, lifted, sems,
):
    fgain, fbias = of_norm(vectors, "upper_fgain"), of_norm(vectors, "upper_fbias")
    gone = Mover((out, mixed, grad_d, grad_mixed), (out_to, mixed_to, grad_d_to, grad_mixed_to), sems)
    step = pl.program_id(0)
    n, d = near.shape
    last = pl.num_programs(0) - 1

    @pl.when(step == 0)
    def _():
        slots = sel.shape[0]
        flag[...] = tn(sel[...], jnp.ones((slots, PAIR), bf16))
        for rows in tiles(n, 256):
            here = jnp.concatenate([flag[rows]] * (d // PAIR), axis=1) > 0.5
            placed = tn(sel[:, rows], asked[...])
            mixed[rows] = jnp.where(here, placed, near[rows].astype(f32)).astype(bf16)
            h = hidden_c[rows] + nn(mixed[rows], wo[...])
            hidden_d[rows] = h
            hidden_e[rows] = h
            normed[rows] = norm_rows(h, fgain[...], fbias[...]).astype(bf16)
        gone.start(1)
        normed_t[...] = by_owner(perm[...], normed[...])
        grad_norm[...] = jnp.zeros_like(grad_norm)

    @pl.when(step < last)
    def _():
        for rows in tiles(n, 256):
            a, s = gelu_both(nn(normed[rows], up[...]))
            a = a.astype(bf16)
            hidden_e[rows] += nn(a, down[...])
            place_hidden(seq_order, step, a, rows, active_t)
            g = (nt(cot[rows], down[...]) * s).astype(bf16)
            grad_norm[rows] += nt(g, up[...])
            lifted[rows] = g
        two_halves(normed_t, lifted, up_keep, up_send)
        two_halves(active_t, cot, down_keep, down_send)

    @pl.when(step == last)
    def _():
        for rows in tiles(n, 256):
            out[rows] = hidden_e[rows].astype(bf16)
        gone.start(0)
        finish_back(n, hidden_d, cot, fgain, grad_norm, grad_d, sums)
        gone.start(2)
        for rows in tiles(n, 256):
            branch = grad_d[rows].astype(bf16)
            lifted[rows] = branch
            grad_mixed[rows] = nt(branch, wo[...]).astype(bf16)
        grad_asked[...] = nn(sel[...], grad_mixed[...]).astype(bf16)
        for rows in tiles(n, 256):
            here = jnp.concatenate([flag[rows]] * (d // PAIR), axis=1) > 0.5
            g = grad_mixed[rows]
            grad_mixed[rows] = jnp.where(here, 0.0, g.astype(f32)).astype(bf16)
        gone.start(3)
        normed_t[...] = by_owner(perm[...], mixed[...])
        two_halves(normed_t, lifted, up_keep, up_send)
        gone.wait()


def upper_both(doc_order, seq_order, hidden_c, near, asked, sel, cot, wo, vectors, perm, up, down):
    n, d = near.shape
    ff, slots = up.shape[1], sel.shape[0]
    docs, seqs = doc_order.shape[0], seq_order.shape[0]
    into, outof, shapes = hidden_specs(d, ff, docs)
    fc = ff // docs
    moved = [sds((n, d), t) for t in (bf16, bf16, f32, bf16)]
    grad_asked, *halves, sums, out, mixed, grad_d, grad_mixed = pl.pallas_call(
        upper_kernel,
        out_shape=[sds((slots, d), bf16), *shapes, sds((8, d), f32), *moved],
        grid_spec=pltpu.PrefetchScalarGridSpec(
            num_scalar_prefetch=2,
            grid=(docs + 1,),
            in_specs=[
                whole(n, d), whole(n, d), whole(slots, d), whole(slots, n), whole(n, d), whole(d, d),
                whole(len(NORMS), d), whole(d, d), *into,
            ],
            out_specs=[whole(slots, d), *outof, whole(8, d), *[anywhere()] * len(moved)],
            scratch_shapes=[
                *[pltpu.VMEM(x.shape, x.dtype) for x in moved],
                pltpu.VMEM((n, d), f32), pltpu.VMEM((n, d), bf16), pltpu.VMEM((n, d), f32), pltpu.VMEM((n, d), f32),
                pltpu.VMEM((n, PAIR), f32), pltpu.VMEM((d, n), bf16), hidden_scratch(n, fc, seqs),
                pltpu.VMEM((n, fc), bf16), pltpu.SemaphoreType.DMA((len(moved),)),
            ],
        ),
        **params(12 * n * d * ff + 6 * n * d * d, 8 * d * ff + 40 * n * d),
    )(doc_order, seq_order, hidden_c, near, asked, sel, cot, wo, vectors, perm, up, down)
    return out, mixed, grad_d, grad_mixed, grad_asked, *halves, sums


def unpool(held, gp, following, taps, made):
    m = gp.shape[0]
    last = lax.broadcasted_iota(jnp.int32, gp.shape, 0) == m - 1
    later = jnp.where(last, following, pltpu.roll(gp, m - 1, 0))
    made[pl.ds(0, m, stride=STRIDE)] = taps[2:3] * gp
    made[pl.ds(1, m, stride=STRIDE)] = taps[3:4] * gp
    made[pl.ds(2, m, stride=STRIDE)] = taps[4:5] * gp + taps[0:1] * later
    made[pl.ds(3, m, stride=STRIDE)] = taps[1:2] * later
    return [
        jnp.sum(gp * held[pl.ds(6 + t, m, stride=STRIDE)], axis=0, keepdims=True) for t in range(TAPS)
    ]


def upper_pairs_kernel(came, outs, gone, gkv, held, made, normed_t):
    gw_keep, gw_send, grad_norm, sums = outs
    normed, perm = came.got(0), came.got(1)
    normed_t[...] = by_owner(perm[...], normed[...])
    gp, from_left, from_right, following, rim = (came.got(i) for i in range(2, 7))
    sums[...] = jnp.zeros_like(sums)
    n, d = normed.shape
    m = n // STRIDE
    for i in range(2):
        x, taps, w = (came.got(7 + 3 * i + j) for j in range(3))
        for c in tiles(d, PAIR):
            held[:8] = rim[RAW - 8 :, i * d + c.start : i * d + c.stop].astype(f32)
            held[8:] = x[:, c].astype(f32)
            total = gp[i, :, c]
            edge = jnp.zeros((m - 2 * SIDE, PAIR), f32)
            total = total + jnp.concatenate([from_left[i, :, c], edge, from_right[i, :SIDE, c]], axis=0)
            later = from_right[i, SIDE : SIDE + 1, c] + following[i, 0:1, c]
            parts = unpool(held, total, later, taps[:, c], made)
            gkv[:, c] = made[...].astype(bf16)
            for t, part in enumerate(parts):
                sums[8 * i + t : 8 * i + t + 1, c] = part
        if i == 0:
            grad_norm[...] = nt(gkv[...], w[...])
        else:
            grad_norm[...] += nt(gkv[...], w[...])
            gone.start(2, 3)
        part = slice(i * d, (i + 1) * d)
        two_halves(normed_t, gkv, gw_keep.at[:, part], gw_send.at[:, part])
    gone.start(0, 1)


def upper_pairs_back(gp, from_left, from_right, following, k, v, rim, kpool, vpool, normed, wk, wv, perm):
    n, d = k.shape
    return moved_call(
        upper_pairs_kernel,
        (normed, perm, gp, from_left, from_right, following, rim, k, kpool, wk, v, vpool, wv),
        [sds((d // 2, 2 * d), bf16)] * 2 + [sds((n, d), f32), sds((16, d), f32)],
        [
            pltpu.VMEM((n, d), bf16),
            pltpu.VMEM((n + 8, PAIR), f32),
            pltpu.VMEM((n, PAIR), f32),
            pltpu.VMEM((d, n), bf16),
        ],
        (10 * n * d * d, 20 * n * d),
    )


def upper_queries_kernel(came, outs, gone, grad_norm):
    gq, grad_c, branch, sums = outs
    gq_near, gq_asked, sel = (came.got(i) for i in range(3))
    n, d = gq_near.shape
    for rows in tiles(n, 256):
        gq[rows] = (gq_near[rows].astype(f32) + tn(sel[:, rows], gq_asked[...])).astype(bf16)
    gone.start(0)
    wq, pairs_norm = came.got(3), came.got(4)
    for rows in tiles(n, 256):
        grad_norm[rows] = pairs_norm[rows] + nt(gq[rows], wq[...])
    hidden, grad, vectors = (came.got(i) for i in range(5, 8))
    gain = of_norm(vectors, "upper_again")
    finish_back(n, hidden, grad, gain, grad_norm, grad_c, sums)
    branch[...] = grad_c[...].astype(bf16)
    gone.start(1, 2, 3)


def upper_queries_back(gq_near, gq_asked, sel, hidden, grad, pairs_norm, gain, wq):
    n, d = gq_near.shape
    return moved_call(
        upper_queries_kernel,
        (gq_near, gq_asked, sel, wq, pairs_norm, hidden, grad, gain),
        [sds((n, d), bf16), sds((n, d), f32), sds((n, d), bf16), sds((8, d), f32)],
        [pltpu.VMEM((n, d), f32)],
        (2 * n * d * d, 24 * n * d),
    )


def lower_project_kernel(came, outs, gone, gkv, grad_norm, low_t, sums):
    gw_keep, gw_send, grad_in = outs
    normed, low = came.got(0), came.got(1)
    n, d = normed.shape
    low_t[...] = by_owner(low[...], normed[...])
    gq, wq = came.got(2), came.got(3)
    grad_norm[...] = nt(gq[...], wq[...])
    two_halves(low_t, gq, gw_keep.at[:, :d], gw_send.at[:, :d])
    left, right = came.got(4), came.got(5)
    for i in range(2):
        g, w = came.got(6 + 2 * i), came.got(7 + 2 * i)
        gkv[...] = g[...].astype(bf16)
        gkv[:REACH_ONE] = (g[:REACH_ONE] + left[i]).astype(bf16)
        gkv[n - REACH_ONE :] = (g[n - REACH_ONE :] + right[i]).astype(bf16)
        grad_norm[...] += nt(gkv[...], w[...])
        part = slice((1 + i) * d, (2 + i) * d)
        two_halves(low_t, gkv, gw_keep.at[:, part], gw_send.at[:, part])
    x, grad, vectors = (came.got(i) for i in range(10, 13))
    gain = of_norm(vectors, "lower_again")
    sums[...] = jnp.zeros_like(sums)
    for rows in tiles(n, 128):
        back, by_gain, by_bias = norm_back(x[rows].astype(f32), gain[...], grad_norm[rows])
        grad_in[rows] = grad[rows] + back
        sums[0:1] += by_gain
        sums[1:2] += by_bias
    gone.start(2)
    at = 8
    for i in range(13, 17):
        part = came.got(i)
        sums[at : at + part.shape[0]] = part[...]
        at += part.shape[0]
    for rows, out in zip(tiles(d, d // 2), (gw_keep, gw_send)):
        out[:, 3 * d :] = nt(low[rows], sums[...].astype(bf16)).astype(bf16)
    gone.start(0, 1)


def lower_project_back(gq, gk, gv, left, right, normed, x, grad, gain, wq, wk, wv, low, *sums):
    n, d = gq.shape
    return moved_call(
        lower_project_kernel,
        (normed, low, gq, wq, left, right, gk, wk, gv, wv, x, grad, gain, *sums),
        [sds((d // 2, 3 * d + PAIR), bf16)] * 2 + [sds((n, d), f32)],
        [pltpu.VMEM((n, d), bf16), pltpu.VMEM((n, d), f32), pltpu.VMEM((d, n), bf16), pltpu.VMEM((PAIR, d), f32)],
        (14 * n * d * d, 24 * n * d),
    )


def lower_back_kernel(
    doc_order, seq_order, branch_c, normed, vectors, perm, active, slope, up, down, grad_c, hidden_b, mixed, wo, gq_upper, normed_upper,
    up_keep, up_send, down_keep, down_send, grad_b, grad_mixed, sums,
    branch, grad_norm, normed_t, active_t, lifted, grad_held, hidden_held, mixed_held, wo_held, gq_held, upper_held, sems,
):
    step = pl.program_id(0)
    n, d = branch_c.shape
    last = pl.num_programs(0) - 2
    fgain = of_norm(vectors, "lower_fgain")
    late = Mover(
        (grad_c, hidden_b, mixed, wo, gq_upper, normed_upper),
        (grad_held, hidden_held, mixed_held, wo_held, gq_held, upper_held),
        sems,
    )

    @pl.when(step == 0)
    def _():
        late.start()
        normed_t[...] = by_owner(perm[...], normed[...])
        grad_norm[...] = jnp.zeros_like(grad_norm)

    @pl.when(step < last)
    def _():
        for rows in tiles(n, 256):
            g = (nt(branch_c[rows], down[...]) * slope[rows].astype(f32)).astype(bf16)
            grad_norm[rows] += nt(g, up[...])
            lifted[rows] = g
            place_hidden(seq_order, step, active[rows], rows, active_t)
        two_halves(active_t, branch_c, down_keep, down_send)
        two_halves(normed_t, lifted, up_keep, up_send)

    @pl.when(step == last)
    def _():
        late.wait()
        finish_back(n, hidden_held, grad_held, fgain, grad_norm, grad_b, sums)
        for rows in tiles(n, 256):
            branch[rows] = grad_b[rows].astype(bf16)
            grad_mixed[rows] = nt(branch[rows], wo_held[...]).astype(bf16)
        normed_t[...] = by_owner(perm[...], mixed_held[...])
        two_halves(normed_t, branch, up_keep, up_send)

    @pl.when(step == last + 1)
    def _():
        normed_t[...] = by_owner(perm[...], upper_held[...])
        two_halves(normed_t, gq_held, up_keep, up_send)


def lower_back(
    doc_order, seq_order, branch_c, grad_c, hidden_b, normed, active, slope, mixed, wo, vectors, perm, up, down, gq_upper,
    normed_upper,
):
    n, d = grad_c.shape
    ff = up.shape[1]
    docs, seqs = doc_order.shape[0], seq_order.shape[0]
    fc = ff // docs
    into, outof, shapes = hidden_specs(d, ff, docs, 2)
    lanes = pl.BlockSpec((n, fc), lambda c, *_: (0, jnp.minimum(c, docs - 1)))
    return pl.pallas_call(
        lower_back_kernel,
        out_shape=[*shapes, sds((n, d), f32), sds((n, d), bf16), sds((8, d), f32)],
        grid_spec=pltpu.PrefetchScalarGridSpec(
            num_scalar_prefetch=2,
            grid=(docs + 2,),
            in_specs=[
                whole(n, d), whole(n, d), whole(len(NORMS), d), whole(d, d), lanes, lanes, *into, *[anywhere()] * 6,
            ],
            out_specs=[*outof, whole(n, d), whole(n, d), whole(8, d)],
            scratch_shapes=[
                pltpu.VMEM((n, d), bf16), pltpu.VMEM((n, d), f32), pltpu.VMEM((d, n), bf16),
                hidden_scratch(n, fc, seqs), pltpu.VMEM((n, fc), bf16),
                pltpu.VMEM((n, d), f32), pltpu.VMEM((n, d), f32), pltpu.VMEM((n, d), bf16), pltpu.VMEM((d, d), bf16),
                pltpu.VMEM((n, d), bf16), pltpu.VMEM((n, d), bf16), pltpu.SemaphoreType.DMA((6,)),
            ],
        ),
        **params(8 * n * d * ff + 4 * n * d * d, 12 * n * ff + 30 * n * d),
    )(
        doc_order, seq_order, branch_c, normed, vectors, perm, active, slope, up, down, grad_c, hidden_b, mixed, wo,
        gq_upper, normed_upper,
    )


def shifted(value, steps):
    count = lax.axis_size("seq")
    pairs = [(i, i + steps) for i in range(count) if 0 <= i + steps < count]
    return lax.ppermute(value, "seq", pairs)


def exchanged(value, axis, bit):
    count = lax.axis_size(axis)
    return lax.ppermute(value, axis, [(i, i ^ bit) for i in range(count)])


def bits(axis, first=1):
    count = lax.axis_size(axis)
    return [(axis, 1 << b) for b in range(count.bit_length()) if first <= 1 << b < count]


def orders():
    cores = [("seq", 1)]
    return cores + bits("doc") + bits("seq", 2), cores + bits("doc")[::-1] + bits("seq", 2)


def owners(order):
    count = lax.axis_size("doc") * lax.axis_size("seq")
    flips = {"doc": [], "seq": []}
    for axis in flips:
        for p in range(count):
            flips[axis].append(sum(b for i, (a, b) in enumerate(order) if a == axis and p >> (len(order) - 1 - i) & 1))
    return tuple(lax.axis_index(a) ^ jnp.array(flips[a], jnp.int32) for a in ("doc", "seq"))


def permutation(order, d):
    doc, seq = owners(order)
    owner = doc * lax.axis_size("seq") + seq
    size = d // owner.shape[0]
    source = (owner[:, None] * size + jnp.arange(size, dtype=jnp.int32)[None, :]).reshape(-1)
    return (source[:, None] == jnp.arange(d, dtype=jnp.int32)[None, :]).astype(bf16)


def hidden_orders(order):
    def places(axis):
        steps = [b for a, b in order if a == axis]
        value = jnp.arange(lax.axis_size(axis), dtype=jnp.int32) ^ lax.axis_index(axis)
        place = jnp.zeros_like(value)
        for b in steps:
            place = 2 * place + (value // b) % 2
        return place

    return places("doc"), places("seq")


class Halving:
    def __init__(self, keep, send, order):
        self.order, self.at, self.rows = order, 1, keep.shape[0]
        self.terms = [keep, exchanged(send, *order[0])]

    def prepare(self):
        self.rows //= 2
        self.send = self.total(self.rows).astype(bf16)

    def go(self):
        self.terms = self.terms + [exchanged(self.send, *self.order[self.at])]
        self.at += 1

    def left(self):
        return self.at < len(self.order)

    def total(self, start=0):
        out = None
        for t in self.terms:
            t = t[start : start + self.rows].astype(f32)
            out = t if out is None else out + t
        return out


def stepped(order):
    steps = []
    for axis, bit in order:
        if axis == "seq" and bit > 1 and steps[-1][0][0] == "seq" and steps[-1][0][1] > 1 and len(steps[-1]) == 1:
            steps[-1] = steps[-1] + [(axis, bit)]
        else:
            steps.append([(axis, bit)])
    return steps


def flips(step):
    axis = step[0][0]
    places = range(len(step))
    return [(axis, sum(step[i][1] for i in places if p >> (len(step) - 1 - i) & 1)) for p in range(1, 1 << len(step))]


def tied(*values):
    return lax.optimization_barrier(values)


def arrived(values, *halvings):
    values, terms = tied(values, [h.terms for h in halvings])
    for h, t in zip(halvings, terms):
        h.terms = t
    return values


def sent(values, *halvings):
    for h in halvings:
        h.prepare()
    values, _ = tied(values, [h.send for h in halvings])
    for h in halvings:
        h.go()
    return values


def in_turn(halvings):
    before = None
    for h in halvings:
        if h.left():
            if before is not None:
                h.terms, _ = tied(h.terms, before)
            h.prepare()
            before = h.send
            h.go()


def others(value, step):
    return [exchanged(value, *f) for f in flips(step)]


def summed(value, steps):
    for step in steps:
        value = sum(others(value, step), value)
    return value


def merged_apart(part, steps):
    half = part.shape[0] // 2
    axis, bit = steps[0][0]
    second = (lax.axis_index(axis) & bit) > 0
    mine = jnp.where(second, part[half:], part[:half])
    other = exchanged(jnp.where(second, part[:half], part[half:]), axis, bit)
    mine = merged(merge(mine, other), steps[1:])
    other = exchanged(mine, axis, bit)
    return jnp.concatenate([jnp.where(second, other, mine), jnp.where(second, mine, other)], axis=0)


def merge(*parts):
    tops = [p[:, HDIM : HDIM + 1] for p in parts]
    top = functools.reduce(jnp.maximum, tops)
    total = sum(p * jnp.exp(t - top) for p, t in zip(parts, tops))
    row = lax.broadcasted_iota(jnp.int32, total.shape, 1)
    return jnp.where(row == HDIM, top, total)


def merged(part, steps):
    for step in steps:
        part = merge(part, *others(part, step))
    return part


def body(
    tokens, cotangent, counts, positions, lower_again, lower_abias, lower_query, lower_key, lower_value, lower_out,
    lower_fgain, lower_fbias, lower_up, lower_down, upper_again, upper_abias, upper_query, upper_key, upper_value,
    upper_out, upper_fgain, upper_fbias, upper_up, upper_down, upper_kpool, upper_vpool,
):
    seq_count = lax.axis_size("seq")
    seq_index = lax.axis_index("seq")
    x, cot = tokens[0], cotangent[0]
    n, d = x.shape
    m = n // STRIDE
    flags = jnp.stack([seq_index == 0, seq_index == seq_count - 1]).astype(jnp.int32)
    slot_count = positions.shape[1]
    slots = jnp.arange(slot_count, dtype=jnp.int32)
    place = jnp.where(slots < counts[0], positions[0] - seq_index * n, -1)
    sel = (place[:, None] == jnp.arange(n, dtype=jnp.int32)[None, :]).astype(bf16)
    kpool = jnp.pad(upper_kpool, ((0, 8 - TAPS), (0, 0)))
    vpool = jnp.pad(upper_vpool, ((0, 8 - TAPS), (0, 0)))
    taps = jnp.concatenate([kpool, vpool], axis=1)
    low_first, high_first = orders()
    perm_low, perm_high = permutation(low_first, d), permutation(high_first, d)
    doc_order, seq_order = hidden_orders(high_first)
    along = stepped(bits("seq"))

    first_norm = jnp.concatenate([lower_again, lower_abias]).reshape(2, d)
    norm_a, ka, va, qa = project(x, first_norm, lower_key, lower_value, lower_query)
    qa, lower_again = tied(qa, lower_again)
    vectors = jnp.concatenate(
        [
            lower_again, lower_abias, lower_fgain, lower_fbias, upper_again, upper_abias, upper_fgain, upper_fbias,
        ]
    ).reshape(len(NORMS), d)
    ends = lambda rows: jnp.concatenate([ka[rows], va[rows]], axis=1)
    left = shifted(ends(slice(n - REACH_ONE, n)), 1)
    right = shifted(ends(slice(0, REACH_ONE)), -1)
    mixed_a, weights_a = local_attention(flags, qa, ka, va, left, right)
    (
        hidden_b, norm_b, active_b, slope_b, hidden_c, norm_c, qc, kc, vc, pooled, mine, to_left, to_right, asked_q,
    ) = lower_forward(
        x, mixed_a, lower_out, vectors, lower_up, lower_down, upper_query, upper_key, upper_value, kpool, vpool, sel,
    )
    from_left = shifted(to_right, 1)
    from_right = shifted(to_left, -1)
    asked_q = summed(asked_q, along[:1])
    more = others(asked_q, along[1])
    near, weights_c, kw, vw = near_attention(flags, qc, pooled, from_left, from_right, mine, taps)
    asked_q, more, kw = tied(asked_q, more, kw)
    asked_q = summed(sum(more, asked_q), along[2:])
    part = merged_apart(asked_part(asked_q, kw, vw), along)
    total = part[:, HDIM + 1 : HDIM + 2]
    logsum = jnp.broadcast_to(part[:, HDIM : HDIM + 1] + jnp.log(total), (d // PAIR, 8, 2 * slot_count))
    asked = part[:, :HDIM] / total
    asked = asked.reshape(d // PAIR, HDIM, 2, slot_count).transpose(3, 0, 2, 1).reshape(slot_count, d)

    (
        out, mixed_c, grad_d, grad_mixed_c, grad_asked, up_keep, up_send, down_keep, down_send, sums_d,
    ) = upper_both(
        doc_order, seq_order, hidden_c, near, asked.astype(bf16), sel, cot, upper_out, vectors, perm_low, upper_up,
        upper_down,
    )
    flat = lambda x: x.reshape(-1, d)
    gu_up = Halving(up_keep, up_send, low_first)
    gu_down = Halving(flat(down_keep), flat(down_send), high_first)
    more = others(grad_asked, along[0])
    gq_near, near_own, to_left, to_right = near_back(qc, kw, vw, weights_c, grad_mixed_c)
    grad_asked, more, near_own, to_left, to_right = arrived(
        (grad_asked, more, near_own, to_left, to_right), gu_up, gu_down
    )
    grad_asked = sum(more, grad_asked)
    more = others(grad_asked, along[1])
    from_left_back = shifted(to_right, 1)
    from_right_back = shifted(to_left, -1)
    grad_asked, more = sent((grad_asked, more), gu_up, gu_down)
    grad_asked = summed(sum(more, grad_asked), along[2:])
    gq_asked, gp, following = asked_back(
        flags, asked_q, kw, vw, logsum, asked, grad_asked, near_own, to_right[:, :8]
    )
    gq_asked = summed(gq_asked, along[:1])
    more = others(gq_asked, along[1])
    gp, _ = tied(gp, gq_asked)
    gw_keep, gw_send, pairs_norm, sums_p = upper_pairs_back(
        gp, from_left_back, from_right_back, following, kc, vc, from_left[SIDE:], kpool, vpool, norm_c, upper_key,
        upper_value, perm_high,
    )
    gq_asked, more, pairs_norm, gw_send = tied(gq_asked, more, pairs_norm, gw_send)
    gu_pair = Halving(gw_keep, gw_send, high_first)
    gq_asked = summed(sum(more, gq_asked), along[2:])
    pairs_norm = arrived(pairs_norm, gu_up, gu_down)
    pairs_norm = sent(pairs_norm, gu_up, gu_down)
    gq_upper, grad_c, branch_c, sums_c = upper_queries_back(
        gq_near, gq_asked, sel, hidden_c, grad_d, pairs_norm, vectors, upper_query
    )
    branch_c = arrived(branch_c, gu_pair)
    branch_c = sent(branch_c, gu_pair)
    up_keep, up_send, down_keep, down_send, grad_b, grad_mixed_a, sums_b = lower_back(
        doc_order, seq_order, branch_c, grad_c, hidden_b, norm_b, active_b, slope_b, mixed_a, lower_out,
        vectors, perm_low, lower_up, lower_down, gq_upper, norm_c,
    )
    grad_mixed_a, up_send, down_send = arrived((grad_mixed_a, up_send, down_send), gu_up, gu_down, gu_pair)
    gl_up = Halving(up_keep, up_send, low_first)
    gl_down = Halving(flat(down_keep), flat(down_send), high_first)
    grad_mixed_a = sent(grad_mixed_a, gu_up, gu_down, gu_pair)
    grad_mixed_a = arrived(grad_mixed_a, gl_up, gl_down)
    in_turn([gl_up, gl_down])
    grad_mixed_a, _ = tied(grad_mixed_a, gl_down.send)
    gq, gk, gv, to_left, to_right = local_back(qa, ka, va, left, right, weights_a, grad_mixed_a)
    back_last = shifted(to_left, -1)
    back_first = shifted(to_right, 1)
    grad_b, gq = arrived((grad_b, gq), gu_up, gu_pair)
    back_first, back_last = sent((back_first, back_last), gu_up, gu_pair)
    back_first, back_last = arrived((back_first, back_last), gu_down)
    grad_b = sent(grad_b, gu_down)
    gw_keep, gw_send, grad_in = lower_project_back(
        gq, gk, gv, back_first, back_last, norm_a, x, grad_b, vectors, lower_query, lower_key, lower_value,
        perm_low, sums_b, sums_c, sums_d, sums_p,
    )
    gw_send = arrived(gw_send, gu_pair, gu_up, gu_down, gl_up, gl_down)
    gl_qkv = Halving(gw_keep, gw_send, low_first)
    in_turn([gl_up, gl_down, gl_qkv, gu_pair])
    gl_down.terms = arrived(gl_down.terms, gu_pair)
    in_turn([gl_down, gl_up, gl_qkv, gl_up, gl_down])
    gl_qkv.terms = arrived(gl_qkv.terms, gl_up)
    in_turn([gl_qkv])
    gl_qkv.terms = arrived(gl_qkv.terms, gl_down)
    in_turn([gl_qkv])
    every = (gl_up, gl_down, gl_qkv, gu_up, gu_down, gu_pair)
    while any(h.left() for h in every):
        in_turn(every)
    for h in every:
        if h is not gl_qkv:
            h.terms, _ = tied(h.terms, gl_qkv.send)
    gu_up, gu_down, gu_pair, gl_up, gl_down, gl_qkv = (
        h.total() for h in (gu_up, gu_down, gu_pair, gl_up, gl_down, gl_qkv)
    )
    small = gl_qkv[:, 3 * d :].T
    sums_a, sums_b, sums_c, sums_d, sums_p = (small[r] for r in (*tiles(32, 8), slice(32, 48)))
    ff = lower_up.shape[1]
    part = lambda got, i: got[:, i * d : (i + 1) * d]
    return (
        out[None],
        grad_in[None],
        sums_a[0],
        sums_a[1],
        part(gl_qkv, 0),
        part(gl_qkv, 1),
        part(gl_qkv, 2),
        gl_up[:, ff : ff + d],
        sums_b[0],
        sums_b[1],
        gl_up[:, :ff],
        gl_down,
        sums_c[0],
        sums_c[1],
        gl_up[:, ff + d :],
        part(gu_pair, 0),
        part(gu_pair, 1),
        gu_up[:, ff:],
        sums_d[0],
        sums_d[1],
        gu_up[:, :ff],
        gu_down,
        sums_p[0:TAPS],
        sums_p[8 : 8 + TAPS],
    )


def solution(mesh):
    tokens = P("doc", "seq", None)
    every = ("doc", "seq")
    vector, matrix, taps = P(every), P(every, None), P(None, every)
    layer = (vector, vector, matrix, matrix, matrix, matrix, vector, vector, matrix, matrix)
    return jax.shard_map(
        body,
        mesh=mesh,
        in_specs=(tokens, tokens, P("doc"), P("doc", None)) + (P(),) * 22,
        out_specs=(tokens, tokens) + layer + layer + (taps, taps),
        check_vma=False,
    )
```

```python
import functools

import jax
import jax.numpy as jnp
from jax import lax
from jax.experimental import pallas as pl
from jax.experimental.pallas import tpu as pltpu
from jax.sharding import PartitionSpec as P

HDIM = 64
REACH_ONE = 64
REACH_TWO = 256
STRIDE = 4
TAPS = 5
QB = 128
PAIR = 2 * HDIM
WIN_ONE = QB + 2 * REACH_ONE
SIDE = REACH_TWO // STRIDE
WIN_TWO = QB // STRIDE + 2 * SIDE
RAW = 16
eps = 1e-05
GROUP = 6
far_below = -1e30
scale = HDIM**-0.5
f32 = jnp.float32
bf16 = jnp.bfloat16

MILLS = 0.34
MILLS_POLY = (
    0.13590356504727755,
    0.13101844409724564,
    0.1513778923259517,
    -0.01998659482308463,
    0.25210690821609844,
    -0.1936388145328779,
    0.04321858184569336,
)
INV_SQRT_2PI = 0.3989422804014327


def nn(a, b):
    return lax.dot_general(a, b, (((1,), (0,)), ((), ())), preferred_element_type=f32)


def nt(a, b):
    return lax.dot_general(a, b, (((1,), (1,)), ((), ())), preferred_element_type=f32)


def tn(a, b):
    return lax.dot_general(a, b, (((0,), (0,)), ((), ())), preferred_element_type=f32)


def norm_rows(x, gain, bias):
    average = jnp.mean(x, axis=-1, keepdims=True)
    centred = x - average
    variance = jnp.mean(centred * centred, axis=-1, keepdims=True)
    return centred * lax.rsqrt(variance + eps) * gain + bias


def norm_back(x, gain, grad):
    average = jnp.mean(x, axis=-1, keepdims=True)
    centred = x - average
    variance = jnp.mean(centred * centred, axis=-1, keepdims=True)
    spread = lax.rsqrt(variance + eps)
    unit = centred * spread
    lifted = grad * gain
    first = jnp.mean(lifted, axis=-1, keepdims=True)
    second = jnp.mean(lifted * unit, axis=-1, keepdims=True)
    back = spread * (lifted - first - unit * second)
    return back, jnp.sum(grad * unit, axis=0, keepdims=True), jnp.sum(grad, axis=0, keepdims=True)


def gelu_both(u):
    t = 1.0 / (1.0 + MILLS * jnp.abs(u))
    e = jnp.exp(-0.5 * (u * u))
    poly = jnp.full_like(u, MILLS_POLY[-1])
    for c in MILLS_POLY[-2::-1]:
        poly = poly * t + c
    tail = poly * (t * e)
    cdf = jnp.where(u >= 0, 1.0 - tail, tail)
    return u * cdf, cdf + u * e * INV_SQRT_2PI


def whole(*shape):
    return pl.BlockSpec(shape, lambda *_: (0,) * len(shape), pipeline_mode=pl.Buffered(1))


def smem():
    return pl.BlockSpec(memory_space=pltpu.SMEM)


def params(flops, size, mib=58):
    return dict(
        compiler_params=pltpu.CompilerParams(vmem_limit_bytes=mib << 20),
        cost_estimate=pl.CostEstimate(flops=flops, bytes_accessed=size, transcendentals=0),
    )


def sds(shape, dtype):
    return jax.ShapeDtypeStruct(shape, dtype)


def anywhere():
    return pl.BlockSpec(memory_space=pl.ANY)


class Mover:
    def __init__(self, sources, buffers, sems):
        self.buffers = buffers
        self.copies = [pltpu.make_async_copy(s, b, sems.at[i]) for i, (s, b) in enumerate(zip(sources, buffers))]

    def start(self, *which):
        for i in which or range(len(self.copies)):
            self.copies[i].start()

    def wait(self, *which):
        for i in which or range(len(self.copies)):
            self.copies[i].wait()

    def got(self, i):
        self.copies[i].wait()
        return self.buffers[i]


def moved_call(kernel, ins, outs, scratch, cost):
    def body(*refs):
        n_in, n_out = len(ins), len(outs)
        sources, targets, rest = refs[:n_in], refs[n_in : n_in + n_out], refs[n_in + n_out :]
        in_bufs, out_bufs, rest = rest[:n_in], rest[n_in : n_in + n_out], rest[n_in + n_out :]
        in_sems, out_sems, *rest = rest
        came = Mover(sources, in_bufs, in_sems)
        came.start()
        gone = Mover(out_bufs, targets, out_sems)
        kernel(came, out_bufs, gone, *rest)
        gone.wait()

    return pl.pallas_call(
        body,
        out_shape=list(outs),
        in_specs=[anywhere()] * len(ins),
        out_specs=[anywhere()] * len(outs),
        scratch_shapes=[pltpu.VMEM(x.shape, x.dtype) for x in (*ins, *outs)]
        + [pltpu.SemaphoreType.DMA((len(ins),)), pltpu.SemaphoreType.DMA((len(outs),))]
        + scratch,
        **params(*cost),
    )(*ins)


NORMS = ("lower_again", "lower_abias", "lower_fgain", "lower_fbias")
NORMS += ("upper_again", "upper_abias", "upper_fgain", "upper_fbias")


def of_norm(vectors, name):
    i = NORMS.index(name)
    return vectors.at[i : i + 1]


def tiles(rows, step):
    return [slice(i, i + step) for i in range(0, rows, step)]


def project_kernel(came, outs, gone):
    x, vectors = came.got(0), came.got(1)
    gain, bias = vectors.at[0:1], vectors.at[1:2]
    normed = outs[0]
    parts = tiles(x.shape[0], 256)
    for rows in parts:
        normed[rows] = norm_rows(x[rows].astype(f32), gain[...], bias[...]).astype(bf16)
    gone.start(0)
    for i in range(1, 4):
        w = came.got(1 + i)
        for rows in parts:
            outs[i][rows] = nn(normed[rows], w[...]).astype(bf16)
        gone.start(i)


def project(x, vectors, wk, wv, wq):
    n, d = x.shape
    return moved_call(
        project_kernel, (x, vectors, wk, wv, wq), [sds((n, d), bf16)] * 4, [], (6 * n * d * d, 10 * n * d + 6 * d * d)
    )


def head_masks(rows):
    lane = lax.broadcasted_iota(jnp.int32, (rows, PAIR), 1)
    return lane < HDIM


def both_heads(x):
    first = head_masks(x.shape[0])
    zero = jnp.zeros_like(x)
    return jnp.concatenate([jnp.where(first, x, zero), jnp.where(first, zero, x)], axis=0)


def own_blocks(x):
    n = x.shape[1] // 2
    return jnp.concatenate([x[:HDIM, :n], x[HDIM:, n:]], axis=0).T


def softmax_columns(scores):
    top = jnp.max(scores, axis=0, keepdims=True)
    raised = jnp.exp(scores - top)
    total = jnp.sum(raised, axis=0, keepdims=True)
    return (raised * (1.0 / total)).astype(bf16)


def window_bias(kind):
    win = WIN_ONE if kind == 1 else WIN_TWO
    key = lax.broadcasted_iota(jnp.int32, (win, QB), 0)
    query = lax.broadcasted_iota(jnp.int32, (win, QB), 1)
    if kind == 1:
        offset, reach = key - query, 2 * REACH_ONE
    else:
        offset, reach = STRIDE * key - query, 2 * REACH_TWO
    return jnp.where((offset >= 0) & (offset <= reach), 0.0, far_below)


def edge_bias(bias, start, edge, length, flags):
    win = bias.shape[0]
    key = lax.broadcasted_iota(jnp.int32, bias.shape, 0) + start
    if start < edge:
        limit = jnp.where(flags[0] > 0, edge, 0)
        bias = jnp.where(key < limit, far_below, bias)
    if start + win > length - edge:
        limit = jnp.where(flags[1] > 0, length - edge, length)
        bias = jnp.where(key >= limit, far_below, bias)
    return bias


def attend_blocks(blocks):
    scores = [nt(kb, both_heads(qb * scale)) for qb, kb, _, _ in blocks]
    weights = [softmax_columns(s + jnp.concatenate([b[3], b[3]], axis=1)) for s, b in zip(scores, blocks)]
    outs = [tn(b[2], w) for b, w in zip(blocks, weights)]
    return [own_blocks(o) for o in outs], weights


def back_blocks(blocks):
    grads = [both_heads(grad) for *_, grad in blocks]
    changes = [nt(b[2], g) for b, g in zip(blocks, grads)]
    values = [nn(b[3], g) for b, g in zip(blocks, grads)]
    scores = []
    for b, change in zip(blocks, changes):
        share = b[3].astype(f32)
        inner = jnp.sum(share * change, axis=0, keepdims=True) / jnp.sum(share, axis=0, keepdims=True)
        scores.append((share * (change - inner)).astype(bf16))
    keys = [nn(g, both_heads(b[0] * scale)) for g, b in zip(scores, blocks)]
    queries = [own_blocks(tn(b[1], g)) * scale for g, b in zip(scores, blocks)]
    return queries, keys, values


def local_kernel(flags, q, k, v, kl, vl, kr, vr, out, weights, kw, vw, base):
    n = q.shape[0]

    @pl.when(pl.program_id(0) == 0)
    def _():
        base[...] = window_bias(1)

    for wide, left, own, right in ((kw, kl, k, kr), (vw, vl, v, vr)):
        wide[:REACH_ONE] = left[...]
        wide[REACH_ONE : REACH_ONE + n] = own[...]
        wide[REACH_ONE + n :] = right[...]
    todo = []
    for b, rows in enumerate(tiles(n, QB)):
        window = slice(b * QB, b * QB + WIN_ONE)
        bias = edge_bias(base[...], b * QB, REACH_ONE, n + 2 * REACH_ONE, flags)
        todo.append((q[rows], kw[window], vw[window], bias))
    for b in range(0, len(todo), GROUP):
        for i, (mixed, w) in enumerate(zip(*attend_blocks(todo[b : b + GROUP]))):
            out[(b + i) * QB : (b + i + 1) * QB] = mixed.astype(bf16)
            weights[0, b + i] = w


def pair_block(rows, offset=0):
    return pl.BlockSpec((rows, PAIR), lambda g, offset=offset: (0, g + offset))


def two_rows(rows):
    return pl.BlockSpec((2, rows, PAIR), lambda g: (0, 0, g))


def local_attention(flags, q, k, v, left, right):
    n, d = q.shape
    pairs, blocks = d // PAIR, n // QB
    wide = n + 2 * REACH_ONE
    return pl.pallas_call(
        local_kernel,
        out_shape=[sds((n, d), bf16), sds((pairs, blocks, WIN_ONE, 2 * QB), bf16)],
        grid=(pairs,),
        in_specs=[smem()]
        + [pair_block(n)] * 3
        + [pair_block(REACH_ONE), pair_block(REACH_ONE, pairs)] * 2,
        out_specs=[
            pair_block(n),
            pl.BlockSpec((1, blocks, WIN_ONE, 2 * QB), lambda g: (g, 0, 0, 0)),
        ],
        scratch_shapes=[
            pltpu.VMEM((wide, PAIR), bf16),
            pltpu.VMEM((wide, PAIR), bf16),
            pltpu.VMEM((WIN_ONE, QB), f32),
        ],
        **params(4 * n * WIN_ONE * d * 2, 12 * n * d),
    )(flags, q, k, v, left, left, right, right)


def local_back_kernel(
    q, k, v, kl, vl, kr, vr, weights, grad, gq, gk, gv, to_left, to_right, kw, vw, ka, va
):
    n = q.shape[0]
    for wide, left, own, right in ((kw, kl, k, kr), (vw, vl, v, vr)):
        wide[:REACH_ONE] = left[...]
        wide[REACH_ONE : REACH_ONE + n] = own[...]
        wide[REACH_ONE + n :] = right[...]
    ka[...] = jnp.zeros_like(ka)
    va[...] = jnp.zeros_like(va)
    todo = []
    for b, rows in enumerate(tiles(n, QB)):
        window = slice(b * QB, b * QB + WIN_ONE)
        todo.append((q[rows], kw[window], vw[window], weights[0, b], grad[rows]))
    for first in range(0, len(todo), GROUP):
        for i, (gqb, gkb, gvb) in enumerate(zip(*back_blocks(todo[first : first + GROUP]))):
            b = first + i
            window = slice(b * QB, b * QB + WIN_ONE)
            gq[b * QB : (b + 1) * QB] = gqb.astype(bf16)
            ka[window] += gkb
            va[window] += gvb
    for i, (wide, own) in enumerate(((ka, gk), (va, gv))):
        to_left[i] = wide[:REACH_ONE]
        own[...] = wide[REACH_ONE : REACH_ONE + n]
        to_right[i] = wide[REACH_ONE + n :]


def local_back(q, k, v, left, right, weights, grad):
    n, d = q.shape
    pairs, blocks = d // PAIR, n // QB
    wide = n + 2 * REACH_ONE
    return pl.pallas_call(
        local_back_kernel,
        out_shape=[sds((n, d), bf16), sds((n, d), f32), sds((n, d), f32)] + [sds((2, REACH_ONE, d), f32)] * 2,
        grid=(pairs,),
        in_specs=[pair_block(n)] * 3
        + [pair_block(REACH_ONE), pair_block(REACH_ONE, pairs)] * 2
        + [pl.BlockSpec((1, blocks, WIN_ONE, 2 * QB), lambda g: (g, 0, 0, 0))]
        + [pair_block(n)],
        out_specs=[pair_block(n)] * 3 + [two_rows(REACH_ONE)] * 2,
        scratch_shapes=[pltpu.VMEM((wide, PAIR), bf16)] * 2 + [pltpu.VMEM((wide, PAIR), f32)] * 2,
        **params(10 * n * WIN_ONE * d * 2, 24 * n * d),
    )(q, k, v, left, left, right, right, weights, grad)


def first_pooled(tile, rim, raw, taps):
    row = (
        taps[0:1] * rim[0:1].astype(f32)
        + taps[1:2] * rim[1:2].astype(f32)
        + taps[2:3] * raw[0:1].astype(f32)
        + taps[3:4] * raw[1:2].astype(f32)
        + taps[4:5] * raw[2:3].astype(f32)
    )
    first = lax.broadcasted_iota(jnp.int32, tile.shape, 0) == 0
    return jnp.where(first, row, tile.astype(f32)).astype(bf16)


def pooled_window(wide, left, own, right, mine, taps):
    n = own.shape[0]
    wide[:SIDE] = left[:SIDE]
    wide[SIDE : SIDE + n] = own[...]
    wide[SIDE + n :] = right[:SIDE]
    rim = left[SIDE:].astype(f32)[RAW - 2 :]
    raw = mine[:RAW].astype(f32)
    wide[SIDE : SIDE + RAW] = first_pooled(own[:RAW], rim, raw, taps)
    rim = mine[RAW:].astype(f32)[RAW - 2 :]
    raw = right[SIDE:].astype(f32)
    wide[SIDE + n : SIDE + n + RAW] = first_pooled(right[:RAW], rim, raw, taps)


def near_kernel(flags, q, pk, pv, lk, lv, rk, rv, mk, mv, tk, tv, out, weights, kw, vw, base):
    n = q.shape[0]

    @pl.when(pl.program_id(0) == 0)
    def _():
        base[...] = window_bias(2)

    pooled_window(kw, lk, pk, rk, mk, tk[...])
    pooled_window(vw, lv, pv, rv, mv, tv[...])
    step = QB // STRIDE
    todo = []
    for b, rows in enumerate(tiles(n, QB)):
        window = slice(b * step, b * step + WIN_TWO)
        bias = edge_bias(base[...], b * step, SIDE, kw.shape[0], flags)
        todo.append((q[rows], kw[window], vw[window], bias))
    for b in range(0, len(todo), GROUP):
        for i, (mixed, w) in enumerate(zip(*attend_blocks(todo[b : b + GROUP]))):
            out[(b + i) * QB : (b + i + 1) * QB] = mixed.astype(bf16)
            weights[0, b + i] = w


def near_attention(flags, q, pooled, left, right, mine, taps):
    n, d = q.shape
    pairs, blocks, m = d // PAIR, n // QB, n // STRIDE
    wide = m + 2 * SIDE
    two = lambda rows: [pair_block(rows), pair_block(rows, pairs)]
    return pl.pallas_call(
        near_kernel,
        out_shape=[
            sds((n, d), bf16),
            sds((pairs, blocks, WIN_TWO, 2 * QB), bf16),
            sds((wide, d), bf16),
            sds((wide, d), bf16),
        ],
        grid=(pairs,),
        in_specs=[smem(), pair_block(n)] + two(m) + two(SIDE + RAW) * 2 + two(2 * RAW) + two(8),
        out_specs=[
            pair_block(n),
            pl.BlockSpec((1, blocks, WIN_TWO, 2 * QB), lambda g: (g, 0, 0, 0)),
            pair_block(wide),
            pair_block(wide),
        ],
        scratch_shapes=[pltpu.VMEM((WIN_TWO, QB), f32)],
        **params(4 * n * WIN_TWO * d * 2, 10 * n * d),
    )(flags, q, pooled, pooled, left, left, right, right, mine, mine, taps, taps)


def asked_kernel(q, kw, vw, out):
    own = slice(SIDE, kw.shape[0] - SIDE)
    slots = q.shape[0]
    column = lax.broadcasted_iota(jnp.int32, (HDIM, 2 * slots), 1)
    row = lax.broadcasted_iota(jnp.int32, (8, 2 * slots), 0)
    parts = tiles(q.shape[1], PAIR)
    scores = [nt(kw[own, c], both_heads(q[:, c] * scale)) for c in parts]
    tops = [jnp.max(s, axis=0, keepdims=True) for s in scores]
    raised = [jnp.exp(s - top).astype(bf16) for s, top in zip(scores, tops)]
    sums = [tn(vw[own, c], r) for c, r in zip(parts, raised)]
    for g, (top, r, x) in enumerate(zip(tops, raised, sums)):
        total = jnp.sum(r.astype(f32), axis=0, keepdims=True)
        out[g, :HDIM] = jnp.where(column < slots, x[:HDIM], x[HDIM:])
        out[g, HDIM:] = jnp.where(row == 0, top, jnp.where(row == 1, total, 0.0))


def asked_part(q, kw, vw):
    slots, d = q.shape
    pairs, wide = d // PAIR, kw.shape[0]
    return pl.pallas_call(
        asked_kernel,
        out_shape=sds((pairs, HDIM + 8, 2 * slots), f32),
        grid=(1,),
        in_specs=[whole(slots, d), whole(wide, d), whole(wide, d)],
        out_specs=whole(pairs, HDIM + 8, 2 * slots),
        **params(4 * slots * wide * d, 4 * wide * d),
    )(q, kw, vw)


def near_back_kernel(q, kw, vw, weights, grad, gq, own, to_left, to_right, gk, gv):
    n = q.shape[0]
    gk[...] = jnp.zeros_like(gk)
    gv[...] = jnp.zeros_like(gv)
    step = QB // STRIDE
    todo = []
    for b, rows in enumerate(tiles(n, QB)):
        window = slice(b * step, b * step + WIN_TWO)
        todo.append((q[rows], kw[window], vw[window], weights[0, b], grad[rows]))
    for first in range(0, len(todo), GROUP):
        for i, (gqb, gkb, gvb) in enumerate(zip(*back_blocks(todo[first : first + GROUP]))):
            b = first + i
            window = slice(b * step, b * step + WIN_TWO)
            gq[b * QB : (b + 1) * QB] = gqb.astype(bf16)
            gk[window] += gkb
            gv[window] += gvb
    m = gk.shape[0] - 2 * SIDE
    for i, wide in enumerate((gk, gv)):
        own[i] = wide[SIDE : SIDE + m]
        to_left[i] = wide[: SIDE + 8]
        to_right[i] = wide[SIDE + m :]


def near_back(q, kw, vw, weights, grad):
    n, d = q.shape
    pairs, blocks, wide = d // PAIR, n // QB, kw.shape[0]
    sizes = (wide - 2 * SIDE, SIDE + 8, SIDE)
    return pl.pallas_call(
        near_back_kernel,
        out_shape=[sds((n, d), bf16)] + [sds((2, r, d), f32) for r in sizes],
        grid=(pairs,),
        in_specs=[pair_block(n), pair_block(wide), pair_block(wide)]
        + [pl.BlockSpec((1, blocks, WIN_TWO, 2 * QB), lambda g: (g, 0, 0, 0))]
        + [pair_block(n)],
        out_specs=[pair_block(n)] + [two_rows(r) for r in sizes],
        scratch_shapes=[pltpu.VMEM((wide, PAIR), f32)] * 2,
        **params(10 * n * WIN_TWO * d * 2, 20 * n * d),
    )(q, kw, vw, weights, grad)


def asked_back_kernel(flags, q, kw, vw, logsum, mixed, grad, near, near_next, gq, own, following):
    m = near.shape[1]
    reach = slice(SIDE, SIDE + m + RAW)
    slots = q.shape[0]
    at_end = lax.broadcasted_iota(jnp.int32, (8, PAIR), 0) * 0 + flags[1] > 0
    parts = tiles(q.shape[1], PAIR)
    queries = [both_heads(q[:, c] * scale) for c in parts]
    grads = [both_heads(grad[:, c]) for c in parts]
    scores = [nt(kw[reach, c], x) for c, x in zip(parts, queries)]
    changes = [nt(vw[reach, c], x) for c, x in zip(parts, grads)]
    weights = [jnp.exp(s - logsum[g, 0:1]) for g, s in enumerate(scores)]
    values = [nn(w.astype(bf16), x) for w, x in zip(weights, grads)]
    grad_scores = []
    for c, w, change in zip(parts, weights, changes):
        by_feature = (grad[:, c].astype(f32) * mixed[:, c]).T
        inner = [jnp.sum(by_feature[rows], axis=0, keepdims=True) for rows in tiles(PAIR, HDIM)]
        grad_scores.append((w * (change - jnp.concatenate(inner, axis=1))).astype(bf16))
    keys = [nn(x, y) for x, y in zip(grad_scores, queries)]
    backs = [tn(x[:m], kw[reach, c][:m]) * scale for c, x in zip(parts, grad_scores)]
    for c, key, value, back in zip(parts, keys, values, backs):
        for i, wide in enumerate((key, value)):
            own[i, :, c] = near[i, :, c] + wide[:m]
            following[i, :, c] = jnp.where(at_end, 0.0, near_next[i, :, c] + wide[m : m + 8])
        gq[:, c] = jnp.where(head_masks(slots), back[:slots], back[slots:]).astype(bf16)


def asked_back(flags, q, kw, vw, logsum, mixed, grad, near, near_next):
    slots, d = q.shape
    pairs, wide, m = d // PAIR, kw.shape[0], near.shape[1]
    return pl.pallas_call(
        asked_back_kernel,
        out_shape=[sds((slots, d), bf16), sds((2, m, d), f32), sds((2, 8, d), f32)],
        grid=(1,),
        in_specs=[
            smem(), whole(slots, d), whole(wide, d), whole(wide, d), whole(pairs, 8, 2 * slots), whole(slots, d),
            whole(slots, d), whole(2, m, d), whole(2, 8, d),
        ],
        out_specs=[whole(slots, d), whole(2, m, d), whole(2, 8, d)],
        **params(10 * slots * wide * d, 20 * wide * d),
    )(flags, q, kw, vw, logsum, mixed, grad, near, near_next)


def pool_rows(held, taps):
    m = (held.shape[0] - 8) // STRIDE
    total = taps[0:1] * held[pl.ds(6, m, stride=STRIDE)]
    for t in range(1, TAPS):
        total = total + taps[t : t + 1] * held[pl.ds(6 + t, m, stride=STRIDE)]
    return total.astype(bf16)


def lower_kernel(
    x, mixed, wo, vectors, up, down, kpool, vpool, sel, wq_from, wk_from, wv_from,
    active, slope, pooled, mine, to_left, to_right, asked, *rest,
):
    fgain, fbias = of_norm(vectors, "lower_fgain"), of_norm(vectors, "lower_fbias")
    again, abias = of_norm(vectors, "upper_again"), of_norm(vectors, "upper_abias")
    targets, bufs, (wq, wk, wv, held, in_sems, out_sems) = rest[:7], rest[7:14], rest[14:]
    hidden_b, normed_b, hidden_c, normed_c, q, k, v = bufs
    gone = Mover(bufs, targets, out_sems)
    came = Mover((wq_from, wk_from, wv_from), (wq, wk, wv), in_sems)
    step = pl.program_id(0)
    n, d = x.shape

    @pl.when(step == 0)
    def _():
        came.start()
        for rows in tiles(n, 256):
            h = x[rows].astype(f32) + nn(mixed[rows], wo[...])
            hidden_b[rows] = h
            hidden_c[rows] = h
            normed_b[rows] = norm_rows(h, fgain[...], fbias[...]).astype(bf16)
        gone.start(0, 1)

    for rows in tiles(n, 256):
        a, s = gelu_both(nn(normed_b[rows], up[...]))
        a = a.astype(bf16)
        active[rows] = a
        slope[rows] = s.astype(bf16)
        hidden_c[rows] += nn(a, down[...])

    @pl.when(step == pl.num_programs(0) - 1)
    def _():
        gone.start(2)
        came.wait()
        for rows in tiles(n, 256):
            normed_c[rows] = norm_rows(hidden_c[rows], again[...], abias[...]).astype(bf16)
            q[rows] = nn(normed_c[rows], wq[...]).astype(bf16)
        gone.start(3, 4)
        m = n // STRIDE
        held[:, :8] = jnp.zeros((d // PAIR, 8, PAIR), f32)
        for j, (w, out, taps, lanes) in enumerate(((wk, k, kpool, slice(0, d)), (wv, v, vpool, slice(d, 2 * d)))):
            for rows in tiles(n, 256):
                made = nn(normed_c[rows], w[...]).astype(bf16)
                out[rows] = made
                for i, c in enumerate(tiles(d, PAIR)):
                    held[i, 8 + rows.start : 8 + rows.stop] = made[:, c].astype(f32)
            gone.start(5 + j)
            for i, c in enumerate(tiles(d, PAIR)):
                part = slice(lanes.start + c.start, lanes.start + c.stop)
                pooled[:, part] = pool_rows(held.at[i], taps[:, c])
            mine[:RAW, lanes] = out[:RAW]
            mine[RAW:, lanes] = out[n - RAW :]
        to_right[:SIDE] = pooled[m - SIDE :]
        to_right[SIDE:] = mine[RAW:]
        to_left[:SIDE] = pooled[:SIDE]
        to_left[SIDE:] = mine[:RAW]
        asked[...] = nn(sel[...], q[...]).astype(bf16)
        gone.wait()


def lower_forward(x, mixed, wo, vectors, up, down, wq, wk, wv, kpool, vpool, sel):
    n, d = x.shape
    ff, slots, m = up.shape[1], sel.shape[0], n // STRIDE
    fc = 512
    lanes = pl.BlockSpec((n, fc), lambda c: (0, c))
    moved = [sds((n, d), t) for t in (f32, bf16, f32, bf16, bf16, bf16, bf16)]
    small = [(m, 2 * d), (2 * RAW, 2 * d), (SIDE + RAW, 2 * d), (SIDE + RAW, 2 * d), (slots, d)]
    got = pl.pallas_call(
        lower_kernel,
        out_shape=[sds((n, ff), bf16)] * 2 + [sds(x, bf16) for x in small] + moved,
        grid=(ff // fc,),
        in_specs=[
            whole(n, d), whole(n, d), whole(d, d), whole(len(NORMS), d),
            pl.BlockSpec((d, fc), lambda c: (0, c)), pl.BlockSpec((fc, d), lambda c: (c, 0)),
            whole(8, d), whole(8, d), whole(slots, n), *[anywhere()] * 3,
        ],
        out_specs=[lanes, lanes] + [whole(*x) for x in small] + [anywhere()] * len(moved),
        scratch_shapes=[pltpu.VMEM(x.shape, x.dtype) for x in moved]
        + [pltpu.VMEM((d, d), bf16)] * 3
        + [pltpu.VMEM((d // PAIR, n + 8, PAIR), f32)]
        + [pltpu.SemaphoreType.DMA((3,)), pltpu.SemaphoreType.DMA((len(moved),))],
        **params(4 * n * d * ff + 8 * n * d * d, 8 * n * ff + 40 * n * d),
    )(x, mixed, wo, vectors, up, down, kpool, vpool, sel, wq, wk, wv)
    active, slope, pooled, mine, to_left, to_right, asked, hidden_b, normed_b, hidden_c, normed_c, q, k, v = got
    return (
        hidden_b, normed_b, active, slope, hidden_c, normed_c, q, k, v, pooled, mine, to_left, to_right, asked,
    )


def by_owner(perm, x):
    return nt(perm, x).astype(bf16)


def place_hidden(order, group, chunk, rows, wide):
    count = order.shape[0]
    held = chunk.T
    size = held.shape[0] // count
    for s in range(count):
        start = pl.multiple_of(order[s] * size, size)
        wide[pl.ds(start, size), rows] = held[s * size : (s + 1) * size].astype(wide.dtype)


def hidden_scratch(n, fc, seqs):
    return pltpu.VMEM((fc, n), f32 if fc // seqs % 16 else bf16)


def two_halves(left, right, first, second):
    half = left.shape[0] // 2
    first[...] = nn(left[:half].astype(bf16), right[...]).astype(bf16).reshape(first.shape)
    second[...] = nn(left[half:].astype(bf16), right[...]).astype(bf16).reshape(second.shape)


def finish_back(n, hidden, grad, gain, grad_norm, grad_hidden, sums):
    sums[...] = jnp.zeros_like(sums)
    for rows in tiles(n, 128):
        back, by_gain, by_bias = norm_back(hidden[rows], gain[...], grad_norm[rows])
        grad_hidden[rows] = grad[rows].astype(f32) + back
        sums[0:1] += by_gain
        sums[1:2] += by_bias


def hidden_specs(d, ff, docs, more=1):
    fc = ff // docs
    last = docs - 1
    into = [
        pl.BlockSpec((d, fc), lambda c, *_: (0, jnp.minimum(c, last))),
        pl.BlockSpec((fc, d), lambda c, *_: (jnp.minimum(c, last), 0)),
    ]
    lanes = pl.BlockSpec((d // 2, fc), lambda c, *_: (0, c))
    rows = pl.BlockSpec(
        (1, fc // 2, d), lambda c, docs, *_: (docs[jnp.minimum(c, last)], 0, 0)
    )
    out = [lanes, lanes, rows, rows]
    shapes = [sds((d // 2, ff + more * d), bf16)] * 2 + [sds((docs, fc // 2, d), bf16)] * 2
    return into, out, shapes


def upper_kernel(
    doc_order, seq_order, hidden_c, near, asked, sel, cot, wo, vectors, perm, up, down,
    grad_asked, up_keep, up_send, down_keep, down_send, sums, out_to, mixed_to, grad_d_to, grad_mixed_to,
    out, mixed, grad_d, grad_mixed, hidden_d, normed, hidden_e, grad_norm, flag, normed_t, active_t, lifted, sems,
):
    fgain, fbias = of_norm(vectors, "upper_fgain"), of_norm(vectors, "upper_fbias")
    gone = Mover((out, mixed, grad_d, grad_mixed), (out_to, mixed_to, grad_d_to, grad_mixed_to), sems)
    step = pl.program_id(0)
    n, d = near.shape
    last = pl.num_programs(0) - 1

    @pl.when(step == 0)
    def _():
        slots = sel.shape[0]
        flag[...] = tn(sel[...], jnp.ones((slots, PAIR), bf16))
        for rows in tiles(n, 256):
            here = jnp.concatenate([flag[rows]] * (d // PAIR), axis=1) > 0.5
            placed = tn(sel[:, rows], asked[...])
            mixed[rows] = jnp.where(here, placed, near[rows].astype(f32)).astype(bf16)
            h = hidden_c[rows] + nn(mixed[rows], wo[...])
            hidden_d[rows] = h
            hidden_e[rows] = h
            normed[rows] = norm_rows(h, fgain[...], fbias[...]).astype(bf16)
        gone.start(1)
        normed_t[...] = by_owner(perm[...], normed[...])
        grad_norm[...] = jnp.zeros_like(grad_norm)

    @pl.when(step < last)
    def _():
        for rows in tiles(n, 256):
            a, s = gelu_both(nn(normed[rows], up[...]))
            a = a.astype(bf16)
            hidden_e[rows] += nn(a, down[...])
            place_hidden(seq_order, step, a, rows, active_t)
            g = (nt(cot[rows], down[...]) * s).astype(bf16)
            grad_norm[rows] += nt(g, up[...])
            lifted[rows] = g
        two_halves(normed_t, lifted, up_keep, up_send)
        two_halves(active_t, cot, down_keep, down_send)

    @pl.when(step == last)
    def _():
        for rows in tiles(n, 256):
            out[rows] = hidden_e[rows].astype(bf16)
        gone.start(0)
        finish_back(n, hidden_d, cot, fgain, grad_norm, grad_d, sums)
        gone.start(2)
        for rows in tiles(n, 256):
            branch = grad_d[rows].astype(bf16)
            lifted[rows] = branch
            grad_mixed[rows] = nt(branch, wo[...]).astype(bf16)
        grad_asked[...] = nn(sel[...], grad_mixed[...]).astype(bf16)
        for rows in tiles(n, 256):
            here = jnp.concatenate([flag[rows]] * (d // PAIR), axis=1) > 0.5
            g = grad_mixed[rows]
            grad_mixed[rows] = jnp.where(here, 0.0, g.astype(f32)).astype(bf16)
        gone.start(3)
        normed_t[...] = by_owner(perm[...], mixed[...])
        two_halves(normed_t, lifted, up_keep, up_send)
        gone.wait()


def upper_both(doc_order, seq_order, hidden_c, near, asked, sel, cot, wo, vectors, perm, up, down):
    n, d = near.shape
    ff, slots = up.shape[1], sel.shape[0]
    docs, seqs = doc_order.shape[0], seq_order.shape[0]
    into, outof, shapes = hidden_specs(d, ff, docs)
    fc = ff // docs
    moved = [sds((n, d), t) for t in (bf16, bf16, f32, bf16)]
    grad_asked, *halves, sums, out, mixed, grad_d, grad_mixed = pl.pallas_call(
        upper_kernel,
        out_shape=[sds((slots, d), bf16), *shapes, sds((8, d), f32), *moved],
        grid_spec=pltpu.PrefetchScalarGridSpec(
            num_scalar_prefetch=2,
            grid=(docs + 1,),
            in_specs=[
                whole(n, d), whole(n, d), whole(slots, d), whole(slots, n), whole(n, d), whole(d, d),
                whole(len(NORMS), d), whole(d, d), *into,
            ],
            out_specs=[whole(slots, d), *outof, whole(8, d), *[anywhere()] * len(moved)],
            scratch_shapes=[
                *[pltpu.VMEM(x.shape, x.dtype) for x in moved],
                pltpu.VMEM((n, d), f32), pltpu.VMEM((n, d), bf16), pltpu.VMEM((n, d), f32), pltpu.VMEM((n, d), f32),
                pltpu.VMEM((n, PAIR), f32), pltpu.VMEM((d, n), bf16), hidden_scratch(n, fc, seqs),
                pltpu.VMEM((n, fc), bf16), pltpu.SemaphoreType.DMA((len(moved),)),
            ],
        ),
        **params(12 * n * d * ff + 6 * n * d * d, 8 * d * ff + 40 * n * d),
    )(doc_order, seq_order, hidden_c, near, asked, sel, cot, wo, vectors, perm, up, down)
    return out, mixed, grad_d, grad_mixed, grad_asked, *halves, sums


def unpool(held, gp, following, taps, made):
    m = gp.shape[0]
    last = lax.broadcasted_iota(jnp.int32, gp.shape, 0) == m - 1
    later = jnp.where(last, following, pltpu.roll(gp, m - 1, 0))
    made[pl.ds(0, m, stride=STRIDE)] = taps[2:3] * gp
    made[pl.ds(1, m, stride=STRIDE)] = taps[3:4] * gp
    made[pl.ds(2, m, stride=STRIDE)] = taps[4:5] * gp + taps[0:1] * later
    made[pl.ds(3, m, stride=STRIDE)] = taps[1:2] * later
    return [
        jnp.sum(gp * held[pl.ds(6 + t, m, stride=STRIDE)], axis=0, keepdims=True) for t in range(TAPS)
    ]


def upper_pairs_kernel(came, outs, gone, gkv, held, made, normed_t):
    gw_keep, gw_send, grad_norm, sums = outs
    normed, perm = came.got(0), came.got(1)
    normed_t[...] = by_owner(perm[...], normed[...])
    gp, from_left, from_right, following, rim = (came.got(i) for i in range(2, 7))
    sums[...] = jnp.zeros_like(sums)
    n, d = normed.shape
    m = n // STRIDE
    for i in range(2):
        x, taps, w = (came.got(7 + 3 * i + j) for j in range(3))
        for c in tiles(d, PAIR):
            held[:8] = rim[RAW - 8 :, i * d + c.start : i * d + c.stop].astype(f32)
            held[8:] = x[:, c].astype(f32)
            total = gp[i, :, c]
            edge = jnp.zeros((m - 2 * SIDE, PAIR), f32)
            total = total + jnp.concatenate([from_left[i, :, c], edge, from_right[i, :SIDE, c]], axis=0)
            later = from_right[i, SIDE : SIDE + 1, c] + following[i, 0:1, c]
            parts = unpool(held, total, later, taps[:, c], made)
            gkv[:, c] = made[...].astype(bf16)
            for t, part in enumerate(parts):
                sums[8 * i + t : 8 * i + t + 1, c] = part
        if i == 0:
            grad_norm[...] = nt(gkv[...], w[...])
        else:
            grad_norm[...] += nt(gkv[...], w[...])
            gone.start(2, 3)
        part = slice(i * d, (i + 1) * d)
        two_halves(normed_t, gkv, gw_keep.at[:, part], gw_send.at[:, part])
    gone.start(0, 1)


def upper_pairs_back(gp, from_left, from_right, following, k, v, rim, kpool, vpool, normed, wk, wv, perm):
    n, d = k.shape
    return moved_call(
        upper_pairs_kernel,
        (normed, perm, gp, from_left, from_right, following, rim, k, kpool, wk, v, vpool, wv),
        [sds((d // 2, 2 * d), bf16)] * 2 + [sds((n, d), f32), sds((16, d), f32)],
        [
            pltpu.VMEM((n, d), bf16),
            pltpu.VMEM((n + 8, PAIR), f32),
            pltpu.VMEM((n, PAIR), f32),
            pltpu.VMEM((d, n), bf16),
        ],
        (10 * n * d * d, 20 * n * d),
    )


def upper_queries_kernel(came, outs, gone, grad_norm):
    gq, grad_c, branch, sums = outs
    gq_near, gq_asked, sel = (came.got(i) for i in range(3))
    n, d = gq_near.shape
    for rows in tiles(n, 256):
        gq[rows] = (gq_near[rows].astype(f32) + tn(sel[:, rows], gq_asked[...])).astype(bf16)
    gone.start(0)
    wq, pairs_norm = came.got(3), came.got(4)
    for rows in tiles(n, 256):
        grad_norm[rows] = pairs_norm[rows] + nt(gq[rows], wq[...])
    hidden, grad, vectors = (came.got(i) for i in range(5, 8))
    gain = of_norm(vectors, "upper_again")
    finish_back(n, hidden, grad, gain, grad_norm, grad_c, sums)
    branch[...] = grad_c[...].astype(bf16)
    gone.start(1, 2, 3)


def upper_queries_back(gq_near, gq_asked, sel, hidden, grad, pairs_norm, gain, wq):
    n, d = gq_near.shape
    return moved_call(
        upper_queries_kernel,
        (gq_near, gq_asked, sel, wq, pairs_norm, hidden, grad, gain),
        [sds((n, d), bf16), sds((n, d), f32), sds((n, d), bf16), sds((8, d), f32)],
        [pltpu.VMEM((n, d), f32)],
        (2 * n * d * d, 24 * n * d),
    )


def lower_project_kernel(came, outs, gone, gkv, grad_norm, low_t, sums):
    gw_keep, gw_send, grad_in = outs
    normed, low = came.got(0), came.got(1)
    n, d = normed.shape
    low_t[...] = by_owner(low[...], normed[...])
    gq, wq = came.got(2), came.got(3)
    grad_norm[...] = nt(gq[...], wq[...])
    two_halves(low_t, gq, gw_keep.at[:, :d], gw_send.at[:, :d])
    left, right = came.got(4), came.got(5)
    for i in range(2):
        g, w = came.got(6 + 2 * i), came.got(7 + 2 * i)
        gkv[...] = g[...].astype(bf16)
        gkv[:REACH_ONE] = (g[:REACH_ONE] + left[i]).astype(bf16)
        gkv[n - REACH_ONE :] = (g[n - REACH_ONE :] + right[i]).astype(bf16)
        grad_norm[...] += nt(gkv[...], w[...])
        part = slice((1 + i) * d, (2 + i) * d)
        two_halves(low_t, gkv, gw_keep.at[:, part], gw_send.at[:, part])
    x, grad, vectors = (came.got(i) for i in range(10, 13))
    gain = of_norm(vectors, "lower_again")
    sums[...] = jnp.zeros_like(sums)
    for rows in tiles(n, 128):
        back, by_gain, by_bias = norm_back(x[rows].astype(f32), gain[...], grad_norm[rows])
        grad_in[rows] = grad[rows] + back
        sums[0:1] += by_gain
        sums[1:2] += by_bias
    gone.start(2)
    at = 8
    for i in range(13, 17):
        part = came.got(i)
        sums[at : at + part.shape[0]] = part[...]
        at += part.shape[0]
    for rows, out in zip(tiles(d, d // 2), (gw_keep, gw_send)):
        out[:, 3 * d :] = nt(low[rows], sums[...].astype(bf16)).astype(bf16)
    gone.start(0, 1)


def lower_project_back(gq, gk, gv, left, right, normed, x, grad, gain, wq, wk, wv, low, *sums):
    n, d = gq.shape
    return moved_call(
        lower_project_kernel,
        (normed, low, gq, wq, left, right, gk, wk, gv, wv, x, grad, gain, *sums),
        [sds((d // 2, 3 * d + PAIR), bf16)] * 2 + [sds((n, d), f32)],
        [pltpu.VMEM((n, d), bf16), pltpu.VMEM((n, d), f32), pltpu.VMEM((d, n), bf16), pltpu.VMEM((PAIR, d), f32)],
        (14 * n * d * d, 24 * n * d),
    )


def lower_back_kernel(
    doc_order, seq_order, branch_c, normed, vectors, perm, active, slope, up, down, grad_c, hidden_b, mixed, wo, gq_upper, normed_upper,
    up_keep, up_send, down_keep, down_send, grad_b, grad_mixed, sums,
    branch, grad_norm, normed_t, active_t, lifted, grad_held, hidden_held, mixed_held, wo_held, gq_held, upper_held, sems,
):
    step = pl.program_id(0)
    n, d = branch_c.shape
    last = pl.num_programs(0) - 2
    fgain = of_norm(vectors, "lower_fgain")
    late = Mover(
        (grad_c, hidden_b, mixed, wo, gq_upper, normed_upper),
        (grad_held, hidden_held, mixed_held, wo_held, gq_held, upper_held),
        sems,
    )

    @pl.when(step == 0)
    def _():
        late.start()
        normed_t[...] = by_owner(perm[...], normed[...])
        grad_norm[...] = jnp.zeros_like(grad_norm)

    @pl.when(step < last)
    def _():
        for rows in tiles(n, 256):
            g = (nt(branch_c[rows], down[...]) * slope[rows].astype(f32)).astype(bf16)
            grad_norm[rows] += nt(g, up[...])
            lifted[rows] = g
            place_hidden(seq_order, step, active[rows], rows, active_t)
        two_halves(active_t, branch_c, down_keep, down_send)
        two_halves(normed_t, lifted, up_keep, up_send)

    @pl.when(step == last)
    def _():
        late.wait()
        finish_back(n, hidden_held, grad_held, fgain, grad_norm, grad_b, sums)
        for rows in tiles(n, 256):
            branch[rows] = grad_b[rows].astype(bf16)
            grad_mixed[rows] = nt(branch[rows], wo_held[...]).astype(bf16)
        normed_t[...] = by_owner(perm[...], mixed_held[...])
        two_halves(normed_t, branch, up_keep, up_send)

    @pl.when(step == last + 1)
    def _():
        normed_t[...] = by_owner(perm[...], upper_held[...])
        two_halves(normed_t, gq_held, up_keep, up_send)


def lower_back(
    doc_order, seq_order, branch_c, grad_c, hidden_b, normed, active, slope, mixed, wo, vectors, perm, up, down, gq_upper,
    normed_upper,
):
    n, d = grad_c.shape
    ff = up.shape[1]
    docs, seqs = doc_order.shape[0], seq_order.shape[0]
    fc = ff // docs
    into, outof, shapes = hidden_specs(d, ff, docs, 2)
    lanes = pl.BlockSpec((n, fc), lambda c, *_: (0, jnp.minimum(c, docs - 1)))
    return pl.pallas_call(
        lower_back_kernel,
        out_shape=[*shapes, sds((n, d), f32), sds((n, d), bf16), sds((8, d), f32)],
        grid_spec=pltpu.PrefetchScalarGridSpec(
            num_scalar_prefetch=2,
            grid=(docs + 2,),
            in_specs=[
                whole(n, d), whole(n, d), whole(len(NORMS), d), whole(d, d), lanes, lanes, *into, *[anywhere()] * 6,
            ],
            out_specs=[*outof, whole(n, d), whole(n, d), whole(8, d)],
            scratch_shapes=[
                pltpu.VMEM((n, d), bf16), pltpu.VMEM((n, d), f32), pltpu.VMEM((d, n), bf16),
                hidden_scratch(n, fc, seqs), pltpu.VMEM((n, fc), bf16),
                pltpu.VMEM((n, d), f32), pltpu.VMEM((n, d), f32), pltpu.VMEM((n, d), bf16), pltpu.VMEM((d, d), bf16),
                pltpu.VMEM((n, d), bf16), pltpu.VMEM((n, d), bf16), pltpu.SemaphoreType.DMA((6,)),
            ],
        ),
        **params(8 * n * d * ff + 4 * n * d * d, 12 * n * ff + 30 * n * d),
    )(
        doc_order, seq_order, branch_c, normed, vectors, perm, active, slope, up, down, grad_c, hidden_b, mixed, wo,
        gq_upper, normed_upper,
    )


def shifted(value, steps):
    count = lax.axis_size("seq")
    pairs = [(i, i + steps) for i in range(count) if 0 <= i + steps < count]
    return lax.ppermute(value, "seq", pairs)


def exchanged(value, axis, bit):
    count = lax.axis_size(axis)
    return lax.ppermute(value, axis, [(i, i ^ bit) for i in range(count)])


def bits(axis, first=1):
    count = lax.axis_size(axis)
    return [(axis, 1 << b) for b in range(count.bit_length()) if first <= 1 << b < count]


def orders():
    cores = [("seq", 1)]
    return cores + bits("doc") + bits("seq", 2), cores + bits("doc")[::-1] + bits("seq", 2)


def owners(order):
    count = lax.axis_size("doc") * lax.axis_size("seq")
    flips = {"doc": [], "seq": []}
    for axis in flips:
        for p in range(count):
            flips[axis].append(sum(b for i, (a, b) in enumerate(order) if a == axis and p >> (len(order) - 1 - i) & 1))
    return tuple(lax.axis_index(a) ^ jnp.array(flips[a], jnp.int32) for a in ("doc", "seq"))


def permutation(order, d):
    doc, seq = owners(order)
    owner = doc * lax.axis_size("seq") + seq
    size = d // owner.shape[0]
    source = (owner[:, None] * size + jnp.arange(size, dtype=jnp.int32)[None, :]).reshape(-1)
    return (source[:, None] == jnp.arange(d, dtype=jnp.int32)[None, :]).astype(bf16)


def hidden_orders(order):
    def places(axis):
        steps = [b for a, b in order if a == axis]
        value = jnp.arange(lax.axis_size(axis), dtype=jnp.int32) ^ lax.axis_index(axis)
        place = jnp.zeros_like(value)
        for b in steps:
            place = 2 * place + (value // b) % 2
        return place

    return places("doc"), places("seq")


class Halving:
    def __init__(self, keep, send, order):
        self.order, self.at, self.rows = order, 1, keep.shape[0]
        self.terms = [keep, exchanged(send, *order[0])]

    def prepare(self):
        self.rows //= 2
        self.send = self.total(self.rows).astype(bf16)

    def go(self):
        self.terms = self.terms + [exchanged(self.send, *self.order[self.at])]
        self.at += 1

    def left(self):
        return self.at < len(self.order)

    def total(self, start=0):
        out = None
        for t in self.terms:
            t = t[start : start + self.rows].astype(f32)
            out = t if out is None else out + t
        return out


def stepped(order):
    steps = []
    for axis, bit in order:
        if axis == "seq" and bit > 1 and steps[-1][0][0] == "seq" and steps[-1][0][1] > 1 and len(steps[-1]) == 1:
            steps[-1] = steps[-1] + [(axis, bit)]
        else:
            steps.append([(axis, bit)])
    return steps


def flips(step):
    axis = step[0][0]
    places = range(len(step))
    return [(axis, sum(step[i][1] for i in places if p >> (len(step) - 1 - i) & 1)) for p in range(1, 1 << len(step))]


def tied(*values):
    return lax.optimization_barrier(values)


def arrived(values, *halvings):
    values, terms = tied(values, [h.terms for h in halvings])
    for h, t in zip(halvings, terms):
        h.terms = t
    return values


def sent(values, *halvings):
    for h in halvings:
        h.prepare()
    values, _ = tied(values, [h.send for h in halvings])
    for h in halvings:
        h.go()
    return values


def in_turn(halvings):
    before = None
    for h in halvings:
        if h.left():
            if before is not None:
                h.terms, _ = tied(h.terms, before)
            h.prepare()
            before = h.send
            h.go()


def others(value, step):
    return [exchanged(value, *f) for f in flips(step)]


def summed(value, steps):
    for step in steps:
        value = sum(others(value, step), value)
    return value


def merged_apart(part, steps):
    half = part.shape[0] // 2
    axis, bit = steps[0][0]
    second = (lax.axis_index(axis) & bit) > 0
    mine = jnp.where(second, part[half:], part[:half])
    other = exchanged(jnp.where(second, part[:half], part[half:]), axis, bit)
    mine = merged(merge(mine, other), steps[1:])
    other = exchanged(mine, axis, bit)
    return jnp.concatenate([jnp.where(second, other, mine), jnp.where(second, mine, other)], axis=0)


def merge(*parts):
    tops = [p[:, HDIM : HDIM + 1] for p in parts]
    top = functools.reduce(jnp.maximum, tops)
    total = sum(p * jnp.exp(t - top) for p, t in zip(parts, tops))
    row = lax.broadcasted_iota(jnp.int32, total.shape, 1)
    return jnp.where(row == HDIM, top, total)


def merged(part, steps):
    for step in steps:
        part = merge(part, *others(part, step))
    return part


def body(
    tokens, cotangent, counts, positions, lower_again, lower_abias, lower_query, lower_key, lower_value, lower_out,
    lower_fgain, lower_fbias, lower_up, lower_down, upper_again, upper_abias, upper_query, upper_key, upper_value,
    upper_out, upper_fgain, upper_fbias, upper_up, upper_down, upper_kpool, upper_vpool,
):
    seq_count = lax.axis_size("seq")
    seq_index = lax.axis_index("seq")
    x, cot = tokens[0], cotangent[0]
    n, d = x.shape
    m = n // STRIDE
    flags = jnp.stack([seq_index == 0, seq_index == seq_count - 1]).astype(jnp.int32)
    slot_count = positions.shape[1]
    slots = jnp.arange(slot_count, dtype=jnp.int32)
    place = jnp.where(slots < counts[0], positions[0] - seq_index * n, -1)
    sel = (place[:, None] == jnp.arange(n, dtype=jnp.int32)[None, :]).astype(bf16)
    kpool = jnp.pad(upper_kpool, ((0, 8 - TAPS), (0, 0)))
    vpool = jnp.pad(upper_vpool, ((0, 8 - TAPS), (0, 0)))
    taps = jnp.concatenate([kpool, vpool], axis=1)
    low_first, high_first = orders()
    perm_low, perm_high = permutation(low_first, d), permutation(high_first, d)
    doc_order, seq_order = hidden_orders(high_first)
    along = stepped(bits("seq"))

    first_norm = jnp.concatenate([lower_again, lower_abias]).reshape(2, d)
    norm_a, ka, va, qa = project(x, first_norm, lower_key, lower_value, lower_query)
    qa, lower_again = tied(qa, lower_again)
    vectors = jnp.concatenate(
        [
            lower_again, lower_abias, lower_fgain, lower_fbias, upper_again, upper_abias, upper_fgain, upper_fbias,
        ]
    ).reshape(len(NORMS), d)
    ends = lambda rows: jnp.concatenate([ka[rows], va[rows]], axis=1)
    left = shifted(ends(slice(n - REACH_ONE, n)), 1)
    right = shifted(ends(slice(0, REACH_ONE)), -1)
    mixed_a, weights_a = local_attention(flags, qa, ka, va, left, right)
    (
        hidden_b, norm_b, active_b, slope_b, hidden_c, norm_c, qc, kc, vc, pooled, mine, to_left, to_right, asked_q,
    ) = lower_forward(
        x, mixed_a, lower_out, vectors, lower_up, lower_down, upper_query, upper_key, upper_value, kpool, vpool, sel,
    )
    from_left = shifted(to_right, 1)
    from_right = shifted(to_left, -1)
    asked_q = summed(asked_q, along[:1])
    more = others(asked_q, along[1])
    near, weights_c, kw, vw = near_attention(flags, qc, pooled, from_left, from_right, mine, taps)
    asked_q, more, kw = tied(asked_q, more, kw)
    asked_q = summed(sum(more, asked_q), along[2:])
    part = merged_apart(asked_part(asked_q, kw, vw), along)
    total = part[:, HDIM + 1 : HDIM + 2]
    logsum = jnp.broadcast_to(part[:, HDIM : HDIM + 1] + jnp.log(total), (d // PAIR, 8, 2 * slot_count))
    asked = part[:, :HDIM] / total
    asked = asked.reshape(d // PAIR, HDIM, 2, slot_count).transpose(3, 0, 2, 1).reshape(slot_count, d)

    (
        out, mixed_c, grad_d, grad_mixed_c, grad_asked, up_keep, up_send, down_keep, down_send, sums_d,
    ) = upper_both(
        doc_order, seq_order, hidden_c, near, asked.astype(bf16), sel, cot, upper_out, vectors, perm_low, upper_up,
        upper_down,
    )
    flat = lambda x: x.reshape(-1, d)
    gu_up = Halving(up_keep, up_send, low_first)
    gu_down = Halving(flat(down_keep), flat(down_send), high_first)
    more = others(grad_asked, along[0])
    gq_near, near_own, to_left, to_right = near_back(qc, kw, vw, weights_c, grad_mixed_c)
    grad_asked, more, near_own, to_left, to_right = arrived(
        (grad_asked, more, near_own, to_left, to_right), gu_up, gu_down
    )
    grad_asked = sum(more, grad_asked)
    more = others(grad_asked, along[1])
    from_left_back = shifted(to_right, 1)
    from_right_back = shifted(to_left, -1)
    grad_asked, more = sent((grad_asked, more), gu_up, gu_down)
    grad_asked = summed(sum(more, grad_asked), along[2:])
    gq_asked, gp, following = asked_back(
        flags, asked_q, kw, vw, logsum, asked, grad_asked, near_own, to_right[:, :8]
    )
    gq_asked = summed(gq_asked, along[:1])
    more = others(gq_asked, along[1])
    gp, _ = tied(gp, gq_asked)
    gw_keep, gw_send, pairs_norm, sums_p = upper_pairs_back(
        gp, from_left_back, from_right_back, following, kc, vc, from_left[SIDE:], kpool, vpool, norm_c, upper_key,
        upper_value, perm_high,
    )
    gq_asked, more, pairs_norm, gw_send = tied(gq_asked, more, pairs_norm, gw_send)
    gu_pair = Halving(gw_keep, gw_send, high_first)
    gq_asked = summed(sum(more, gq_asked), along[2:])
    pairs_norm = arrived(pairs_norm, gu_up, gu_down)
    pairs_norm = sent(pairs_norm, gu_up, gu_down)
    gq_upper, grad_c, branch_c, sums_c = upper_queries_back(
        gq_near, gq_asked, sel, hidden_c, grad_d, pairs_norm, vectors, upper_query
    )
    branch_c = arrived(branch_c, gu_pair)
    branch_c = sent(branch_c, gu_pair)
    up_keep, up_send, down_keep, down_send, grad_b, grad_mixed_a, sums_b = lower_back(
        doc_order, seq_order, branch_c, grad_c, hidden_b, norm_b, active_b, slope_b, mixed_a, lower_out,
        vectors, perm_low, lower_up, lower_down, gq_upper, norm_c,
    )
    grad_mixed_a, up_send, down_send = arrived((grad_mixed_a, up_send, down_send), gu_up, gu_down, gu_pair)
    gl_up = Halving(up_keep, up_send, low_first)
    gl_down = Halving(flat(down_keep), flat(down_send), high_first)
    grad_mixed_a = sent(grad_mixed_a, gu_up, gu_down, gu_pair)
    grad_mixed_a = arrived(grad_mixed_a, gl_up, gl_down)
    in_turn([gl_up, gl_down])
    grad_mixed_a, _ = tied(grad_mixed_a, gl_down.send)
    gq, gk, gv, to_left, to_right = local_back(qa, ka, va, left, right, weights_a, grad_mixed_a)
    back_last = shifted(to_left, -1)
    back_first = shifted(to_right, 1)
    grad_b, gq = arrived((grad_b, gq), gu_up, gu_pair)
    back_first, back_last = sent((back_first, back_last), gu_up, gu_pair)
    back_first, back_last = arrived((back_first, back_last), gu_down)
    grad_b = sent(grad_b, gu_down)
    gw_keep, gw_send, grad_in = lower_project_back(
        gq, gk, gv, back_first, back_last, norm_a, x, grad_b, vectors, lower_query, lower_key, lower_value,
        perm_low, sums_b, sums_c, sums_d, sums_p,
    )
    gw_send = arrived(gw_send, gu_pair, gu_up, gu_down, gl_up, gl_down)
    gl_qkv = Halving(gw_keep, gw_send, low_first)
    in_turn([gl_up, gl_down, gl_qkv, gu_pair])
    gl_down.terms = arrived(gl_down.terms, gu_pair)
    in_turn([gl_down, gl_up, gl_qkv, gl_up, gl_down])
    gl_qkv.terms = arrived(gl_qkv.terms, gl_up)
    in_turn([gl_qkv])
    gl_qkv.terms = arrived(gl_qkv.terms, gl_down)
    in_turn([gl_qkv])
    every = (gl_up, gl_down, gl_qkv, gu_up, gu_down, gu_pair)
    while any(h.left() for h in every):
        in_turn(every)
    for h in every:
        if h is not gl_qkv:
            h.terms, _ = tied(h.terms, gl_qkv.send)
    gu_up, gu_down, gu_pair, gl_up, gl_down, gl_qkv = (
        h.total() for h in (gu_up, gu_down, gu_pair, gl_up, gl_down, gl_qkv)
    )
    small = gl_qkv[:, 3 * d :].T
    sums_a, sums_b, sums_c, sums_d, sums_p = (small[r] for r in (*tiles(32, 8), slice(32, 48)))
    ff = lower_up.shape[1]
    part = lambda got, i: got[:, i * d : (i + 1) * d]
    return (
        out[None],
        grad_in[None],
        sums_a[0],
        sums_a[1],
        part(gl_qkv, 0),
        part(gl_qkv, 1),
        part(gl_qkv, 2),
        gl_up[:, ff : ff + d],
        sums_b[0],
        sums_b[1],
        gl_up[:, :ff],
        gl_down,
        sums_c[0],
        sums_c[1],
        gl_up[:, ff + d :],
        part(gu_pair, 0),
        part(gu_pair, 1),
        gu_up[:, ff:],
        sums_d[0],
        sums_d[1],
        gu_up[:, :ff],
        gu_down,
        sums_p[0:TAPS],
        sums_p[8 : 8 + TAPS],
    )


def solution(mesh):
    tokens = P("doc", "seq", None)
    every = ("doc", "seq")
    vector, matrix, taps = P(every), P(every, None), P(None, every)
    layer = (vector, vector, matrix, matrix, matrix, matrix, vector, vector, matrix, matrix)
    return jax.shard_map(
        body,
        mesh=mesh,
        in_specs=(tokens, tokens, P("doc"), P("doc", None)) + (P(),) * 22,
        out_specs=(tokens, tokens) + layer + layer + (taps, taps),
        check_vma=False,
    )
```
